128 devices in a mesh: hi: 4 (over z_hi, core), lo: 32 (over y, x, z_lo).
Axes of the slice: x: 4, y: 4, z: 4 (z_hi: 2, z_lo: 2; z = z_hi * 2 + z_lo), core: 2. Of those that a mesh axis runs over, the one named last changes fastest.
Arguments:
- src_position: float32 [16384, 2, 128], P(('hi', 'lo')), may hold values from -1 to 1
- src_weight: float32 [16384, 2, 128], P(('hi', 'lo')), may hold values from -6 to 6
- src_phase: float32 [16384, 128], P(('hi', 'lo')), may hold values from -3.140625 to 3.140625
- block_box: int32 [16384], P(('hi', 'lo')), may hold values from 0 to 32767
- block_count: int32 [128], P(('hi', 'lo')), may hold values from 1 to 128, as said below
- node_rate: float32 [32768, 64], P(('hi', 'lo')), may hold values from -3.140625 to 3.140625
- target_phase: float32 [32768, 256], P(('hi', 'lo')), may hold values from -3.140625 to 3.140625
Outputs:
- target_field: float32 [2, 32768, 256], P(None, ('hi', 'lo'))
The draws below stay inside these ranges and needn't reach their ends.
Inputs may be any that keep to these rules, and one draw needn't show every extreme that they name: `block_count`: every device has at least one live block, and some device has all 128 live.
All inputs are finite; a program needn't handle non-finite values.
Results may differ from the reference program's by a relative error of at most 0.0003.
Values sent between devices are 32-bit elements; how exact they have to be, the bound alone decides.
A program may use at most 128 MiB of HBM per device.

```python
import math
import jax
import jax.numpy as jnp
from jax import lax

RANK = 64
LB = 256
SLOTS = 128
BLK = 128
TGT_SIDE = 16
TGT_BOX = 256
NBOXES = 32768
NBLOCKS = 16384
N_HI = 4
N_LO = 32


def draw_block_count(key, part):
    key = jax.random.fold_in(key, 7)
    first, second = jax.random.split(key)
    counts = jax.random.randint(first, (N_HI * N_LO,), 1, SLOTS + 1)
    full_device = jax.random.randint(second, (), 0, N_HI * N_LO)
    return jnp.where(jnp.arange(N_HI * N_LO) == full_device, SLOTS, counts).astype(jnp.int32)


def plant(values, stream_key, least, high):
    place = [jax.random.randint(jax.random.fold_in(stream_key, axis), (), 0, length) for axis, length in enumerate(values.shape)]
    widest = values.shape.index(max(values.shape))
    next_to = place[:widest] + [(place[widest] + 1) % values.shape[widest]] + place[widest + 1:]
    return values.at[tuple(place)].set(least).at[tuple(next_to)].set(high)


def levels(key, dims, shards, least, high):
    level, own = 1.0, jax.random.fold_in(key, 6)
    for axis_at, shards_of in shards:
        draws = jnp.exp(jax.random.uniform(jax.random.fold_in(own, axis_at), (shards_of,), jnp.float32, least / len(shards), high / len(shards)))
        level = level * jnp.repeat(draws, dims[axis_at] // shards_of).reshape([-1 if axis == axis_at else 1 for axis in range(len(dims))])
    return level


def gaussian(stream_key, shape, deviation, most, cuts=(), kind=jnp.bfloat16):
    array = deviation * jax.random.normal(stream_key, shape, jnp.float32)
    if cuts:
        array = array * levels(stream_key, shape, cuts, -0.22, 0.18)
    return jnp.clip(array, -most, most).astype(kind)


def setup_inputs(seed: int = 0) -> dict:
    splits = jax.random.split(jax.random.key(seed), 8)
    src_position = jnp.clip(jax.random.uniform(splits[0], (NBLOCKS, 2, BLK), jnp.float32, -1.0, 1.0) * levels(splits[0], (NBLOCKS, 2, BLK), ((0, 128),), -0.4, 0.0), -1.0, 1.0)
    src_weight = gaussian(splits[1], (NBLOCKS, 2, BLK), 1.0, 6.0, ((0, 128),), jnp.float32)
    src_phase = jnp.clip(jax.random.uniform(splits[2], (NBLOCKS, BLK), jnp.float32, -3.140625, 3.140625), -3.140625, 3.140625)
    block_box = plant(jax.random.randint(splits[3], (NBLOCKS,), 0, NBOXES), jax.random.fold_in(splits[3], 1), 0, NBOXES - 1).astype(jnp.int32)
    block_count = draw_block_count(jax.random.fold_in(splits[7], 71), 0)
    node_rate = jnp.clip(jax.random.uniform(splits[5], (NBOXES, RANK), jnp.float32, -3.140625, 3.140625), -3.140625, 3.140625)
    target_phase = jnp.clip(jax.random.uniform(splits[6], (NBOXES, TGT_BOX), jnp.float32, -3.140625, 3.140625), -3.140625, 3.140625)
    return {"src_position": src_position, "src_weight": src_weight, "src_phase": src_phase, "block_box": block_box, "block_count": block_count, "node_rate": node_rate, "target_phase": target_phase}


HIGH = lax.Precision.HIGHEST


def cheb_nodes():
    order = jnp.arange(8).astype(jnp.float32)
    return jnp.cos((2.0 * order + 1.0) * math.pi / 16.0)


def lagrange(points):
    nodes = cheb_nodes()
    columns = []
    for index in range(8):
        value = jnp.ones_like(points)
        for other in range(8):
            if other != index:
                value = value * (points - nodes[other]) / (nodes[index] - nodes[other])
        columns.append(value)
    return jnp.stack(columns, axis=0)


def leaf(position, weight, phase):
    basis_x = lagrange(position[:, 0, :])
    basis_y = lagrange(position[:, 1, :])
    cosv = jnp.cos(phase)
    sinv = jnp.sin(phase)
    real = weight[:, 0, :] * cosv - weight[:, 1, :] * sinv
    imag = weight[:, 0, :] * sinv + weight[:, 1, :] * cosv
    part_re = jnp.einsum("akp,bkp->kab", basis_x * real, basis_y, precision=HIGH)
    part_im = jnp.einsum("akp,bkp->kab", basis_x * imag, basis_y, precision=HIGH)
    count = position.shape[0]
    return 0.5 * jnp.concatenate([part_re.reshape(count, 64), part_im.reshape(count, 64)], axis=1)


def translation(step, child):
    nodes = cheb_nodes()
    inner = lagrange((nodes + (2.0 * child - 1.0)) / 2.0).T
    eye_eight = jnp.eye(8, dtype=jnp.float32)
    if step % 2 == 0:
        middle = jnp.kron(inner, eye_eight)
    else:
        middle = jnp.kron(eye_eight, inner)
    return jnp.kron(jnp.eye(2, dtype=jnp.float32), middle)


def rotate(values, theta):
    cosv = jnp.cos(theta)
    sinv = jnp.sin(theta)
    real = values[..., :64]
    imag = values[..., 64:]
    return jnp.concatenate([cosv * real - sinv * imag, sinv * real + cosv * imag], axis=-1)


def level(own, partner, rate, bitval, step):
    theta = rate * (step + 1.0)
    own_t = rotate(own, theta)
    partner_t = rotate(partner, theta)
    first = jnp.where(bitval == 0, own_t, partner_t)
    second = jnp.where(bitval == 0, partner_t, own_t)
    left = jnp.einsum("...kt,tu->...ku", first, translation(step, 0), precision=HIGH)
    right = jnp.einsum("...kt,tu->...ku", second, translation(step, 1), precision=HIGH)
    return 0.70710678 * (left + right)


def evaluate(state, target_phase, side):
    grid = (2.0 * jnp.arange(side).astype(jnp.float32) + 1.0) / side - 1.0
    basis = lagrange(grid)
    table = jnp.einsum("am,bn->abmn", basis, basis, precision=HIGH).reshape(64, side * side)
    value_re = jnp.dot(state[:, :64], table, precision=HIGH)
    value_im = jnp.dot(state[:, 64:], table, precision=HIGH)
    cosv = jnp.cos(target_phase)
    sinv = jnp.sin(target_phase)
    return jnp.stack([value_re * cosv - value_im * sinv, value_re * sinv + value_im * cosv], axis=0)


def reference(src_position, src_weight, src_phase, block_box, block_count, node_rate, target_phase):
    devices = N_HI * N_LO
    blocks = jnp.arange(NBLOCKS)
    live = (blocks % SLOTS) < block_count[blocks // SLOTS]
    coeff = jnp.where(live[:, None], leaf(src_position, src_weight, src_phase), 0.0)
    state = jax.ops.segment_sum(coeff, block_box, NBOXES).reshape(devices, LB, 128)
    rates = node_rate.reshape(devices, LB, 64)
    index = jnp.arange(devices)
    for step in range(devices.bit_length() - 1):
        partner = state[index ^ (1 << step)]
        bitval = ((index >> step) & 1).reshape(devices, 1, 1)
        state = level(state, partner, rates, bitval, step)
    return evaluate(state.reshape(NBOXES, 128), target_phase, TGT_SIDE)
```

```python
import functools
import math

import jax
import jax.numpy as jnp
import ml_dtypes
import numpy as np
from jax import lax
from jax.experimental import pallas as pl
from jax.experimental.pallas import tpu as pltpu
from jax.sharding import PartitionSpec as P

MESH = pl.DeviceIdType.MESH
F32 = jnp.float32
BF16 = jnp.bfloat16
VMEM = pl.BlockSpec(memory_space=pltpu.VMEM)
SMEM = pl.BlockSpec(memory_space=pltpu.SMEM)
PAY = 136


def np_nodes():
    return np.cos((2.0 * np.arange(8) + 1.0) * math.pi / 16.0)


def np_lagrange(points):
    nodes = np_nodes()
    columns = []
    for index in range(8):
        value = np.ones_like(points)
        for other in range(8):
            if other != index:
                value = value * (points - nodes[other]) / (nodes[index] - nodes[other])
        columns.append(value)
    return np.stack(columns, axis=0)


def split_np(array):
    high = array.astype(np.float32).astype(ml_dtypes.bfloat16)
    low = (array - high.astype(np.float64)).astype(np.float32).astype(ml_dtypes.bfloat16)
    return high, low


def level_weight(parity):
    blocks = []
    for child in range(2):
        inner = np_lagrange((np_nodes() + (2.0 * child - 1.0)) / 2.0).T
        middle = np.kron(inner, np.eye(8)) if parity == 0 else np.kron(np.eye(8), inner)
        blocks.append(np.kron(np.eye(2), middle))
    weight = 0.70710678 * np.concatenate(blocks, axis=0)
    return np.concatenate(split_np(weight), axis=1)


def target_weight(side):
    grid = (2.0 * np.arange(side) + 1.0) / side - 1.0
    basis = np_lagrange(grid)
    table = np.einsum("am,bn->abmn", basis, basis).reshape(64, side * side)
    high, low = split_np(np.kron(np.eye(2), table))
    return np.concatenate([high, high, low], axis=0)


def sincos(angle):
    half = 0.5 * angle
    sq = half * half
    s = -1.0 / 39916800.0
    for term in (1.0 / 362880.0, -1.0 / 5040.0, 1.0 / 120.0, -1.0 / 6.0, 1.0):
        s = s * sq + term
    s = s * half
    c = 1.0 / 479001600.0
    for term in (-1.0 / 3628800.0, 1.0 / 40320.0, -1.0 / 720.0, 1.0 / 24.0, -0.5, 1.0):
        c = c * sq + term
    return 2.0 * s * c, 1.0 - 2.0 * s * s


def lagrange_rows(points):
    nodes = [float(v) for v in np_nodes()]
    diff = [points - v for v in nodes]
    before = [None] * 8
    after = [None] * 8
    for index in range(1, 8):
        before[index] = diff[0] if index == 1 else before[index - 1] * diff[index - 1]
    for index in range(6, -1, -1):
        after[index] = diff[7] if index == 6 else after[index + 1] * diff[index + 1]
    rows = []
    for index in range(8):
        scale = 1.0
        for other in range(8):
            if other != index:
                scale = scale / (nodes[index] - nodes[other])
        if index == 0:
            value = after[0]
        elif index == 7:
            value = before[7]
        else:
            value = before[index] * after[index]
        rows.append(value * scale)
    return rows


def split(value):
    high = value.astype(BF16)
    low = (value - high.astype(F32)).astype(BF16)
    return high, low


def leaf_kernel(pos_ref, wgt_ref, phase_ref, box_ref, count_ref, out_ref, gx, ly, ct):
    slots = phase_ref.shape[0]
    sinv, cosv = sincos(phase_ref[...])
    w_re = wgt_ref[pl.ds(0, slots, stride=2), :]
    w_im = wgt_ref[pl.ds(1, slots, stride=2), :]
    g_re = (0.5 * (w_re * cosv - w_im * sinv)).T
    g_im = (0.5 * (w_re * sinv + w_im * cosv)).T
    x = pos_ref[pl.ds(0, slots, stride=2), :].T
    y = pos_ref[pl.ds(1, slots, stride=2), :].T
    for index, value in enumerate(lagrange_rows(x)):
        gx[index] = value * g_re
        gx[8 + index] = value * g_im
    for index, value in enumerate(lagrange_rows(y)):
        ly[index] = value

    def row(index, carry):
        total = gx[index, 0:8, :][None] * ly[:, 0:8, :]
        for part in range(1, slots // 8):
            rows = slice(8 * part, 8 * part + 8)
            total = total + gx[index, rows, :][None] * ly[:, rows, :]
        ct[pl.ds(pl.multiple_of(index * 8, 8), 8), :] = jnp.sum(total, axis=1)
        return carry

    lax.fori_loop(0, 16, row, 0)
    out_ref[0:slots, :] = ct[...].T
    lane = lax.broadcasted_iota(jnp.int32, (1, slots), 1)
    key = jnp.where(lane < count_ref[0], box_ref[...], -1).astype(F32)
    out_ref[slots:slots + 8, :] = jnp.broadcast_to(key, (8, slots))


def butterfly_kernel(nxy, nq, pay_ref, rate_ref, w0_ref, w1_ref, out_ref,
                     gath, cat, rate_s, rate_r, rate_s2, rate_r2,
                     sib_s, sib_r, own, zrecv, ret_s, ret_r, fin_s, fin_r,
                     g_send, g_recv, r_send, r_recv, r2_send, r2_recv,
                     b_send, b_recv, z_send, z_recv, t_send, t_recv, f_send, f_recv):
    ndev = nxy * nq
    lb = 2 * ndev
    lx = nxy.bit_length() - 1
    slots = gath.shape[1] - 8
    hi = lax.axis_index("hi")
    lo = lax.axis_index("lo")
    xy = lax.div(lo, 2)
    zlo = lax.rem(lo, 2)
    q = hi * 2 + zlo
    core = lax.rem(hi, 2)
    z = lax.div(hi, 2) * 2 + zlo

    def dev(q_at, xy_at):
        return lax.div(q_at, 2), xy_at * 2 + lax.rem(q_at, 2)

    def xy_peer(step):
        return lax.rem(xy + step, nxy)

    def q_peer(step):
        return lax.rem(q + step, nq)

    def q_of(z_at, core_at):
        return lax.div(z_at, 2) * 4 + core_at * 2 + lax.rem(z_at, 2)

    def rcopy(src, dst, send, recv, target):
        return pltpu.make_async_remote_copy(
            src_ref=src, dst_ref=dst, send_sem=send, recv_sem=recv,
            device_id=target, device_id_type=MESH)

    barrier = pltpu.get_barrier_semaphore()

    def greet_xy(step, carry):
        pl.semaphore_signal(barrier, inc=1, device_id=dev(q, xy_peer(step)), device_id_type=MESH)
        return carry

    def greet_q(step, carry):
        pl.semaphore_signal(barrier, inc=1, device_id=dev(q_peer(step), xy), device_id_type=MESH)
        return carry

    lax.fori_loop(1, nxy, greet_xy, 0)
    lax.fori_loop(1, nq, greet_q, 0)

    rate_lo = rate_ref[0:ndev, :]
    rate_hi = rate_ref[ndev:lb, :]
    packed = jnp.concatenate([rate_lo, rate_hi], axis=1)
    rate_s[...] = packed.reshape(nxy, nq, 128)
    pl.semaphore_wait(barrier, nxy - 1 + nq - 1)

    def gather_copy(step):
        return rcopy(pay_ref, gath.at[xy], g_send.at[step], g_recv.at[step], dev(q, xy_peer(step)))

    def rate_copy(step):
        to = xy_peer(step)
        return rcopy(rate_s.at[to], rate_r.at[xy], r_send.at[step], r_recv.at[step], dev(q, to))

    def send_all(step, carry):
        gather_copy(step).start()
        return carry

    def send_rate(step, carry):
        rate_copy(step).start()
        return carry

    lax.fori_loop(1, nxy, send_rate, 0)
    lax.fori_loop(1, nxy, send_all, 0)
    gath[xy] = pay_ref[...]
    rate_r[xy] = rate_s[xy]

    def wait_rate(step, carry):
        rate_copy(step).wait()
        return carry

    lax.fori_loop(1, nxy, wait_rate, 0)
    turned = jnp.transpose(rate_r[...], (1, 0, 2))
    rate_s2[...] = turned

    def rate2_copy(step):
        to = q_peer(step)
        return rcopy(rate_s2.at[to], rate_r2.at[q], r2_send.at[step], r2_recv.at[step], dev(to, xy))

    def send_rate2(step, carry):
        rate2_copy(step).start()
        return carry

    lax.fori_loop(1, nq, send_rate2, 0)
    rate_r2[q] = rate_s2[q]

    def wait_gather(step, carry):
        gather_copy(step).wait()
        return carry

    lax.fori_loop(1, nxy, wait_gather, 0)

    def split_rows(index, carry):
        high, low = split(gath[index, 0:slots, :])
        rows = pl.ds(pl.multiple_of(index * slots, slots), slots)
        cat[rows, 0:128] = high
        cat[rows, 128:256] = low
        return carry

    lax.fori_loop(0, nxy, split_rows, 0)

    n = gath[:, slots, :].astype(jnp.int32)
    lbits = lb.bit_length() - 1
    dbits = ndev.bit_length() - 1
    j = n & (lb - 1)
    owner = n >> lbits
    holder = j & (ndev - 1)
    q_d = ((owner >> (lx + 1)) << 1) | (owner & 1)
    xy_d = (owner >> 1) & (nxy - 1)
    local = ((j >> dbits) << dbits) + q_d * nxy + xy_d
    code = (holder & (nq - 1)) * lb + local
    code = jnp.where((n >= 0) & ((holder >> 3) == xy), code, -1)
    row_id = lax.broadcasted_iota(jnp.int32, (lb, slots), 0)

    def chunk(q_at):
        rel = code - q_at * lb
        hot = [jnp.where(rel[i:i + 1, :] == row_id, 1.0, 0.0).astype(BF16) for i in range(nxy)]
        both = jnp.dot(jnp.concatenate(hot, axis=1), cat[...], preferred_element_type=F32)
        return both[:, 0:128] + both[:, 128:256]

    def sib_copy(off):
        return rcopy(sib_s.at[off], sib_r.at[off], b_send.at[off], b_recv.at[off],
                     dev(q_of(z, 1 - core), xy))

    def z_copy(off):
        return rcopy(own.at[off], zrecv.at[off], z_send.at[off], z_recv.at[off],
                     dev(q_of(lax.rem(z + off, 4), core), xy))

    def fold(off):
        sib_copy(off).wait()
        own[off] = own[off] + sib_r[off]

    def scatter(step, carry):
        off = 3 - step
        to = lax.rem(z + off, 4)
        sib_s[off] = chunk(q_of(to, 1 - core))
        sib_copy(off).start()

        @pl.when(step >= 1)
        def _():
            fold(off + 1)
            z_copy(off + 1).start()

        own[off] = chunk(q_of(to, core))
        return carry

    lax.fori_loop(0, 4, scatter, 0)

    def wait_rate2(step, carry):
        rate2_copy(step).wait()
        return carry

    lax.fori_loop(1, nq, wait_rate2, 0)
    sin_p, cos_p = sincos(rate_r2[...].reshape(ndev, 128))
    left = lax.broadcasted_iota(jnp.int32, (ndev, 128), 1) < 64
    cos_o = pltpu.roll(cos_p, 64, 1)
    sin_o = pltpu.roll(sin_p, 64, 1)
    cos1 = jnp.concatenate([jnp.where(left, cos_p, cos_o), jnp.where(left, cos_o, cos_p)], axis=0)
    sin1 = jnp.concatenate([jnp.where(left, -sin_p, sin_o), jnp.where(left, -sin_o, sin_p)], axis=0)

    fold(0)

    def wait_z(step, carry):
        z_copy(step).wait()
        own[0] = own[0] + zrecv[step]
        return carry

    lax.fori_loop(1, 4, wait_z, 0)

    state = own[0]
    cosv, sinv = cos1, sin1
    sub = lax.broadcasted_iota(jnp.int32, (lb // 8, 8, 128), 1)
    for step in range(dbits):
        if step > 0:
            cosv, sinv = cosv * cos1 - sinv * sin1, sinv * cos1 + cosv * sin1
        bit = lx if step == 0 else (step - 1 if step <= lx else step)
        if bit < 3:
            tiles = state.reshape(lb // 8, 8, 128)
            dist = 1 << bit
            upper = (sub & dist) != 0
            first = jnp.where(upper, pltpu.roll(tiles, dist, 1), tiles).reshape(lb, 128)
            second = jnp.where(upper, tiles, pltpu.roll(tiles, 8 - dist, 1)).reshape(lb, 128)
        else:
            pairs = state.reshape(lb >> (bit + 1), 2, 1 << bit, 128)
            first = jnp.concatenate([pairs[:, 0:1], pairs[:, 0:1]], axis=1).reshape(lb, 128)
            second = jnp.concatenate([pairs[:, 1:2], pairs[:, 1:2]], axis=1).reshape(lb, 128)
        first = cosv * first + sinv * pltpu.roll(first, 64, 1)
        second = cosv * second + sinv * pltpu.roll(second, 64, 1)
        high, low = split(jnp.concatenate([first, second], axis=1))
        w_ref = w0_ref if step % 2 == 0 else w1_ref
        main = jnp.dot(high, w_ref[...], preferred_element_type=F32)
        rest = jnp.dot(low, w_ref[:, 0:128], preferred_element_type=F32)
        state = main[:, 0:128] + (main[:, 128:256] + rest)

    for jj in range(2):
        ret_s[:, jj] = state[jj * ndev:(jj + 1) * ndev].reshape(nq, nxy, 128)

    def ret_copy(step):
        to = q_peer(step)
        return rcopy(ret_s.at[to], ret_r.at[q], t_send.at[step], t_recv.at[step], dev(to, xy))

    def send_ret(step, carry):
        ret_copy(step).start()
        return carry

    def wait_ret(step, carry):
        ret_copy(step).wait()
        return carry

    lax.fori_loop(1, nq, send_ret, 0)
    ret_r[q] = ret_s[q]
    lax.fori_loop(1, nq, wait_ret, 0)
    back = ret_r[...].reshape(nq * 2, nxy, 128)
    fin_s[...] = jnp.transpose(back, (1, 0, 2))

    def fin_copy(step):
        to = xy_peer(step)
        return rcopy(fin_s.at[to], fin_r.at[xy], f_send.at[step], f_recv.at[step], dev(q, to))

    def send_fin(step, carry):
        fin_copy(step).start()
        return carry

    def wait_fin(step, carry):
        fin_copy(step).wait()
        return carry

    lax.fori_loop(1, nxy, send_fin, 0)
    fin_r[xy] = fin_s[xy]
    lax.fori_loop(1, nxy, wait_fin, 0)
    out_ref[...] = fin_r[...].reshape(lb, 128)


def target_kernel(state_ref, phase_ref, table_ref, out_ref):
    lb, points = phase_ref.shape
    half = lb // 2
    for jj in range(2):
        rows = slice(jj * half, jj * half + half)
        high, low = split(state_ref[pl.ds(jj, half, stride=2), :])
        stacked = jnp.concatenate([high, low, high], axis=1)
        value = jnp.dot(stacked, table_ref[...], preferred_element_type=F32)
        sinv, cosv = sincos(phase_ref[rows, :])
        v_re = value[:, 0:points]
        v_im = value[:, points:2 * points]
        out_ref[0, rows, :] = v_re * cosv - v_im * sinv
        out_ref[1, rows, :] = v_re * sinv + v_im * cosv


def local(nxy, nq, side, src_position, src_weight, src_phase, block_box, block_count, node_rate, target_phase):
    slots, points = src_phase.shape
    lb = node_rate.shape[0]
    ndev = nxy * nq
    payload = pl.pallas_call(
        leaf_kernel,
        out_shape=jax.ShapeDtypeStruct((slots + 8, 128), F32),
        in_specs=[VMEM, VMEM, VMEM, VMEM, SMEM],
        out_specs=VMEM,
        scratch_shapes=[
            pltpu.VMEM((16, points, slots), F32),
            pltpu.VMEM((8, points, slots), F32),
            pltpu.VMEM((128, slots), F32),
        ],
        compiler_params=pltpu.CompilerParams(vmem_limit_bytes=32 * 2**20),
        name="leaf",
    )(src_position.reshape(2 * slots, points), src_weight.reshape(2 * slots, points), src_phase,
      block_box.reshape(1, slots), block_count)

    dma = pltpu.SemaphoreType.DMA
    state = pl.pallas_call(
        functools.partial(butterfly_kernel, nxy, nq),
        out_shape=jax.ShapeDtypeStruct((lb, 128), F32),
        in_specs=[VMEM] * 4,
        out_specs=VMEM,
        scratch_shapes=[
            pltpu.VMEM((nxy, slots + 8, 128), F32),
            pltpu.VMEM((nxy * slots, 256), BF16),
            pltpu.VMEM((nxy, nq, 128), F32),
            pltpu.VMEM((nxy, nq, 128), F32),
            pltpu.VMEM((nq, nxy, 128), F32),
            pltpu.VMEM((nq, nxy, 128), F32),
            pltpu.VMEM((4, lb, 128), F32),
            pltpu.VMEM((4, lb, 128), F32),
            pltpu.VMEM((4, lb, 128), F32),
            pltpu.VMEM((4, lb, 128), F32),
            pltpu.VMEM((nq, 2, nxy, 128), F32),
            pltpu.VMEM((nq, 2, nxy, 128), F32),
            pltpu.VMEM((nxy, 2 * nq, 128), F32),
            pltpu.VMEM((nxy, 2 * nq, 128), F32),
            dma((nxy,)), dma((nxy,)), dma((nxy,)), dma((nxy,)), dma((nq,)), dma((nq,)),
            dma((4,)), dma((4,)), dma((4,)), dma((4,)),
            dma((nq,)), dma((nq,)), dma((nxy,)), dma((nxy,)),
        ],
        compiler_params=pltpu.CompilerParams(
            collective_id=0, has_side_effects=True, vmem_limit_bytes=48 * 2**20),
        name="butterfly",
    )(payload, node_rate, level_weight(0), level_weight(1))

    return pl.pallas_call(
        target_kernel,
        out_shape=jax.ShapeDtypeStruct((2, lb, target_phase.shape[1]), F32),
        in_specs=[VMEM] * 3,
        out_specs=VMEM,
        compiler_params=pltpu.CompilerParams(vmem_limit_bytes=32 * 2**20),
        name="target",
    )(state, target_phase, target_weight(side))


def solution(mesh):
    n_hi, n_lo = mesh.shape["hi"], mesh.shape["lo"]
    placed = (
        P(("hi", "lo"), None, None),
        P(("hi", "lo"), None, None),
        P(("hi", "lo"), None),
        P(("hi", "lo")),
        P(("hi", "lo")),
        P(("hi", "lo"), None),
        P(("hi", "lo"), None),
    )
    return jax.shard_map(
        functools.partial(local, n_lo // 2, 2 * n_hi, 16),
        mesh=mesh, in_specs=placed, out_specs=P(None, ("hi", "lo"), None), check_vma=False
    )
```

```python
import functools
import math

import jax
import jax.numpy as jnp
import ml_dtypes
import numpy as np
from jax import lax
from jax.experimental import pallas as pl
from jax.experimental.pallas import tpu as pltpu
from jax.sharding import PartitionSpec as P

MESH = pl.DeviceIdType.MESH
F32 = jnp.float32
BF16 = jnp.bfloat16
VMEM = pl.BlockSpec(memory_space=pltpu.VMEM)
SMEM = pl.BlockSpec(memory_space=pltpu.SMEM)


def np_nodes():
    return np.cos((2.0 * np.arange(8) + 1.0) * math.pi / 16.0)


def np_lagrange(points):
    nodes = np_nodes()
    columns = []
    for index in range(8):
        value = np.ones_like(points)
        for other in range(8):
            if other != index:
                value = value * (points - nodes[other]) / (nodes[index] - nodes[other])
        columns.append(value)
    return np.stack(columns, axis=0)


def split_np(array):
    high = array.astype(np.float32).astype(ml_dtypes.bfloat16)
    low = (array - high.astype(np.float64)).astype(np.float32).astype(ml_dtypes.bfloat16)
    return high, low


def level_weight(parity):
    blocks = []
    for child in range(2):
        inner = np_lagrange((np_nodes() + (2.0 * child - 1.0)) / 2.0).T
        middle = np.kron(inner, np.eye(8)) if parity == 0 else np.kron(np.eye(8), inner)
        blocks.append(np.kron(np.eye(2), middle))
    weight = 0.70710678 * np.concatenate(blocks, axis=0)
    return np.concatenate(split_np(weight), axis=1)


def target_weight(side):
    grid = (2.0 * np.arange(side) + 1.0) / side - 1.0
    basis = np_lagrange(grid)
    table = np.einsum("am,bn->abmn", basis, basis).reshape(64, side * side)
    high, low = split_np(np.kron(np.eye(2), table))
    return np.concatenate([high, high, low], axis=0)


def sincos(angle):
    half = 0.5 * angle
    sq = half * half
    s = -1.0 / 39916800.0
    for term in (1.0 / 362880.0, -1.0 / 5040.0, 1.0 / 120.0, -1.0 / 6.0, 1.0):
        s = s * sq + term
    s = s * half
    c = 1.0 / 479001600.0
    for term in (-1.0 / 3628800.0, 1.0 / 40320.0, -1.0 / 720.0, 1.0 / 24.0, -0.5, 1.0):
        c = c * sq + term
    return 2.0 * s * c, 1.0 - 2.0 * s * s


def lagrange_rows(points):
    nodes = [float(v) for v in np_nodes()]
    diff = [points - v for v in nodes]
    before = [None] * 8
    after = [None] * 8
    for index in range(1, 8):
        before[index] = diff[0] if index == 1 else before[index - 1] * diff[index - 1]
    for index in range(6, -1, -1):
        after[index] = diff[7] if index == 6 else after[index + 1] * diff[index + 1]
    rows = []
    for index in range(8):
        scale = 1.0
        for other in range(8):
            if other != index:
                scale = scale / (nodes[index] - nodes[other])
        if index == 0:
            value = after[0]
        elif index == 7:
            value = before[7]
        else:
            value = before[index] * after[index]
        rows.append(value * scale)
    return rows


def split(value):
    high = value.astype(BF16)
    low = (value - high.astype(F32)).astype(BF16)
    return high, low


def leaf(pos_ref, wgt_ref, phase_ref, gx, ly, ct):
    slots = phase_ref.shape[0]
    sinv, cosv = sincos(phase_ref[...])
    w_re = wgt_ref[pl.ds(0, slots, stride=2), :]
    w_im = wgt_ref[pl.ds(1, slots, stride=2), :]
    g_re = (0.5 * (w_re * cosv - w_im * sinv)).T
    g_im = (0.5 * (w_re * sinv + w_im * cosv)).T
    x = pos_ref[pl.ds(0, slots, stride=2), :].T
    y = pos_ref[pl.ds(1, slots, stride=2), :].T
    for index, value in enumerate(lagrange_rows(x)):
        gx[index] = value * g_re
        gx[8 + index] = value * g_im
    for index, value in enumerate(lagrange_rows(y)):
        ly[index] = value

    def row(index, carry):
        total = gx[index, 0:8, :][None] * ly[:, 0:8, :]
        for part in range(1, slots // 8):
            rows = slice(8 * part, 8 * part + 8)
            total = total + gx[index, rows, :][None] * ly[:, rows, :]
        ct[pl.ds(pl.multiple_of(index * 8, 8), 8), :] = jnp.sum(total, axis=1)
        return carry

    lax.fori_loop(0, 16, row, 0)
    return ct[...].T


def butterfly_kernel(pos_hbm, wgt_hbm, phase_hbm, rate_hbm, w0_hbm, w1_hbm, box_ref, count_ref, out_ref,
                     pos_ref, wgt_ref, phase_ref, rate_ref, w0_ref, w1_ref, gx, ly, ct,
                     gath_a, gath_b, cat, rate_s, rate_r, rate_s2, rate_r2,
                     sib_s, sib_r, own, zrecv, z2recv, ret_s, ret_r, fin_s, fin_r,
                     in_sem, g_send, g_recv, r_send, r_recv, r2_send, r2_recv,
                     b_send, b_recv, z_send, z_recv, t_send, t_recv, f_send, f_recv):
    nxy, nq = 16, 8
    ndev = nxy * nq
    lb = 2 * ndev
    lx = 4
    slots = 128
    hi = lax.axis_index("hi")
    lo = lax.axis_index("lo")
    xy = lax.div(lo, 2)
    zlo = lax.rem(lo, 2)
    q = hi * 2 + zlo
    core = lax.rem(hi, 2)
    z = lax.div(hi, 2) * 2 + zlo

    loads = [
        pltpu.make_async_copy(src, dst, in_sem.at[i])
        for i, (src, dst) in enumerate([
            (phase_hbm, phase_ref), (wgt_hbm, wgt_ref), (pos_hbm, pos_ref),
            (rate_hbm, rate_ref), (w0_hbm, w0_ref), (w1_hbm, w1_ref)])
    ]
    for load in loads:
        load.start()

    def dev(q_at, xy_at):
        return lax.div(q_at, 2), xy_at * 2 + lax.rem(q_at, 2)

    def xy_peer(step):
        return lax.rem(xy + step, nxy)

    def q_peer(step):
        return lax.rem(q + step, nq)

    def q_of(z_at, core_at):
        return lax.div(z_at, 2) * 4 + core_at * 2 + lax.rem(z_at, 2)

    def rcopy(src, dst, send, recv, target):
        return pltpu.make_async_remote_copy(
            src_ref=src, dst_ref=dst, send_sem=send, recv_sem=recv,
            device_id=target, device_id_type=MESH)

    barrier = pltpu.get_barrier_semaphore()

    def greet_xy(step, carry):
        pl.semaphore_signal(barrier, inc=1, device_id=dev(q, xy_peer(step)), device_id_type=MESH)
        return carry

    def greet_q(step, carry):
        pl.semaphore_signal(barrier, inc=1, device_id=dev(q_peer(step), xy), device_id_type=MESH)
        return carry

    lax.fori_loop(1, nxy, greet_xy, 0)
    lax.fori_loop(1, nq, greet_q, 0)

    x_at = lax.rem(xy, 4)
    y_at = lax.div(xy, 4)
    for load in loads[0:3]:
        load.wait()
    coeff = leaf(pos_ref, wgt_ref, phase_ref, gx, ly, ct)
    lane = lax.broadcasted_iota(jnp.int32, (1, slots), 1)
    key = jnp.where(lane < count_ref[0], box_ref[...], -1).astype(F32)
    gath_a[y_at * 4 + x_at, 0:64, :] = coeff[64:128]
    gath_a[y_at * 4 + x_at, 64:72, :] = jnp.broadcast_to(key, (8, slots))
    gath_b[x_at * 4 + y_at] = coeff[0:64]
    loads[3].wait()
    rate_s[...] = jnp.concatenate([rate_ref[:, 0:ndev], rate_ref[:, ndev:lb]], axis=0).T
    pl.semaphore_wait(barrier, nxy - 1 + nq - 1)

    xs = {0: x_at, -1: lax.rem(x_at + 3, 4), 1: lax.rem(x_at + 1, 4), 2: lax.rem(x_at + 2, 4)}
    ys = {0: y_at, -1: lax.rem(y_at + 3, 4), 1: lax.rem(y_at + 1, 4), 2: lax.rem(y_at + 2, 4)}
    order = (0, -1, 1, 2)
    sent = []

    def block(part, first, second, rows=None):
        ref = gath_a if part == 0 else gath_b
        at = ys[second] * 4 + xs[first] if part == 0 else xs[second] * 4 + ys[first]
        return ref.at[at] if rows is None else ref.at[at, rows]

    def halves(part):
        return (slice(0, 40), slice(40, 72)) if part == 0 else (slice(0, 32), slice(32, 64))

    def ring_copy(part, axis, sem, first, second, way, rows=None):
        along_x = (part == 0) == (axis == 0)
        to = ys[0] * 4 + xs[way] if along_x else ys[way] * 4 + xs[0]
        ref = block(part, first, second, rows)
        return rcopy(ref, ref, g_send.at[part, sem], g_recv.at[part, sem], dev(q, to))

    def start(copy):
        copy.start()
        sent.append(copy)

    for part in range(2):
        start(ring_copy(part, 0, 0, 0, 0, 1))
        start(ring_copy(part, 0, 1, 0, 0, -1))
    for part in range(2):
        start(ring_copy(part, 1, 4, 0, 0, 1))
        start(ring_copy(part, 1, 5, 0, 0, -1))

    def rate_copy(step):
        to = xy_peer(step)
        rows_to = pl.ds(pl.multiple_of(to * nq, nq), nq)
        rows_me = pl.ds(pl.multiple_of(xy * nq, nq), nq)
        return rcopy(rate_s.at[rows_to], rate_r.at[rows_me], r_send.at[step], r_recv.at[step], dev(q, to))

    def send_rate(step, carry):
        rate_copy(step).start()
        return carry

    lax.fori_loop(1, nxy, send_rate, 0)
    rows_me = pl.ds(pl.multiple_of(xy * nq, nq), nq)
    rate_r[rows_me, :] = rate_s[rows_me, :]

    for part in range(2):
        low, high = halves(part)
        ring_copy(part, 0, 0, -1, 0, 1).wait_recv()
        start(ring_copy(part, 0, 2, -1, 0, 1, low))
        ring_copy(part, 0, 1, 1, 0, -1).wait_recv()
        start(ring_copy(part, 0, 3, 1, 0, -1, high))
    for part in range(2):
        for r in (1, 2):
            start(ring_copy(part, 1, 4 + 4 * r, order[r], 0, 1))
            start(ring_copy(part, 1, 5 + 4 * r, order[r], 0, -1))
    for part in range(2):
        low, high = halves(part)
        ring_copy(part, 0, 2, 2, 0, 1, low).wait_recv()
        ring_copy(part, 0, 3, 2, 0, -1, high).wait_recv()
        start(ring_copy(part, 1, 4 + 12, 2, 0, 1))
        start(ring_copy(part, 1, 5 + 12, 2, 0, -1))
    for r in range(4):
        for part in range(2):
            low, high = halves(part)
            ring_copy(part, 1, 4 + 4 * r, order[r], -1, 1).wait_recv()
            start(ring_copy(part, 1, 6 + 4 * r, order[r], -1, 1, low))
            ring_copy(part, 1, 5 + 4 * r, order[r], 1, -1).wait_recv()
            start(ring_copy(part, 1, 7 + 4 * r, order[r], 1, -1, high))

    def wait_rate(step, carry):
        rate_copy(step).wait()
        return carry

    lax.fori_loop(1, nxy, wait_rate, 0)
    for at in range(nq):
        rate_s2[at] = rate_r[pl.ds(at, nxy, stride=nq), :]

    def rate2_copy(step):
        to = q_peer(step)
        return rcopy(rate_s2.at[to], rate_r2.at[q], r2_send.at[step], r2_recv.at[step], dev(to, xy))

    def send_rate2(step, carry):
        rate2_copy(step).start()
        return carry

    lax.fori_loop(1, nq, send_rate2, 0)
    rate_r2[q] = rate_s2[q]

    for r in range(4):
        for part in range(2):
            low, high = halves(part)
            ring_copy(part, 1, 6 + 4 * r, order[r], 2, 1, low).wait_recv()
            ring_copy(part, 1, 7 + 4 * r, order[r], 2, -1, high).wait_recv()

    def split_rows(index, carry):
        rows_a = pl.ds(pl.multiple_of(index * slots + 64, 64), 64)
        rows_b = pl.ds(pl.multiple_of(index * slots, 64), 64)
        high, low = split(gath_a[index, 0:64, :])
        cat[rows_a, 0:128] = high
        cat[rows_a, 128:256] = low
        high, low = split(gath_b[lax.rem(index, 4) * 4 + lax.div(index, 4)])
        cat[rows_b, 0:128] = high
        cat[rows_b, 128:256] = low
        return carry

    lax.fori_loop(0, nxy, split_rows, 0)

    n = gath_a[:, 64, :].astype(jnp.int32)
    lbits = lb.bit_length() - 1
    dbits = ndev.bit_length() - 1
    j = n & (lb - 1)
    owner = n >> lbits
    holder = j & (ndev - 1)
    q_d = ((owner >> (lx + 1)) << 1) | (owner & 1)
    xy_d = (owner >> 1) & (nxy - 1)
    local_row = ((j >> dbits) << dbits) + q_d * nxy + xy_d
    code = (holder & (nq - 1)) * lb + local_row
    code = jnp.where((n >= 0) & ((holder >> 3) == xy), code, -1)
    row_id = lax.broadcasted_iota(jnp.int32, (lb, slots), 0)

    def chunk(q_at):
        rel = code - q_at * lb
        hot = [jnp.where(rel[i:i + 1, :] == row_id, 1.0, 0.0).astype(BF16) for i in range(nxy)]
        both = jnp.dot(jnp.concatenate(hot, axis=1), cat[...], preferred_element_type=F32)
        return both[:, 0:128] + both[:, 128:256]

    def sib_copy(off):
        return rcopy(sib_s.at[off], sib_r.at[off], b_send.at[off], b_recv.at[off],
                     dev(q_of(z, 1 - core), xy))

    def z_dev(off):
        return dev(q_of(lax.rem(z + off, 4), core), xy)

    up_half = rcopy(own.at[2, 0:ndev], z2recv.at[0], z_send.at[0], z_recv.at[0], z_dev(1))
    down_half = rcopy(own.at[2, ndev:lb], z2recv.at[1], z_send.at[1], z_recv.at[1], z_dev(3))
    up_full = rcopy(own.at[1], zrecv.at[0], z_send.at[2], z_recv.at[2], z_dev(1))
    down_full = rcopy(own.at[3], zrecv.at[1], z_send.at[3], z_recv.at[3], z_dev(3))

    def fold(off):
        sib_copy(off).wait()
        own[off] = own[off] + sib_r[off]

    def scatter(step, carry):
        off = lax.rem(step + 2, 4)
        to = lax.rem(z + off, 4)
        sib_s[off] = chunk(q_of(to, 1 - core))
        sib_copy(off).start()

        @pl.when(step == 1)
        def _():
            fold(2)
            up_half.start()
            down_half.start()

        @pl.when(step == 3)
        def _():
            fold(3)
            down_half.wait_recv()
            own[3, ndev:lb] = own[3, ndev:lb] + z2recv[1]
            down_full.start()

        own[off] = chunk(q_of(to, core))
        return carry

    lax.fori_loop(0, 4, scatter, 0)
    fold(1)
    up_half.wait_recv()
    own[1, 0:ndev] = own[1, 0:ndev] + z2recv[0]
    up_full.start()
    fold(0)

    def wait_rate2(step, carry):
        rate2_copy(step).wait()
        return carry

    lax.fori_loop(1, nq, wait_rate2, 0)
    sin_p, cos_p = sincos(rate_r2[...].reshape(ndev, 128))
    left = lax.broadcasted_iota(jnp.int32, (ndev, 128), 1) < 64
    cos_o = pltpu.roll(cos_p, 64, 1)
    sin_o = pltpu.roll(sin_p, 64, 1)
    cos1 = jnp.concatenate([jnp.where(left, cos_p, cos_o), jnp.where(left, cos_o, cos_p)], axis=0)
    sin1 = jnp.concatenate([jnp.where(left, -sin_p, sin_o), jnp.where(left, -sin_o, sin_p)], axis=0)
    for load in loads[4:6]:
        load.wait()

    down_full.wait_recv()
    up_full.wait_recv()
    state = own[0] + (zrecv[0] + zrecv[1])

    cosv, sinv = cos1, sin1
    sub = lax.broadcasted_iota(jnp.int32, (lb // 8, 8, 128), 1)
    for step in range(dbits):
        if step > 0:
            cosv, sinv = cosv * cos1 - sinv * sin1, sinv * cos1 + cosv * sin1
        bit = lx if step == 0 else (step - 1 if step <= lx else step)
        if bit < 3:
            tiles = state.reshape(lb // 8, 8, 128)
            dist = 1 << bit
            upper = (sub & dist) != 0
            first = jnp.where(upper, pltpu.roll(tiles, dist, 1), tiles).reshape(lb, 128)
            second = jnp.where(upper, tiles, pltpu.roll(tiles, 8 - dist, 1)).reshape(lb, 128)
        else:
            pairs = state.reshape(lb >> (bit + 1), 2, 1 << bit, 128)
            first = jnp.concatenate([pairs[:, 0:1], pairs[:, 0:1]], axis=1).reshape(lb, 128)
            second = jnp.concatenate([pairs[:, 1:2], pairs[:, 1:2]], axis=1).reshape(lb, 128)
        first = cosv * first + sinv * pltpu.roll(first, 64, 1)
        second = cosv * second + sinv * pltpu.roll(second, 64, 1)
        high, low = split(jnp.concatenate([first, second], axis=1))
        w_ref = w0_ref if step % 2 == 0 else w1_ref
        main = jnp.dot(high, w_ref[...], preferred_element_type=F32)
        rest = jnp.dot(low, w_ref[:, 0:128], preferred_element_type=F32)
        state = main[:, 0:128] + (main[:, 128:256] + rest)

    for at in range(nq):
        for jj in range(2):
            base = jj * ndev + at * nxy
            ret_s[at, jj * nxy:(jj + 1) * nxy] = state[base:base + nxy]

    def ret_copy(step):
        to = q_peer(step)
        rows = pl.ds(pl.multiple_of(q * 2 * nxy, 2 * nxy), 2 * nxy)
        return rcopy(ret_s.at[to], ret_r.at[rows], t_send.at[step], t_recv.at[step], dev(to, xy))

    def send_ret(step, carry):
        ret_copy(step).start()
        return carry

    def wait_ret(step, carry):
        ret_copy(step).wait()
        return carry

    lax.fori_loop(1, nq, send_ret, 0)
    ret_r[pl.ds(pl.multiple_of(q * 2 * nxy, 2 * nxy), 2 * nxy), :] = ret_s[q]
    lax.fori_loop(1, nq, wait_ret, 0)
    for at in range(nxy):
        fin_s[at] = ret_r[pl.ds(at, 2 * nq, stride=nxy), :]

    def fin_copy(step):
        to = xy_peer(step)
        return rcopy(fin_s.at[to], fin_r.at[xy], f_send.at[step], f_recv.at[step], dev(q, to))

    def send_fin(step, carry):
        fin_copy(step).start()
        return carry

    def wait_fin(step, carry):
        fin_copy(step).wait()
        return carry

    lax.fori_loop(1, nxy, send_fin, 0)
    fin_r[xy] = fin_s[xy]
    for copy in sent + [up_half, down_half, up_full, down_full]:
        copy.wait_send()
    lax.fori_loop(1, nxy, wait_fin, 0)
    out_ref[...] = fin_r[...].reshape(lb, 128)


def target_kernel(state_ref, phase_ref, table_ref, out_ref):
    lb, points = phase_ref.shape
    half = lb // 2
    for jj in range(2):
        rows = slice(jj * half, jj * half + half)
        high, low = split(state_ref[pl.ds(jj, half, stride=2), :])
        stacked = jnp.concatenate([high, low, high], axis=1)
        value = jnp.dot(stacked, table_ref[...], preferred_element_type=F32)
        sinv, cosv = sincos(phase_ref[rows, :])
        v_re = value[:, 0:points]
        v_im = value[:, points:2 * points]
        out_ref[0, rows, :] = v_re * cosv - v_im * sinv
        out_ref[1, rows, :] = v_re * sinv + v_im * cosv


def local(side, src_position, src_weight, src_phase, block_box, block_count, node_rate, target_phase):
    slots, points = src_phase.shape
    lb = node_rate.shape[0]
    nxy, nq = 16, 8
    dma = pltpu.SemaphoreType.DMA
    any_space = pl.BlockSpec(memory_space=pltpu.HBM)
    state = pl.pallas_call(
        butterfly_kernel,
        out_shape=jax.ShapeDtypeStruct((lb, 128), F32),
        in_specs=[any_space] * 6 + [VMEM, SMEM],
        out_specs=VMEM,
        scratch_shapes=[
            pltpu.VMEM((2 * slots, points), F32),
            pltpu.VMEM((2 * slots, points), F32),
            pltpu.VMEM((slots, points), F32),
            pltpu.VMEM((64, lb), F32),
            pltpu.VMEM((256, 256), BF16),
            pltpu.VMEM((256, 256), BF16),
            pltpu.VMEM((16, points, slots), F32),
            pltpu.VMEM((8, points, slots), F32),
            pltpu.VMEM((128, slots), F32),
            pltpu.VMEM((nxy, 72, 128), F32),
            pltpu.VMEM((nxy, 64, 128), F32),
            pltpu.VMEM((nxy * slots, 256), BF16),
            pltpu.VMEM((nxy * nq, 128), F32),
            pltpu.VMEM((nxy * nq, 128), F32),
            pltpu.VMEM((nq, nxy, 128), F32),
            pltpu.VMEM((nq, nxy, 128), F32),
            pltpu.VMEM((4, lb, 128), F32),
            pltpu.VMEM((4, lb, 128), F32),
            pltpu.VMEM((4, lb, 128), F32),
            pltpu.VMEM((2, lb, 128), F32),
            pltpu.VMEM((2, lb // 2, 128), F32),
            pltpu.VMEM((nq, 2 * nxy, 128), F32),
            pltpu.VMEM((lb, 128), F32),
            pltpu.VMEM((nxy, 2 * nq, 128), F32),
            pltpu.VMEM((nxy, 2 * nq, 128), F32),
            dma((6,)),
            dma((2, 20)), dma((2, 20)), dma((nxy,)), dma((nxy,)), dma((nq,)), dma((nq,)),
            dma((4,)), dma((4,)), dma((4,)), dma((4,)),
            dma((nq,)), dma((nq,)), dma((nxy,)), dma((nxy,)),
        ],
        compiler_params=pltpu.CompilerParams(
            collective_id=0, has_side_effects=True, vmem_limit_bytes=60 * 2**20),
        name="butterfly",
    )(src_position.reshape(2 * slots, points), src_weight.reshape(2 * slots, points), src_phase, node_rate.T,
      level_weight(0), level_weight(1), block_box.reshape(1, slots), block_count)

    return pl.pallas_call(
        target_kernel,
        out_shape=jax.ShapeDtypeStruct((2, lb, target_phase.shape[1]), F32),
        in_specs=[VMEM] * 3,
        out_specs=VMEM,
        compiler_params=pltpu.CompilerParams(vmem_limit_bytes=32 * 2**20),
        name="target",
    )(state, target_phase, target_weight(side))


def solution(mesh):
    placed = (
        P(("hi", "lo"), None, None),
        P(("hi", "lo"), None, None),
        P(("hi", "lo"), None),
        P(("hi", "lo")),
        P(("hi", "lo")),
        P(("hi", "lo"), None),
        P(("hi", "lo"), None),
    )
    return jax.shard_map(
        functools.partial(local, 16),
        mesh=mesh, in_specs=placed, out_specs=P(None, ("hi", "lo"), None), check_vma=False
    )
```

```python
import functools
import math

import jax
import jax.numpy as jnp
import ml_dtypes
import numpy as np
from jax import lax
from jax.experimental import pallas as pl
from jax.experimental.pallas import tpu as pltpu
from jax.sharding import PartitionSpec as P

MESH = pl.DeviceIdType.MESH
F32 = jnp.float32
BF16 = jnp.bfloat16
VMEM = pl.BlockSpec(memory_space=pltpu.VMEM)
SMEM = pl.BlockSpec(memory_space=pltpu.SMEM)


def np_nodes():
    return np.cos((2.0 * np.arange(8) + 1.0) * math.pi / 16.0)


def np_lagrange(points):
    nodes = np_nodes()
    columns = []
    for index in range(8):
        value = np.ones_like(points)
        for other in range(8):
            if other != index:
                value = value * (points - nodes[other]) / (nodes[index] - nodes[other])
        columns.append(value)
    return np.stack(columns, axis=0)


def split_np(array):
    high = array.astype(np.float32).astype(ml_dtypes.bfloat16)
    low = (array - high.astype(np.float64)).astype(np.float32).astype(ml_dtypes.bfloat16)
    return high, low


def level_weight(parity):
    blocks = []
    for child in range(2):
        inner = np_lagrange((np_nodes() + (2.0 * child - 1.0)) / 2.0).T
        middle = np.kron(inner, np.eye(8)) if parity == 0 else np.kron(np.eye(8), inner)
        blocks.append(np.kron(np.eye(2), middle))
    weight = 0.70710678 * np.concatenate(blocks, axis=0)
    return np.concatenate(split_np(weight), axis=1)


def target_weight(side):
    grid = (2.0 * np.arange(side) + 1.0) / side - 1.0
    basis = np_lagrange(grid)
    table = np.einsum("am,bn->abmn", basis, basis).reshape(64, side * side)
    high, low = split_np(np.kron(np.eye(2), table))
    return np.concatenate([high, high, low], axis=0)


def sincos(angle):
    half = 0.5 * angle
    sq = half * half
    s = -1.0 / 39916800.0
    for term in (1.0 / 362880.0, -1.0 / 5040.0, 1.0 / 120.0, -1.0 / 6.0, 1.0):
        s = s * sq + term
    s = s * half
    c = 1.0 / 479001600.0
    for term in (-1.0 / 3628800.0, 1.0 / 40320.0, -1.0 / 720.0, 1.0 / 24.0, -0.5, 1.0):
        c = c * sq + term
    return 2.0 * s * c, 1.0 - 2.0 * s * s


def lagrange_rows(points):
    nodes = [float(v) for v in np_nodes()]
    diff = [points - v for v in nodes]
    before = [None] * 8
    after = [None] * 8
    for index in range(1, 8):
        before[index] = diff[0] if index == 1 else before[index - 1] * diff[index - 1]
    for index in range(6, -1, -1):
        after[index] = diff[7] if index == 6 else after[index + 1] * diff[index + 1]
    rows = []
    for index in range(8):
        scale = 1.0
        for other in range(8):
            if other != index:
                scale = scale / (nodes[index] - nodes[other])
        if index == 0:
            value = after[0]
        elif index == 7:
            value = before[7]
        else:
            value = before[index] * after[index]
        rows.append(value * scale)
    return rows


def split(value):
    high = value.astype(BF16)
    low = (value - high.astype(F32)).astype(BF16)
    return high, low


def leaf(pos_ref, wgt_ref, phase_ref, gx, ly, ct):
    slots = phase_ref.shape[0]
    sinv, cosv = sincos(phase_ref[...])
    w_re = wgt_ref[pl.ds(0, slots, stride=2), :]
    w_im = wgt_ref[pl.ds(1, slots, stride=2), :]
    g_re = (0.5 * (w_re * cosv - w_im * sinv)).T
    g_im = (0.5 * (w_re * sinv + w_im * cosv)).T
    x = pos_ref[pl.ds(0, slots, stride=2), :].T
    y = pos_ref[pl.ds(1, slots, stride=2), :].T
    for index, value in enumerate(lagrange_rows(x)):
        gx[index] = value * g_re
        gx[8 + index] = value * g_im
    for index, value in enumerate(lagrange_rows(y)):
        ly[index] = value

    def row(index, carry):
        total = gx[index, 0:8, :][None] * ly[:, 0:8, :]
        for part in range(1, slots // 8):
            rows = slice(8 * part, 8 * part + 8)
            total = total + gx[index, rows, :][None] * ly[:, rows, :]
        ct[pl.ds(pl.multiple_of(index * 8, 8), 8), :] = jnp.sum(total, axis=1)
        return carry

    lax.fori_loop(0, 16, row, 0)
    return ct[...].T


def exact_kernel(pos_hbm, wgt_hbm, phase_hbm, rate_hbm, w0_hbm, w1_hbm, box_ref, count_ref, out_ref,
                     pos_ref, wgt_ref, phase_ref, rate_ref, w0_ref, w1_ref, gx, ly, ct,
                     gath_a, gath_b, cat, rate_s, rate_r, rate_s2, rate_r2,
                     sib_s, sib_r, own, zrecv, z2recv, ret_s, ret_r, fin_s, fin_r,
                     in_sem, g_send, g_recv, r_send, r_recv, r2_send, r2_recv,
                     b_send, b_recv, z_send, z_recv, t_send, t_recv, f_send, f_recv):
    nxy, nq = 16, 8
    ndev = nxy * nq
    lb = 2 * ndev
    lx = 4
    slots = 128
    hi = lax.axis_index("hi")
    lo = lax.axis_index("lo")
    xy = lax.div(lo, 2)
    zlo = lax.rem(lo, 2)
    q = hi * 2 + zlo
    core = lax.rem(hi, 2)
    z = lax.div(hi, 2) * 2 + zlo

    loads = [
        pltpu.make_async_copy(src, dst, in_sem.at[i])
        for i, (src, dst) in enumerate([
            (phase_hbm, phase_ref), (wgt_hbm, wgt_ref), (pos_hbm, pos_ref),
            (rate_hbm, rate_ref), (w0_hbm, w0_ref), (w1_hbm, w1_ref)])
    ]
    for load in loads:
        load.start()

    def dev(q_at, xy_at):
        return lax.div(q_at, 2), xy_at * 2 + lax.rem(q_at, 2)

    def xy_peer(step):
        return lax.rem(xy + step, nxy)

    def q_peer(step):
        return lax.rem(q + step, nq)

    def q_of(z_at, core_at):
        return lax.div(z_at, 2) * 4 + core_at * 2 + lax.rem(z_at, 2)

    def rcopy(src, dst, send, recv, target):
        return pltpu.make_async_remote_copy(
            src_ref=src, dst_ref=dst, send_sem=send, recv_sem=recv,
            device_id=target, device_id_type=MESH)

    barrier = pltpu.get_barrier_semaphore()

    def greet_xy(step, carry):
        pl.semaphore_signal(barrier, inc=1, device_id=dev(q, xy_peer(step)), device_id_type=MESH)
        return carry

    def greet_q(step, carry):
        pl.semaphore_signal(barrier, inc=1, device_id=dev(q_peer(step), xy), device_id_type=MESH)
        return carry

    lax.fori_loop(1, nxy, greet_xy, 0)
    lax.fori_loop(1, nq, greet_q, 0)

    x_at = lax.rem(xy, 4)
    y_at = lax.div(xy, 4)
    for load in loads[0:3]:
        load.wait()
    coeff = leaf(pos_ref, wgt_ref, phase_ref, gx, ly, ct)
    lane = lax.broadcasted_iota(jnp.int32, (1, slots), 1)
    key = jnp.where(lane < count_ref[0], box_ref[...], -1).astype(F32)
    gath_a[y_at * 4 + x_at, 0:64, :] = coeff[64:128]
    gath_a[y_at * 4 + x_at, 64:72, :] = jnp.broadcast_to(key, (8, slots))
    gath_b[x_at * 4 + y_at] = coeff[0:64]
    loads[3].wait()
    rate_s[...] = jnp.concatenate([rate_ref[:, 0:ndev], rate_ref[:, ndev:lb]], axis=0).T
    pl.semaphore_wait(barrier, nxy - 1 + nq - 1)

    xs = {0: x_at, -1: lax.rem(x_at + 3, 4), 1: lax.rem(x_at + 1, 4), 2: lax.rem(x_at + 2, 4)}
    ys = {0: y_at, -1: lax.rem(y_at + 3, 4), 1: lax.rem(y_at + 1, 4), 2: lax.rem(y_at + 2, 4)}
    order = (0, -1, 1, 2)
    sent = []

    def block(part, first, second, rows=None):
        ref = gath_a if part == 0 else gath_b
        at = ys[second] * 4 + xs[first] if part == 0 else xs[second] * 4 + ys[first]
        return ref.at[at] if rows is None else ref.at[at, rows]

    def halves(part):
        return (slice(0, 40), slice(40, 72)) if part == 0 else (slice(0, 32), slice(32, 64))

    def ring_copy(part, axis, sem, first, second, way, rows=None):
        along_x = (part == 0) == (axis == 0)
        to = ys[0] * 4 + xs[way] if along_x else ys[way] * 4 + xs[0]
        ref = block(part, first, second, rows)
        return rcopy(ref, ref, g_send.at[part, sem], g_recv.at[part, sem], dev(q, to))

    def start(copy):
        copy.start()
        sent.append(copy)

    for part in range(2):
        start(ring_copy(part, 0, 0, 0, 0, 1))
        start(ring_copy(part, 0, 1, 0, 0, -1))
    for part in range(2):
        start(ring_copy(part, 1, 4, 0, 0, 1))
        start(ring_copy(part, 1, 5, 0, 0, -1))

    def rate_copy(step):
        to = xy_peer(step)
        rows_to = pl.ds(pl.multiple_of(to * nq, nq), nq)
        rows_me = pl.ds(pl.multiple_of(xy * nq, nq), nq)
        return rcopy(rate_s.at[rows_to], rate_r.at[rows_me], r_send.at[step], r_recv.at[step], dev(q, to))

    def send_rate(step, carry):
        rate_copy(step).start()
        return carry

    lax.fori_loop(1, nxy, send_rate, 0)
    rows_me = pl.ds(pl.multiple_of(xy * nq, nq), nq)
    rate_r[rows_me, :] = rate_s[rows_me, :]

    for part in range(2):
        low, high = halves(part)
        ring_copy(part, 0, 0, -1, 0, 1).wait_recv()
        start(ring_copy(part, 0, 2, -1, 0, 1, low))
        ring_copy(part, 0, 1, 1, 0, -1).wait_recv()
        start(ring_copy(part, 0, 3, 1, 0, -1, high))
    for part in range(2):
        for r in (1, 2):
            start(ring_copy(part, 1, 4 + 4 * r, order[r], 0, 1))
            start(ring_copy(part, 1, 5 + 4 * r, order[r], 0, -1))
    for part in range(2):
        low, high = halves(part)
        ring_copy(part, 0, 2, 2, 0, 1, low).wait_recv()
        ring_copy(part, 0, 3, 2, 0, -1, high).wait_recv()
        start(ring_copy(part, 1, 4 + 12, 2, 0, 1))
        start(ring_copy(part, 1, 5 + 12, 2, 0, -1))
    for r in range(4):
        for part in range(2):
            low, high = halves(part)
            ring_copy(part, 1, 4 + 4 * r, order[r], -1, 1).wait_recv()
            start(ring_copy(part, 1, 6 + 4 * r, order[r], -1, 1, low))
            ring_copy(part, 1, 5 + 4 * r, order[r], 1, -1).wait_recv()
            start(ring_copy(part, 1, 7 + 4 * r, order[r], 1, -1, high))

    def wait_rate(step, carry):
        rate_copy(step).wait()
        return carry

    lax.fori_loop(1, nxy, wait_rate, 0)
    for at in range(nq):
        rate_s2[at] = rate_r[pl.ds(at, nxy, stride=nq), :]

    def rate2_copy(step):
        to = q_peer(step)
        return rcopy(rate_s2.at[to], rate_r2.at[q], r2_send.at[step], r2_recv.at[step], dev(to, xy))

    def send_rate2(step, carry):
        rate2_copy(step).start()
        return carry

    lax.fori_loop(1, nq, send_rate2, 0)
    rate_r2[q] = rate_s2[q]

    for r in range(4):
        for part in range(2):
            low, high = halves(part)
            ring_copy(part, 1, 6 + 4 * r, order[r], 2, 1, low).wait_recv()
            ring_copy(part, 1, 7 + 4 * r, order[r], 2, -1, high).wait_recv()

    def split_rows(index, carry):
        rows_a = pl.ds(pl.multiple_of(index * slots + 64, 64), 64)
        rows_b = pl.ds(pl.multiple_of(index * slots, 64), 64)
        high, low = split(gath_a[index, 0:64, :])
        cat[rows_a, 0:128] = high
        cat[rows_a, 128:256] = low
        high, low = split(gath_b[lax.rem(index, 4) * 4 + lax.div(index, 4)])
        cat[rows_b, 0:128] = high
        cat[rows_b, 128:256] = low
        return carry

    lax.fori_loop(0, nxy, split_rows, 0)

    n = gath_a[:, 64, :].astype(jnp.int32)
    lbits = lb.bit_length() - 1
    dbits = ndev.bit_length() - 1
    j = n & (lb - 1)
    owner = n >> lbits
    holder = j & (ndev - 1)
    q_d = ((owner >> (lx + 1)) << 1) | (owner & 1)
    xy_d = (owner >> 1) & (nxy - 1)
    local_row = ((j >> dbits) << dbits) + q_d * nxy + xy_d
    code = (holder & (nq - 1)) * lb + local_row
    code = jnp.where((n >= 0) & ((holder >> 3) == xy), code, -1)
    row_id = lax.broadcasted_iota(jnp.int32, (lb, slots), 0)

    def chunk(q_at):
        rel = code - q_at * lb
        hot = [jnp.where(rel[i:i + 1, :] == row_id, 1.0, 0.0).astype(BF16) for i in range(nxy)]
        both = jnp.dot(jnp.concatenate(hot, axis=1), cat[...], preferred_element_type=F32)
        return both[:, 0:128] + both[:, 128:256]

    def sib_copy(off):
        return rcopy(sib_s.at[off], sib_r.at[off], b_send.at[off], b_recv.at[off],
                     dev(q_of(z, 1 - core), xy))

    def z_dev(off):
        return dev(q_of(lax.rem(z + off, 4), core), xy)

    up_half = rcopy(own.at[2, 0:ndev], z2recv.at[0], z_send.at[0], z_recv.at[0], z_dev(1))
    down_half = rcopy(own.at[2, ndev:lb], z2recv.at[1], z_send.at[1], z_recv.at[1], z_dev(3))
    up_full = rcopy(own.at[1], zrecv.at[0], z_send.at[2], z_recv.at[2], z_dev(1))
    down_full = rcopy(own.at[3], zrecv.at[1], z_send.at[3], z_recv.at[3], z_dev(3))

    def fold(off):
        sib_copy(off).wait()
        own[off] = own[off] + sib_r[off]

    def scatter(step, carry):
        off = lax.rem(step + 2, 4)
        to = lax.rem(z + off, 4)
        sib_s[off] = chunk(q_of(to, 1 - core))
        sib_copy(off).start()

        @pl.when(step == 1)
        def _():
            fold(2)
            up_half.start()
            down_half.start()

        @pl.when(step == 3)
        def _():
            fold(3)
            down_half.wait_recv()
            own[3, ndev:lb] = own[3, ndev:lb] + z2recv[1]
            down_full.start()

        own[off] = chunk(q_of(to, core))
        return carry

    lax.fori_loop(0, 4, scatter, 0)
    fold(1)
    up_half.wait_recv()
    own[1, 0:ndev] = own[1, 0:ndev] + z2recv[0]
    up_full.start()
    fold(0)

    def wait_rate2(step, carry):
        rate2_copy(step).wait()
        return carry

    lax.fori_loop(1, nq, wait_rate2, 0)
    sin_p, cos_p = sincos(rate_r2[...].reshape(ndev, 128))
    left = lax.broadcasted_iota(jnp.int32, (ndev, 128), 1) < 64
    cos_o = pltpu.roll(cos_p, 64, 1)
    sin_o = pltpu.roll(sin_p, 64, 1)
    cos1 = jnp.concatenate([jnp.where(left, cos_p, cos_o), jnp.where(left, cos_o, cos_p)], axis=0)
    sin1 = jnp.concatenate([jnp.where(left, -sin_p, sin_o), jnp.where(left, -sin_o, sin_p)], axis=0)
    for load in loads[4:6]:
        load.wait()

    down_full.wait_recv()
    up_full.wait_recv()
    state = own[0] + (zrecv[0] + zrecv[1])

    cosv, sinv = cos1, sin1
    sub = lax.broadcasted_iota(jnp.int32, (lb // 8, 8, 128), 1)
    for step in range(dbits):
        if step > 0:
            cosv, sinv = cosv * cos1 - sinv * sin1, sinv * cos1 + cosv * sin1
        bit = lx if step == 0 else (step - 1 if step <= lx else step)
        if bit < 3:
            tiles = state.reshape(lb // 8, 8, 128)
            dist = 1 << bit
            upper = (sub & dist) != 0
            first = jnp.where(upper, pltpu.roll(tiles, dist, 1), tiles).reshape(lb, 128)
            second = jnp.where(upper, tiles, pltpu.roll(tiles, 8 - dist, 1)).reshape(lb, 128)
        else:
            pairs = state.reshape(lb >> (bit + 1), 2, 1 << bit, 128)
            first = jnp.concatenate([pairs[:, 0:1], pairs[:, 0:1]], axis=1).reshape(lb, 128)
            second = jnp.concatenate([pairs[:, 1:2], pairs[:, 1:2]], axis=1).reshape(lb, 128)
        first = cosv * first + sinv * pltpu.roll(first, 64, 1)
        second = cosv * second + sinv * pltpu.roll(second, 64, 1)
        high, low = split(jnp.concatenate([first, second], axis=1))
        w_ref = w0_ref if step % 2 == 0 else w1_ref
        main = jnp.dot(high, w_ref[...], preferred_element_type=F32)
        rest = jnp.dot(low, w_ref[:, 0:128], preferred_element_type=F32)
        state = main[:, 0:128] + (main[:, 128:256] + rest)

    for at in range(nq):
        for jj in range(2):
            base = jj * ndev + at * nxy
            ret_s[at, jj * nxy:(jj + 1) * nxy] = state[base:base + nxy]

    def ret_copy(step):
        to = q_peer(step)
        rows = pl.ds(pl.multiple_of(q * 2 * nxy, 2 * nxy), 2 * nxy)
        return rcopy(ret_s.at[to], ret_r.at[rows], t_send.at[step], t_recv.at[step], dev(to, xy))

    def send_ret(step, carry):
        ret_copy(step).start()
        return carry

    def wait_ret(step, carry):
        ret_copy(step).wait()
        return carry

    lax.fori_loop(1, nq, send_ret, 0)
    ret_r[pl.ds(pl.multiple_of(q * 2 * nxy, 2 * nxy), 2 * nxy), :] = ret_s[q]
    lax.fori_loop(1, nq, wait_ret, 0)
    for at in range(nxy):
        fin_s[at] = ret_r[pl.ds(at, 2 * nq, stride=nxy), :]

    def fin_copy(step):
        to = xy_peer(step)
        return rcopy(fin_s.at[to], fin_r.at[xy], f_send.at[step], f_recv.at[step], dev(q, to))

    def send_fin(step, carry):
        fin_copy(step).start()
        return carry

    def wait_fin(step, carry):
        fin_copy(step).wait()
        return carry

    lax.fori_loop(1, nxy, send_fin, 0)
    fin_r[xy] = fin_s[xy]
    for copy in sent + [up_half, down_half, up_full, down_full]:
        copy.wait_send()
    lax.fori_loop(1, nxy, wait_fin, 0)
    out_ref[...] = fin_r[...].reshape(lb, 128)


S1, S2 = 40, 24
M1, M2 = S1 + 16, S2 + 8


def nt_dot(left, right):
    return lax.dot_general(left, right, (((1,), (1,)), ((), ())), preferred_element_type=F32)


def hot(cond):
    return jnp.where(cond, 1.0, 0.0)


def slot_kernel(pos_hbm, wgt_hbm, phase_hbm, rate_hbm, w0_hbm, w1_hbm, box_ref, count_ref, out_ref, flag_ref,
                pos_ref, wgt_ref, phase_ref, rate_ref, w0_ref, w1_ref, gx, ly, ct,
                rate_s, msg1_s, msg1_r, cat2, msg2_s, msg2_r, ret_s, ret_r, fin_s, fin_r,
                in_sem, a_send, a_recv, c_send, c_recv, t_send, t_recv, f_send, f_recv):
    nxy, nq = 16, 8
    ndev = nxy * nq
    lb = 2 * ndev
    lx = 4
    slots = 128
    lbits = lb.bit_length() - 1
    dbits = ndev.bit_length() - 1
    hi = lax.axis_index("hi")
    lo = lax.axis_index("lo")
    xy = lax.div(lo, 2)
    q = hi * 2 + lax.rem(lo, 2)

    loads = [
        pltpu.make_async_copy(src, dst, in_sem.at[i])
        for i, (src, dst) in enumerate([
            (phase_hbm, phase_ref), (wgt_hbm, wgt_ref), (pos_hbm, pos_ref),
            (rate_hbm, rate_ref), (w0_hbm, w0_ref), (w1_hbm, w1_ref)])
    ]
    for load in loads:
        load.start()

    def dev(q_at, xy_at):
        return lax.div(q_at, 2), xy_at * 2 + lax.rem(q_at, 2)

    def xy_peer(step):
        return lax.rem(xy + step, nxy)

    def q_peer(step):
        return lax.rem(q + step, nq)

    def rcopy(src, dst, send, recv, target):
        return pltpu.make_async_remote_copy(
            src_ref=src, dst_ref=dst, send_sem=send, recv_sem=recv,
            device_id=target, device_id_type=MESH)

    barrier = pltpu.get_barrier_semaphore()

    def greet_xy(step, carry):
        pl.semaphore_signal(barrier, inc=1, device_id=dev(q, xy_peer(step)), device_id_type=MESH)
        return carry

    def greet_q(step, carry):
        pl.semaphore_signal(barrier, inc=1, device_id=dev(q_peer(step), xy), device_id_type=MESH)
        return carry

    lax.fori_loop(1, nq, greet_q, 0)
    lax.fori_loop(1, nxy, greet_xy, 0)

    lane = lax.broadcasted_iota(jnp.int32, (1, slots), 1)
    n = jnp.where(lane < count_ref[0], box_ref[...], -1)
    j = n & (lb - 1)
    owner = n >> lbits
    holder = j & (ndev - 1)
    q_d = ((owner >> (lx + 1)) << 1) | (owner & 1)
    xy_d = (owner >> 1) & (nxy - 1)
    row_at = ((j >> dbits) << dbits) + q_d * nxy + xy_d
    live = n >= 0
    q_to = jnp.where(live, holder & (nq - 1), -1)
    before = hot(lax.broadcasted_iota(jnp.int32, (slots, slots), 0) < lax.broadcasted_iota(jnp.int32, (slots, slots), 1))
    before = before.astype(BF16)
    row128 = lax.broadcasted_iota(jnp.int32, (128, 128), 0)

    to_q = hot(q_to == lax.broadcasted_iota(jnp.int32, (16, slots), 0))
    ahead = jnp.dot(to_q.astype(BF16), before, preferred_element_type=F32)
    rank = jnp.sum(to_q * ahead, axis=0, keepdims=True).astype(jnp.int32)
    slot = jnp.where(live & (rank < S1 - 1), q_to * S1 + rank, -1)
    names = jnp.concatenate([to_q * ((holder >> 3) + 1).astype(F32), to_q * row_at.astype(F32)], axis=0)
    named = nt_dot(names.astype(BF16), hot(rank == row128).astype(BF16))
    named = named[0:8] * 256.0 + named[16:24]
    place = hot(slot == lax.broadcasted_iota(jnp.int32, (nq * S1, slots), 0)).astype(BF16)

    for load in loads[0:4]:
        load.wait()
    rate_s[...] = jnp.concatenate([rate_ref[:, 0:ndev], rate_ref[:, ndev:lb]], axis=0).T
    zeros = jnp.zeros((16, 256), BF16)
    for at in range(nq):
        cat2[at * 64 + 48:at * 64 + 64, :] = zeros
    coeff = leaf(pos_ref, wgt_ref, phase_ref, gx, ly, ct)
    both = jnp.dot(place, jnp.concatenate(split(coeff), axis=1), preferred_element_type=F32)
    both = both[:, 0:128] + both[:, 128:256]
    for at in range(nq):
        msg1_s[at, 0:S1] = both[at * S1:(at + 1) * S1]
        msg1_s[at, S1 - 1:S1] = named[at:at + 1]
        msg1_s[at, S1:M1] = rate_s[pl.ds(at, nxy, stride=nq), :]
    pl.semaphore_wait(barrier, nxy - 1 + nq - 1)

    def first_copy(step):
        to = q_peer(step)
        rows = pl.ds(pl.multiple_of(q * M1, 8), M1)
        return rcopy(msg1_s.at[to], msg1_r.at[rows], a_send.at[step], a_recv.at[step], dev(to, xy))

    def send_first(step, carry):
        first_copy(step).start()
        return carry

    def wait_first(step, carry):
        first_copy(step).wait()
        return carry

    lax.fori_loop(1, nq, send_first, 0)
    msg1_r[pl.ds(pl.multiple_of(q * M1, 8), M1), :] = msg1_s[q]
    lax.fori_loop(1, nq, wait_first, 0)

    meta = msg1_r[pl.ds(S1 - 1, nq, stride=M1), :]
    lanes8 = lax.broadcasted_iota(jnp.int32, (nq, 128), 1)
    over = jnp.max(jnp.where(lanes8 >= S1 - 1, meta, 0.0), axis=(0, 1), keepdims=True)
    meta = jnp.where(lanes8 < S1 - 1, meta, 0.0)
    odd = (lax.broadcasted_iota(jnp.int32, (nq, 128), 0) & 1) == 1
    meta = jnp.where(odd, pltpu.roll(meta, 64, 1), meta)
    codes = [(meta[2 * g:2 * g + 1] + meta[2 * g + 1:2 * g + 2]).astype(jnp.int32) for g in range(4)]
    xy_to = [code >> 8 for code in codes]
    row_to = [((code & 255) + 1).astype(F32) for code in codes]
    id16 = lax.broadcasted_iota(jnp.int32, (nxy, 128), 0) + 1
    to_xy = [hot(value == id16) for value in xy_to]
    counted = jnp.dot(jnp.concatenate(to_xy, axis=0).astype(BF16),
                      jnp.concatenate([before, jnp.ones((128, 128), BF16)], axis=1), preferred_element_type=F32)
    ranks = []
    total = jnp.zeros((nxy, 128), F32)
    for g in range(4):
        part = counted[g * nxy:(g + 1) * nxy]
        ranks.append(jnp.sum(to_xy[g] * (part[:, 0:128] + total), axis=0, keepdims=True).astype(jnp.int32))
        total = total + part[:, 128:256]
    place_id = lax.broadcasted_iota(jnp.int32, (nxy * S2, 128), 0)
    place2 = []
    for g in range(4):
        slot = jnp.where((xy_to[g] > 0) & (ranks[g] < S2 - 1), (xy_to[g] - 1) * S2 + ranks[g], -1)
        place2.append(hot(slot == place_id).astype(BF16))
    for at in range(nq):
        high, low = split(msg1_r[at * M1:at * M1 + 48, :])
        cat2[at * 64:at * 64 + 48, 0:128] = high
        cat2[at * 64:at * 64 + 48, 128:256] = low
    both = jnp.dot(jnp.concatenate(place2, axis=1), cat2[...], preferred_element_type=F32)
    both = both[:, 0:128] + both[:, 128:256]
    names = jnp.concatenate([to_xy[g] * row_to[g] for g in range(4)], axis=1)
    named = nt_dot(names.astype(BF16), jnp.concatenate([hot(ranks[g] == row128).astype(BF16) for g in range(4)], axis=1))
    lanes16 = lax.broadcasted_iota(jnp.int32, (nxy, 128), 1)
    named = named + jnp.where((lanes16 == 127) & (over > 0.0), 1.0, 0.0)
    for at in range(nxy):
        msg2_s[at, 0:S2] = both[at * S2:(at + 1) * S2]
        msg2_s[at, S2 - 1:S2] = named[at:at + 1]
        msg2_s[at, S2:M2] = msg1_r[pl.ds(S1 + at, nq, stride=M1), :]

    def second_copy(step):
        to = xy_peer(step)
        rows = pl.ds(pl.multiple_of(xy * M2, M2), M2)
        return rcopy(msg2_s.at[to], msg2_r.at[rows], c_send.at[step], c_recv.at[step], dev(q, to))

    def send_second(step, carry):
        second_copy(step).start()
        return carry

    def wait_second(step, carry):
        second_copy(step).wait()
        return carry

    lax.fori_loop(1, nxy, send_second, 0)
    msg2_r[pl.ds(pl.multiple_of(xy * M2, M2), M2), :] = msg2_s[xy]
    for load in loads[4:6]:
        load.wait()
    lax.fori_loop(1, nxy, wait_second, 0)

    meta = msg2_r[pl.ds(S2 - 1, nxy, stride=M2), :]
    over = jnp.max(jnp.where(lanes16 >= S2 - 1, meta, 0.0), axis=(0, 1), keepdims=True)
    mark = jnp.where(over > 0.0, jnp.nan, 0.0)
    meta = jnp.where(lanes16 < S2 - 1, meta, 0.0)
    sub4 = lax.broadcasted_iota(jnp.int32, (nxy, 128), 0) & 3
    for turn in range(1, 4):
        meta = jnp.where(sub4 == turn, pltpu.roll(meta, 32 * turn, 1), meta)
    row_id = lax.broadcasted_iota(jnp.int32, (lb, 128), 0)
    put = []
    for g in range(4):
        code = jnp.sum(meta[4 * g:4 * g + 4], axis=0, keepdims=True).astype(jnp.int32) - 1
        put.append(hot(code == row_id).astype(BF16))
    both = jnp.dot(jnp.concatenate(put, axis=1), jnp.concatenate(split(msg2_r[...]), axis=1), preferred_element_type=F32)
    state = both[:, 0:128] + both[:, 128:256]

    rates = jnp.concatenate([msg2_r[pl.ds(S2 + at, nxy, stride=M2), :] for at in range(nq)], axis=0)
    sin_p, cos_p = sincos(rates)
    left = lax.broadcasted_iota(jnp.int32, (ndev, 128), 1) < 64
    cos_o = pltpu.roll(cos_p, 64, 1)
    sin_o = pltpu.roll(sin_p, 64, 1)
    cos1 = jnp.concatenate([jnp.where(left, cos_p, cos_o), jnp.where(left, cos_o, cos_p)], axis=0)
    sin1 = jnp.concatenate([jnp.where(left, -sin_p, sin_o), jnp.where(left, -sin_o, sin_p)], axis=0)

    cosv, sinv = cos1, sin1
    sub = lax.broadcasted_iota(jnp.int32, (lb // 8, 8, 128), 1)
    for step in range(dbits):
        if step > 0:
            cosv, sinv = cosv * cos1 - sinv * sin1, sinv * cos1 + cosv * sin1
        bit = lx if step == 0 else (step - 1 if step <= lx else step)
        if bit < 3:
            tiles = state.reshape(lb // 8, 8, 128)
            dist = 1 << bit
            upper = (sub & dist) != 0
            first = jnp.where(upper, pltpu.roll(tiles, dist, 1), tiles).reshape(lb, 128)
            second = jnp.where(upper, tiles, pltpu.roll(tiles, 8 - dist, 1)).reshape(lb, 128)
        else:
            pairs = state.reshape(lb >> (bit + 1), 2, 1 << bit, 128)
            first = jnp.concatenate([pairs[:, 0:1], pairs[:, 0:1]], axis=1).reshape(lb, 128)
            second = jnp.concatenate([pairs[:, 1:2], pairs[:, 1:2]], axis=1).reshape(lb, 128)
        first = cosv * first + sinv * pltpu.roll(first, 64, 1)
        second = cosv * second + sinv * pltpu.roll(second, 64, 1)
        high, low = split(jnp.concatenate([first, second], axis=1))
        w_ref = w0_ref if step % 2 == 0 else w1_ref
        main = jnp.dot(high, w_ref[...], preferred_element_type=F32)
        rest = jnp.dot(low, w_ref[:, 0:128], preferred_element_type=F32)
        state = main[:, 0:128] + (main[:, 128:256] + rest)

    state = state + mark

    for at in range(nq):
        for jj in range(2):
            base = jj * ndev + at * nxy
            ret_s[at, jj * nxy:(jj + 1) * nxy] = state[base:base + nxy]

    def ret_copy(step):
        to = q_peer(step)
        rows = pl.ds(pl.multiple_of(q * 2 * nxy, 2 * nxy), 2 * nxy)
        return rcopy(ret_s.at[to], ret_r.at[rows], t_send.at[step], t_recv.at[step], dev(to, xy))

    def send_ret(step, carry):
        ret_copy(step).start()
        return carry

    def wait_ret(step, carry):
        ret_copy(step).wait()
        return carry

    lax.fori_loop(1, nq, send_ret, 0)
    ret_r[pl.ds(pl.multiple_of(q * 2 * nxy, 2 * nxy), 2 * nxy), :] = ret_s[q]
    lax.fori_loop(1, nq, wait_ret, 0)
    for at in range(nxy):
        fin_s[at] = ret_r[pl.ds(at, 2 * nq, stride=nxy), :]

    def fin_copy(step):
        to = xy_peer(step)
        return rcopy(fin_s.at[to], fin_r.at[xy], f_send.at[step], f_recv.at[step], dev(q, to))

    def send_fin(step, carry):
        fin_copy(step).start()
        return carry

    def wait_fin(step, carry):
        fin_copy(step).wait()
        return carry

    lax.fori_loop(1, nxy, send_fin, 0)
    fin_r[xy] = fin_s[xy]
    lax.fori_loop(1, nxy, wait_fin, 0)
    result = fin_r[...].reshape(lb, 128)
    out_ref[...] = result
    flag_ref[0] = jnp.max(jnp.where(result != result, 1.0, 0.0)).astype(jnp.int32)


def target_kernel(state_ref, phase_ref, table_ref, out_ref):
    lb, points = phase_ref.shape
    half = lb // 2
    for jj in range(2):
        rows = slice(jj * half, jj * half + half)
        high, low = split(state_ref[pl.ds(jj, half, stride=2), :])
        stacked = jnp.concatenate([high, low, high], axis=1)
        value = jnp.dot(stacked, table_ref[...], preferred_element_type=F32)
        sinv, cosv = sincos(phase_ref[rows, :])
        v_re = value[:, 0:points]
        v_im = value[:, points:2 * points]
        out_ref[0, rows, :] = v_re * cosv - v_im * sinv
        out_ref[1, rows, :] = v_re * sinv + v_im * cosv


def local(side, src_position, src_weight, src_phase, block_box, block_count, node_rate, target_phase):
    slots, points = src_phase.shape
    lb = node_rate.shape[0]
    nxy, nq = 16, 8
    dma = pltpu.SemaphoreType.DMA
    hbm = pl.BlockSpec(memory_space=pltpu.HBM)
    operands = (
        src_position.reshape(2 * slots, points), src_weight.reshape(2 * slots, points), src_phase, node_rate.T,
        level_weight(0), level_weight(1), block_box.reshape(1, slots), block_count)
    held = [
        pltpu.VMEM((2 * slots, points), F32),
        pltpu.VMEM((2 * slots, points), F32),
        pltpu.VMEM((slots, points), F32),
        pltpu.VMEM((64, lb), F32),
        pltpu.VMEM((256, 256), BF16),
        pltpu.VMEM((256, 256), BF16),
        pltpu.VMEM((16, points, slots), F32),
        pltpu.VMEM((8, points, slots), F32),
        pltpu.VMEM((128, slots), F32),
    ]
    returned = [
        pltpu.VMEM((nq, 2 * nxy, 128), F32),
        pltpu.VMEM((lb, 128), F32),
        pltpu.VMEM((nxy, 2 * nq, 128), F32),
        pltpu.VMEM((nxy, 2 * nq, 128), F32),
    ]
    state_shape = jax.ShapeDtypeStruct((lb, 128), F32)

    def exact():
        return pl.pallas_call(
            exact_kernel,
            out_shape=state_shape,
            in_specs=[hbm] * 6 + [VMEM, SMEM],
            out_specs=VMEM,
            scratch_shapes=held + [
                pltpu.VMEM((nxy, 72, 128), F32),
                pltpu.VMEM((nxy, 64, 128), F32),
                pltpu.VMEM((nxy * slots, 256), BF16),
                pltpu.VMEM((nxy * nq, 128), F32),
                pltpu.VMEM((nxy * nq, 128), F32),
                pltpu.VMEM((nq, nxy, 128), F32),
                pltpu.VMEM((nq, nxy, 128), F32),
                pltpu.VMEM((4, lb, 128), F32),
                pltpu.VMEM((4, lb, 128), F32),
                pltpu.VMEM((4, lb, 128), F32),
                pltpu.VMEM((2, lb, 128), F32),
                pltpu.VMEM((2, lb // 2, 128), F32),
            ] + returned + [
                dma((6,)),
                dma((2, 20)), dma((2, 20)), dma((nxy,)), dma((nxy,)), dma((nq,)), dma((nq,)),
                dma((4,)), dma((4,)), dma((4,)), dma((4,)),
                dma((nq,)), dma((nq,)), dma((nxy,)), dma((nxy,)),
            ],
            compiler_params=pltpu.CompilerParams(
                collective_id=1, has_side_effects=True, vmem_limit_bytes=60 * 2**20),
            name="exact",
        )(*operands)

    def targets(state):
        return pl.pallas_call(
            target_kernel,
            out_shape=jax.ShapeDtypeStruct((2, lb, target_phase.shape[1]), F32),
            in_specs=[VMEM] * 3,
            out_specs=VMEM,
            compiler_params=pltpu.CompilerParams(vmem_limit_bytes=32 * 2**20),
            name="target",
        )(state, target_phase, target_weight(side))

    state, flag = pl.pallas_call(
        slot_kernel,
        out_shape=(state_shape, jax.ShapeDtypeStruct((1,), jnp.int32)),
        in_specs=[hbm] * 6 + [VMEM, SMEM],
        out_specs=(VMEM, SMEM),
        scratch_shapes=held + [
            pltpu.VMEM((nxy * nq, 128), F32),
            pltpu.VMEM((nq, M1, 128), F32),
            pltpu.VMEM((nq * M1, 128), F32),
            pltpu.VMEM((nq * 64, 256), BF16),
            pltpu.VMEM((nxy, M2, 128), F32),
            pltpu.VMEM((nxy * M2, 128), F32),
        ] + returned + [
            dma((6,)),
            dma((nq,)), dma((nq,)), dma((nxy,)), dma((nxy,)),
            dma((nq,)), dma((nq,)), dma((nxy,)), dma((nxy,)),
        ],
        compiler_params=pltpu.CompilerParams(
            collective_id=0, has_side_effects=True, vmem_limit_bytes=60 * 2**20),
        name="slots",
    )(*operands)
    return lax.cond(flag[0] > 0, lambda: targets(exact()), lambda: targets(state))


def solution(mesh):
    placed = (
        P(("hi", "lo"), None, None),
        P(("hi", "lo"), None, None),
        P(("hi", "lo"), None),
        P(("hi", "lo")),
        P(("hi", "lo")),
        P(("hi", "lo"), None),
        P(("hi", "lo"), None),
    )
    return jax.shard_map(
        functools.partial(local, 16),
        mesh=mesh, in_specs=placed, out_specs=P(None, ("hi", "lo"), None), check_vma=False
    )
```

```python
import functools
import math

import jax
import jax.numpy as jnp
import ml_dtypes
import numpy as np
from jax import lax
from jax.experimental import pallas as pl
from jax.experimental.pallas import tpu as pltpu
from jax.sharding import PartitionSpec as P

MESH = pl.DeviceIdType.MESH
F32 = jnp.float32
BF16 = jnp.bfloat16
VMEM = pl.BlockSpec(memory_space=pltpu.VMEM)
SMEM = pl.BlockSpec(memory_space=pltpu.SMEM)


def np_nodes():
    return np.cos((2.0 * np.arange(8) + 1.0) * math.pi / 16.0)


def np_lagrange(points):
    nodes = np_nodes()
    columns = []
    for index in range(8):
        value = np.ones_like(points)
        for other in range(8):
            if other != index:
                value = value * (points - nodes[other]) / (nodes[index] - nodes[other])
        columns.append(value)
    return np.stack(columns, axis=0)


def split_np(array):
    high = array.astype(np.float32).astype(ml_dtypes.bfloat16)
    low = (array - high.astype(np.float64)).astype(np.float32).astype(ml_dtypes.bfloat16)
    return high, low


def level_weight(parity):
    blocks = []
    for child in range(2):
        inner = np_lagrange((np_nodes() + (2.0 * child - 1.0)) / 2.0).T
        middle = np.kron(inner, np.eye(8)) if parity == 0 else np.kron(np.eye(8), inner)
        blocks.append(np.kron(np.eye(2), middle))
    weight = 0.70710678 * np.concatenate(blocks, axis=0)
    return np.concatenate(split_np(weight), axis=1)


def target_weight(side):
    grid = (2.0 * np.arange(side) + 1.0) / side - 1.0
    basis = np_lagrange(grid)
    table = np.einsum("am,bn->abmn", basis, basis).reshape(64, side * side)
    high, low = split_np(np.kron(np.eye(2), table))
    return np.concatenate([high, high, low], axis=0)


def sincos(angle):
    half = 0.5 * angle
    sq = half * half
    s = -1.0 / 39916800.0
    for term in (1.0 / 362880.0, -1.0 / 5040.0, 1.0 / 120.0, -1.0 / 6.0, 1.0):
        s = s * sq + term
    s = s * half
    c = 1.0 / 479001600.0
    for term in (-1.0 / 3628800.0, 1.0 / 40320.0, -1.0 / 720.0, 1.0 / 24.0, -0.5, 1.0):
        c = c * sq + term
    return 2.0 * s * c, 1.0 - 2.0 * s * s


def lagrange_rows(points):
    nodes = [float(v) for v in np_nodes()]
    diff = [points - v for v in nodes]
    before = [None] * 8
    after = [None] * 8
    for index in range(1, 8):
        before[index] = diff[0] if index == 1 else before[index - 1] * diff[index - 1]
    for index in range(6, -1, -1):
        after[index] = diff[7] if index == 6 else after[index + 1] * diff[index + 1]
    rows = []
    for index in range(8):
        scale = 1.0
        for other in range(8):
            if other != index:
                scale = scale / (nodes[index] - nodes[other])
        if index == 0:
            value = after[0]
        elif index == 7:
            value = before[7]
        else:
            value = before[index] * after[index]
        rows.append(value * scale)
    return rows


def split(value):
    high = value.astype(BF16)
    low = (value - high.astype(F32)).astype(BF16)
    return high, low


def leaf(pos_ref, wgt_ref, phase_ref, gx, ly, ct):
    slots = phase_ref.shape[0]
    sinv, cosv = sincos(phase_ref[...])
    w_re = wgt_ref[pl.ds(0, slots, stride=2), :]
    w_im = wgt_ref[pl.ds(1, slots, stride=2), :]
    g_re = (0.5 * (w_re * cosv - w_im * sinv)).T
    g_im = (0.5 * (w_re * sinv + w_im * cosv)).T
    x = pos_ref[pl.ds(0, slots, stride=2), :].T
    y = pos_ref[pl.ds(1, slots, stride=2), :].T
    for index, value in enumerate(lagrange_rows(x)):
        gx[index] = value * g_re
        gx[8 + index] = value * g_im
    for index, value in enumerate(lagrange_rows(y)):
        ly[index] = value

    def row(index, carry):
        total = gx[index, 0:8, :][None] * ly[:, 0:8, :]
        for part in range(1, slots // 8):
            rows = slice(8 * part, 8 * part + 8)
            total = total + gx[index, rows, :][None] * ly[:, rows, :]
        ct[pl.ds(pl.multiple_of(index * 8, 8), 8), :] = jnp.sum(total, axis=1)
        return carry

    lax.fori_loop(0, 16, row, 0)
    return ct[...].T


def exact_kernel(pos_hbm, wgt_hbm, phase_hbm, rate_hbm, w0_hbm, w1_hbm, key_ref, out_ref,
                     pos_ref, wgt_ref, phase_ref, rate_ref, w0_ref, w1_ref, gx, ly, ct,
                     gath_a, gath_b, cat, rate_s, rate_r, rate_s2, rate_r2,
                     sib_s, sib_r, own, zrecv, z2recv, ret_s, ret_r, fin_s, fin_r,
                     in_sem, g_send, g_recv, r_send, r_recv, r2_send, r2_recv,
                     b_send, b_recv, z_send, z_recv, t_send, t_recv, f_send, f_recv):
    nxy, nq = 16, 8
    ndev = nxy * nq
    lb = 2 * ndev
    lx = 4
    slots = 128
    hi = lax.axis_index("hi")
    lo = lax.axis_index("lo")
    xy = lax.div(lo, 2)
    zlo = lax.rem(lo, 2)
    q = hi * 2 + zlo
    core = lax.rem(hi, 2)
    z = lax.div(hi, 2) * 2 + zlo

    loads = [
        pltpu.make_async_copy(src, dst, in_sem.at[i])
        for i, (src, dst) in enumerate([
            (phase_hbm, phase_ref), (wgt_hbm, wgt_ref), (pos_hbm, pos_ref),
            (rate_hbm, rate_ref), (w0_hbm, w0_ref), (w1_hbm, w1_ref)])
    ]
    for load in loads:
        load.start()

    def dev(q_at, xy_at):
        return lax.div(q_at, 2), xy_at * 2 + lax.rem(q_at, 2)

    def xy_peer(step):
        return lax.rem(xy + step, nxy)

    def q_peer(step):
        return lax.rem(q + step, nq)

    def q_of(z_at, core_at):
        return lax.div(z_at, 2) * 4 + core_at * 2 + lax.rem(z_at, 2)

    def rcopy(src, dst, send, recv, target):
        return pltpu.make_async_remote_copy(
            src_ref=src, dst_ref=dst, send_sem=send, recv_sem=recv,
            device_id=target, device_id_type=MESH)

    barrier = pltpu.get_barrier_semaphore()

    def greet_xy(step, carry):
        pl.semaphore_signal(barrier, inc=1, device_id=dev(q, xy_peer(step)), device_id_type=MESH)
        return carry

    def greet_q(step, carry):
        pl.semaphore_signal(barrier, inc=1, device_id=dev(q_peer(step), xy), device_id_type=MESH)
        return carry

    lax.fori_loop(1, nxy, greet_xy, 0)
    lax.fori_loop(1, nq, greet_q, 0)

    x_at = lax.rem(xy, 4)
    y_at = lax.div(xy, 4)
    for load in loads[0:3]:
        load.wait()
    coeff = leaf(pos_ref, wgt_ref, phase_ref, gx, ly, ct)
    key = key_ref[...].astype(F32)
    gath_a[y_at * 4 + x_at, 0:64, :] = coeff[64:128]
    gath_a[y_at * 4 + x_at, 64:72, :] = jnp.broadcast_to(key, (8, slots))
    gath_b[x_at * 4 + y_at] = coeff[0:64]
    loads[3].wait()
    rate_s[...] = jnp.concatenate([rate_ref[:, 0:ndev], rate_ref[:, ndev:lb]], axis=0).T
    pl.semaphore_wait(barrier, nxy - 1 + nq - 1)

    xs = {0: x_at, -1: lax.rem(x_at + 3, 4), 1: lax.rem(x_at + 1, 4), 2: lax.rem(x_at + 2, 4)}
    ys = {0: y_at, -1: lax.rem(y_at + 3, 4), 1: lax.rem(y_at + 1, 4), 2: lax.rem(y_at + 2, 4)}
    order = (0, -1, 1, 2)
    sent = []

    def block(part, first, second, rows=None):
        ref = gath_a if part == 0 else gath_b
        at = ys[second] * 4 + xs[first] if part == 0 else xs[second] * 4 + ys[first]
        return ref.at[at] if rows is None else ref.at[at, rows]

    def halves(part):
        return (slice(0, 40), slice(40, 72)) if part == 0 else (slice(0, 32), slice(32, 64))

    def ring_copy(part, axis, sem, first, second, way, rows=None):
        along_x = (part == 0) == (axis == 0)
        to = ys[0] * 4 + xs[way] if along_x else ys[way] * 4 + xs[0]
        ref = block(part, first, second, rows)
        return rcopy(ref, ref, g_send.at[part, sem], g_recv.at[part, sem], dev(q, to))

    def start(copy):
        copy.start()
        sent.append(copy)

    for part in range(2):
        start(ring_copy(part, 0, 0, 0, 0, 1))
        start(ring_copy(part, 0, 1, 0, 0, -1))
    for part in range(2):
        start(ring_copy(part, 1, 4, 0, 0, 1))
        start(ring_copy(part, 1, 5, 0, 0, -1))

    def rate_copy(step):
        to = xy_peer(step)
        rows_to = pl.ds(pl.multiple_of(to * nq, nq), nq)
        rows_me = pl.ds(pl.multiple_of(xy * nq, nq), nq)
        return rcopy(rate_s.at[rows_to], rate_r.at[rows_me], r_send.at[step], r_recv.at[step], dev(q, to))

    def send_rate(step, carry):
        rate_copy(step).start()
        return carry

    lax.fori_loop(1, nxy, send_rate, 0)
    rows_me = pl.ds(pl.multiple_of(xy * nq, nq), nq)
    rate_r[rows_me, :] = rate_s[rows_me, :]

    for part in range(2):
        low, high = halves(part)
        ring_copy(part, 0, 0, -1, 0, 1).wait_recv()
        start(ring_copy(part, 0, 2, -1, 0, 1, low))
        ring_copy(part, 0, 1, 1, 0, -1).wait_recv()
        start(ring_copy(part, 0, 3, 1, 0, -1, high))
    for part in range(2):
        for r in (1, 2):
            start(ring_copy(part, 1, 4 + 4 * r, order[r], 0, 1))
            start(ring_copy(part, 1, 5 + 4 * r, order[r], 0, -1))
    for part in range(2):
        low, high = halves(part)
        ring_copy(part, 0, 2, 2, 0, 1, low).wait_recv()
        ring_copy(part, 0, 3, 2, 0, -1, high).wait_recv()
        start(ring_copy(part, 1, 4 + 12, 2, 0, 1))
        start(ring_copy(part, 1, 5 + 12, 2, 0, -1))
    for r in range(4):
        for part in range(2):
            low, high = halves(part)
            ring_copy(part, 1, 4 + 4 * r, order[r], -1, 1).wait_recv()
            start(ring_copy(part, 1, 6 + 4 * r, order[r], -1, 1, low))
            ring_copy(part, 1, 5 + 4 * r, order[r], 1, -1).wait_recv()
            start(ring_copy(part, 1, 7 + 4 * r, order[r], 1, -1, high))

    def wait_rate(step, carry):
        rate_copy(step).wait()
        return carry

    lax.fori_loop(1, nxy, wait_rate, 0)
    for at in range(nq):
        rate_s2[at] = rate_r[pl.ds(at, nxy, stride=nq), :]

    def rate2_copy(step):
        to = q_peer(step)
        return rcopy(rate_s2.at[to], rate_r2.at[q], r2_send.at[step], r2_recv.at[step], dev(to, xy))

    def send_rate2(step, carry):
        rate2_copy(step).start()
        return carry

    lax.fori_loop(1, nq, send_rate2, 0)
    rate_r2[q] = rate_s2[q]

    for r in range(4):
        for part in range(2):
            low, high = halves(part)
            ring_copy(part, 1, 6 + 4 * r, order[r], 2, 1, low).wait_recv()
            ring_copy(part, 1, 7 + 4 * r, order[r], 2, -1, high).wait_recv()

    def split_rows(index, carry):
        rows_a = pl.ds(pl.multiple_of(index * slots + 64, 64), 64)
        rows_b = pl.ds(pl.multiple_of(index * slots, 64), 64)
        high, low = split(gath_a[index, 0:64, :])
        cat[rows_a, 0:128] = high
        cat[rows_a, 128:256] = low
        high, low = split(gath_b[lax.rem(index, 4) * 4 + lax.div(index, 4)])
        cat[rows_b, 0:128] = high
        cat[rows_b, 128:256] = low
        return carry

    lax.fori_loop(0, nxy, split_rows, 0)

    n = gath_a[:, 64, :].astype(jnp.int32)
    lbits = lb.bit_length() - 1
    dbits = ndev.bit_length() - 1
    j = n & (lb - 1)
    owner = n >> lbits
    holder = j & (ndev - 1)
    q_d = ((owner >> (lx + 1)) << 1) | (owner & 1)
    xy_d = (owner >> 1) & (nxy - 1)
    local_row = ((j >> dbits) << dbits) + q_d * nxy + xy_d
    code = (holder & (nq - 1)) * lb + local_row
    code = jnp.where((n >= 0) & ((holder >> 3) == xy), code, -1)
    row_id = lax.broadcasted_iota(jnp.int32, (lb, slots), 0)

    def chunk(q_at):
        rel = code - q_at * lb
        hot = [jnp.where(rel[i:i + 1, :] == row_id, 1.0, 0.0).astype(BF16) for i in range(nxy)]
        both = jnp.dot(jnp.concatenate(hot, axis=1), cat[...], preferred_element_type=F32)
        return both[:, 0:128] + both[:, 128:256]

    def sib_copy(off):
        return rcopy(sib_s.at[off], sib_r.at[off], b_send.at[off], b_recv.at[off],
                     dev(q_of(z, 1 - core), xy))

    def z_dev(off):
        return dev(q_of(lax.rem(z + off, 4), core), xy)

    up_half = rcopy(own.at[2, 0:ndev], z2recv.at[0], z_send.at[0], z_recv.at[0], z_dev(1))
    down_half = rcopy(own.at[2, ndev:lb], z2recv.at[1], z_send.at[1], z_recv.at[1], z_dev(3))
    up_full = rcopy(own.at[1], zrecv.at[0], z_send.at[2], z_recv.at[2], z_dev(1))
    down_full = rcopy(own.at[3], zrecv.at[1], z_send.at[3], z_recv.at[3], z_dev(3))

    def fold(off):
        sib_copy(off).wait()
        own[off] = own[off] + sib_r[off]

    def scatter(step, carry):
        off = lax.rem(step + 2, 4)
        to = lax.rem(z + off, 4)
        sib_s[off] = chunk(q_of(to, 1 - core))
        sib_copy(off).start()

        @pl.when(step == 1)
        def _():
            fold(2)
            up_half.start()
            down_half.start()

        @pl.when(step == 3)
        def _():
            fold(3)
            down_half.wait_recv()
            own[3, ndev:lb] = own[3, ndev:lb] + z2recv[1]
            down_full.start()

        own[off] = chunk(q_of(to, core))
        return carry

    lax.fori_loop(0, 4, scatter, 0)
    fold(1)
    up_half.wait_recv()
    own[1, 0:ndev] = own[1, 0:ndev] + z2recv[0]
    up_full.start()
    fold(0)

    def wait_rate2(step, carry):
        rate2_copy(step).wait()
        return carry

    lax.fori_loop(1, nq, wait_rate2, 0)
    sin_p, cos_p = sincos(rate_r2[...].reshape(ndev, 128))
    left = lax.broadcasted_iota(jnp.int32, (ndev, 128), 1) < 64
    cos_o = pltpu.roll(cos_p, 64, 1)
    sin_o = pltpu.roll(sin_p, 64, 1)
    cos1 = jnp.concatenate([jnp.where(left, cos_p, cos_o), jnp.where(left, cos_o, cos_p)], axis=0)
    sin1 = jnp.concatenate([jnp.where(left, -sin_p, sin_o), jnp.where(left, -sin_o, sin_p)], axis=0)
    for load in loads[4:6]:
        load.wait()

    down_full.wait_recv()
    up_full.wait_recv()
    state = own[0] + (zrecv[0] + zrecv[1])

    cosv, sinv = cos1, sin1
    sub = lax.broadcasted_iota(jnp.int32, (lb // 8, 8, 128), 1)
    for step in range(dbits):
        if step > 0:
            cosv, sinv = cosv * cos1 - sinv * sin1, sinv * cos1 + cosv * sin1
        bit = lx if step == 0 else (step - 1 if step <= lx else step)
        if bit < 3:
            tiles = state.reshape(lb // 8, 8, 128)
            dist = 1 << bit
            upper = (sub & dist) != 0
            first = jnp.where(upper, pltpu.roll(tiles, dist, 1), tiles).reshape(lb, 128)
            second = jnp.where(upper, tiles, pltpu.roll(tiles, 8 - dist, 1)).reshape(lb, 128)
        else:
            pairs = state.reshape(lb >> (bit + 1), 2, 1 << bit, 128)
            first = jnp.concatenate([pairs[:, 0:1], pairs[:, 0:1]], axis=1).reshape(lb, 128)
            second = jnp.concatenate([pairs[:, 1:2], pairs[:, 1:2]], axis=1).reshape(lb, 128)
        first = cosv * first + sinv * pltpu.roll(first, 64, 1)
        second = cosv * second + sinv * pltpu.roll(second, 64, 1)
        high, low = split(jnp.concatenate([first, second], axis=1))
        w_ref = w0_ref if step % 2 == 0 else w1_ref
        main = jnp.dot(high, w_ref[...], preferred_element_type=F32)
        rest = jnp.dot(low, w_ref[:, 0:128], preferred_element_type=F32)
        state = main[:, 0:128] + (main[:, 128:256] + rest)

    for at in range(nq):
        for jj in range(2):
            base = jj * ndev + at * nxy
            ret_s[at, jj * nxy:(jj + 1) * nxy] = state[base:base + nxy]

    def ret_copy(step):
        to = q_peer(step)
        rows = pl.ds(pl.multiple_of(q * 2 * nxy, 2 * nxy), 2 * nxy)
        return rcopy(ret_s.at[to], ret_r.at[rows], t_send.at[step], t_recv.at[step], dev(to, xy))

    def send_ret(step, carry):
        ret_copy(step).start()
        return carry

    def wait_ret(step, carry):
        ret_copy(step).wait()
        return carry

    lax.fori_loop(1, nq, send_ret, 0)
    ret_r[pl.ds(pl.multiple_of(q * 2 * nxy, 2 * nxy), 2 * nxy), :] = ret_s[q]
    lax.fori_loop(1, nq, wait_ret, 0)
    for at in range(nxy):
        fin_s[at] = ret_r[pl.ds(at, 2 * nq, stride=nxy), :]

    def fin_copy(step):
        to = xy_peer(step)
        return rcopy(fin_s.at[to], fin_r.at[xy], f_send.at[step], f_recv.at[step], dev(q, to))

    def send_fin(step, carry):
        fin_copy(step).start()
        return carry

    def wait_fin(step, carry):
        fin_copy(step).wait()
        return carry

    lax.fori_loop(1, nxy, send_fin, 0)
    fin_r[xy] = fin_s[xy]
    for copy in sent + [up_half, down_half, up_full, down_full]:
        copy.wait_send()
    lax.fori_loop(1, nxy, wait_fin, 0)
    out_ref[...] = fin_r[...].reshape(lb, 128)


S1, S2 = 40, 24
M1, M2 = S1 + 16, S2 + 8


def far(step, size):
    return min(step, size - step)


XY_STEPS = sorted(range(1, 16), key=lambda s: -far(s // 4, 4) - far(s % 4, 4))
Q_STEPS = sorted(range(1, 8), key=lambda s: -far(s // 4 * 2 + s % 2, 4))
ALL_STEPS = sorted(range(1, 128), key=lambda s: -far(s // 64 * 2 + s % 2, 4) - far(s // 8 % 4, 4) - far(s // 2 % 4, 4))


def nt_dot(left, right):
    return lax.dot_general(left, right, (((1,), (1,)), ((), ())), preferred_element_type=F32)


def hot(cond):
    return jnp.where(cond, 1.0, 0.0)


def slot_kernel(pos_hbm, wgt_hbm, phase_hbm, rate_hbm, w0_hbm, w1_hbm, box_hbm, count_ref, out_ref, flag_ref, key_ref,
                pos_ref, wgt_ref, phase_ref, rate_ref, w0_ref, w1_ref, box_ref, gx, ly, ct,
                rate_s, msg1_s, msg1_r, cat2, msg2_s, msg2_r, cos_s, sin_s, ret_s, ret_r,
                in_sem, a_send, a_recv, c_send, c_recv, t_send, t_recv):
    nxy, nq = 16, 8
    ndev = nxy * nq
    lb = 2 * ndev
    slots = 128
    lbits = lb.bit_length() - 1
    dbits = ndev.bit_length() - 1
    hi = lax.axis_index("hi")
    lo = lax.axis_index("lo")
    xy = lax.div(lo, 2)
    q = hi * 2 + lax.rem(lo, 2)

    def dev(q_at, xy_at):
        return lax.div(q_at, 2), xy_at * 2 + lax.rem(q_at, 2)

    def xy_peer(step):
        return lax.rem(xy + step, nxy)

    def q_peer(step):
        return lax.rem(q + step, nq)

    def rcopy(src, dst, send, recv, target):
        return pltpu.make_async_remote_copy(
            src_ref=src, dst_ref=dst, send_sem=send, recv_sem=recv,
            device_id=target, device_id_type=MESH)

    barrier = pltpu.get_barrier_semaphore()
    for step in XY_STEPS:
        pl.semaphore_signal(barrier, inc=1, device_id=dev(q, xy_peer(step)), device_id_type=MESH)
    for step in Q_STEPS:
        pl.semaphore_signal(barrier, inc=1, device_id=dev(q_peer(step), xy), device_id_type=MESH)

    loads = [
        pltpu.make_async_copy(src, dst, in_sem.at[i])
        for i, (src, dst) in enumerate([
            (box_hbm, box_ref), (phase_hbm, phase_ref), (wgt_hbm, wgt_ref), (pos_hbm, pos_ref),
            (rate_hbm, rate_ref), (w0_hbm, w0_ref), (w1_hbm, w1_ref)])
    ]
    for load in loads:
        load.start()

    loads[0].wait()
    lane = lax.broadcasted_iota(jnp.int32, (1, slots), 1)
    n = jnp.where(lane < count_ref[0], box_ref[...], -1)
    key_ref[...] = n
    j = n & (lb - 1)
    owner = n >> lbits
    holder = j & (ndev - 1)
    row_at = owner * 2 + (j >> dbits)
    live = n >= 0
    q_to = jnp.where(live, holder & (nq - 1), -1)
    before = hot(lax.broadcasted_iota(jnp.int32, (slots, slots), 0) < lax.broadcasted_iota(jnp.int32, (slots, slots), 1))
    before = before.astype(BF16)
    row128 = lax.broadcasted_iota(jnp.int32, (128, 128), 0)

    to_q = hot(q_to == lax.broadcasted_iota(jnp.int32, (16, slots), 0))
    ahead = jnp.dot(to_q.astype(BF16), before, preferred_element_type=F32)
    rank = jnp.sum(to_q * ahead, axis=0, keepdims=True).astype(jnp.int32)
    slot = jnp.where(live & (rank < S1 - 1), q_to * S1 + rank, -1)
    names = jnp.concatenate([to_q * ((holder >> 3) + 1).astype(F32), to_q * row_at.astype(F32)], axis=0)
    named = nt_dot(names.astype(BF16), hot(rank == row128).astype(BF16))
    named = named[0:8] * 256.0 + named[16:24]
    place = hot(slot == lax.broadcasted_iota(jnp.int32, (nq * S1, slots), 0)).astype(BF16)

    for load in loads[1:5]:
        load.wait()
    rate_s[...] = jnp.concatenate([rate_ref[:, 0:ndev], rate_ref[:, ndev:lb]], axis=0).T
    zeros = jnp.zeros((16, 256), BF16)
    for at in range(nq):
        cat2[at * 64 + 48:at * 64 + 64, :] = zeros
    coeff = leaf(pos_ref, wgt_ref, phase_ref, gx, ly, ct)
    both = jnp.dot(place, jnp.concatenate(split(coeff), axis=1), preferred_element_type=F32)
    both = both[:, 0:128] + both[:, 128:256]
    for at in range(nq):
        msg1_s[at, 0:S1] = both[at * S1:(at + 1) * S1]
        msg1_s[at, S1 - 1:S1] = named[at:at + 1]
        msg1_s[at, S1:M1] = rate_s[pl.ds(at, nxy, stride=nq), :]
    pl.semaphore_wait(barrier, nxy - 1 + nq - 1)

    def first_copy(step):
        to = q_peer(step)
        rows = pl.ds(pl.multiple_of(q * M1, 8), M1)
        return rcopy(msg1_s.at[to], msg1_r.at[rows], a_send.at[step], a_recv.at[step], dev(to, xy))

    for step in Q_STEPS:
        first_copy(step).start()
    msg1_r[pl.ds(pl.multiple_of(q * M1, 8), M1), :] = msg1_s[q]
    for step in reversed(Q_STEPS):
        first_copy(step).wait_recv()

    meta = msg1_r[pl.ds(S1 - 1, nq, stride=M1), :]
    lanes8 = lax.broadcasted_iota(jnp.int32, (nq, 128), 1)
    over = jnp.max(jnp.where(lanes8 >= S1 - 1, meta, 0.0), axis=(0, 1), keepdims=True)
    meta = jnp.where(lanes8 < S1 - 1, meta, 0.0)
    odd = (lax.broadcasted_iota(jnp.int32, (nq, 128), 0) & 1) == 1
    meta = jnp.where(odd, pltpu.roll(meta, 64, 1), meta)
    codes = [(meta[2 * g:2 * g + 1] + meta[2 * g + 1:2 * g + 2]).astype(jnp.int32) for g in range(4)]
    xy_to = [code >> 8 for code in codes]
    row_to = [((code & 255) + 1).astype(F32) for code in codes]
    id16 = lax.broadcasted_iota(jnp.int32, (nxy, 128), 0) + 1
    to_xy = [hot(value == id16) for value in xy_to]
    counted = jnp.dot(jnp.concatenate(to_xy, axis=0).astype(BF16),
                      jnp.concatenate([before, jnp.ones((128, 128), BF16)], axis=1), preferred_element_type=F32)
    ranks = []
    total = jnp.zeros((nxy, 128), F32)
    for g in range(4):
        part = counted[g * nxy:(g + 1) * nxy]
        ranks.append(jnp.sum(to_xy[g] * (part[:, 0:128] + total), axis=0, keepdims=True).astype(jnp.int32))
        total = total + part[:, 128:256]
    place_id = lax.broadcasted_iota(jnp.int32, (nxy * S2, 128), 0)
    place2 = []
    for g in range(4):
        slot = jnp.where((xy_to[g] > 0) & (ranks[g] < S2 - 1), (xy_to[g] - 1) * S2 + ranks[g], -1)
        place2.append(hot(slot == place_id).astype(BF16))
    for at in range(nq):
        high, low = split(msg1_r[at * M1:at * M1 + 48, :])
        cat2[at * 64:at * 64 + 48, 0:128] = high
        cat2[at * 64:at * 64 + 48, 128:256] = low
    both = jnp.dot(jnp.concatenate(place2, axis=1), cat2[...], preferred_element_type=F32)
    both = both[:, 0:128] + both[:, 128:256]
    names = jnp.concatenate([to_xy[g] * row_to[g] for g in range(4)], axis=1)
    named = nt_dot(names.astype(BF16), jnp.concatenate([hot(ranks[g] == row128).astype(BF16) for g in range(4)], axis=1))
    lanes16 = lax.broadcasted_iota(jnp.int32, (nxy, 128), 1)
    named = named + jnp.where((lanes16 == 127) & (over > 0.0), 1.0, 0.0)
    for at in range(nxy):
        msg2_s[at, 0:S2] = both[at * S2:(at + 1) * S2]
        msg2_s[at, S2 - 1:S2] = named[at:at + 1]
        msg2_s[at, S2:M2] = msg1_r[pl.ds(S1 + at, nq, stride=M1), :]

    def second_copy(step):
        to = xy_peer(step)
        rows = pl.ds(pl.multiple_of(xy * M2, M2), M2)
        return rcopy(msg2_s.at[to], msg2_r.at[rows], c_send.at[step], c_recv.at[step], dev(q, to))

    for step in XY_STEPS:
        second_copy(step).start()
    msg2_r[pl.ds(pl.multiple_of(xy * M2, M2), M2), :] = msg2_s[xy]
    for load in loads[5:7]:
        load.wait()
    for step in reversed(XY_STEPS):
        second_copy(step).wait_recv()

    meta = msg2_r[pl.ds(S2 - 1, nxy, stride=M2), :]
    over = jnp.max(jnp.where(lanes16 >= S2 - 1, meta, 0.0), axis=(0, 1), keepdims=True)
    mark = jnp.where(over > 0.0, jnp.nan, 0.0)
    meta = jnp.where(lanes16 < S2 - 1, meta, 0.0)
    sub4 = lax.broadcasted_iota(jnp.int32, (nxy, 128), 0) & 3
    for turn in range(1, 4):
        meta = jnp.where(sub4 == turn, pltpu.roll(meta, 32 * turn, 1), meta)
    row_id = lax.broadcasted_iota(jnp.int32, (lb, 128), 0)
    put = []
    for g in range(4):
        code = jnp.sum(meta[4 * g:4 * g + 4], axis=0, keepdims=True).astype(jnp.int32) - 1
        put.append(hot(code == row_id).astype(BF16))
    both = jnp.dot(jnp.concatenate(put, axis=1), jnp.concatenate(split(msg2_r[...]), axis=1), preferred_element_type=F32)
    state = both[:, 0:128] + both[:, 128:256]

    rates = jnp.concatenate([msg2_r[pl.ds(S2 + at, nxy, stride=M2), :] for at in range(nq)], axis=0)
    sin_p, cos_p = sincos(rates)
    left = lax.broadcasted_iota(jnp.int32, (ndev, 128), 1) < 64
    cos_o = pltpu.roll(cos_p, 64, 1)
    sin_o = pltpu.roll(sin_p, 64, 1)
    for at in range(nq):
        rows = slice(at * nxy, (at + 1) * nxy)
        base = 2 * (at // 2 * 2 * nxy + at % 2)
        even = pl.ds(base, nxy, stride=4)
        uneven = pl.ds(base + 1, nxy, stride=4)
        lr = left[rows]
        cos_s[even, :] = jnp.where(lr, cos_p[rows], cos_o[rows])
        cos_s[uneven, :] = jnp.where(lr, cos_o[rows], cos_p[rows])
        sin_s[even, :] = jnp.where(lr, -sin_p[rows], sin_o[rows])
        sin_s[uneven, :] = jnp.where(lr, -sin_o[rows], sin_p[rows])
    cos1 = cos_s[...]
    sin1 = sin_s[...]

    cosv, sinv = cos1, sin1
    sub = lax.broadcasted_iota(jnp.int32, (lb // 8, 8, 128), 1)
    for step in range(dbits):
        if step > 0:
            cosv, sinv = cosv * cos1 - sinv * sin1, sinv * cos1 + cosv * sin1
        bit = step + 1
        if bit < 3:
            tiles = state.reshape(lb // 8, 8, 128)
            dist = 1 << bit
            upper = (sub & dist) != 0
            first = jnp.where(upper, pltpu.roll(tiles, dist, 1), tiles).reshape(lb, 128)
            second = jnp.where(upper, tiles, pltpu.roll(tiles, 8 - dist, 1)).reshape(lb, 128)
        else:
            pairs = state.reshape(lb >> (bit + 1), 2, 1 << bit, 128)
            first = jnp.concatenate([pairs[:, 0:1], pairs[:, 0:1]], axis=1).reshape(lb, 128)
            second = jnp.concatenate([pairs[:, 1:2], pairs[:, 1:2]], axis=1).reshape(lb, 128)
        first = cosv * first + sinv * pltpu.roll(first, 64, 1)
        second = cosv * second + sinv * pltpu.roll(second, 64, 1)
        high, low = split(jnp.concatenate([first, second], axis=1))
        w_ref = w0_ref if step % 2 == 0 else w1_ref
        main = jnp.dot(high, w_ref[...], preferred_element_type=F32)
        rest = jnp.dot(low, w_ref[:, 0:128], preferred_element_type=F32)
        state = main[:, 0:128] + (main[:, 128:256] + rest)

    state = state + mark

    ret_s[...] = state.reshape(ndev, 2, 128)
    holder_at = xy * nq + q

    def ret_copy(step):
        hi_to = lax.rem(hi + step // 32, 4)
        lo_to = lax.rem(lo + step % 32, 32)
        return rcopy(ret_s.at[hi_to * 32 + lo_to], ret_r.at[holder_at], t_send, t_recv, (hi_to, lo_to))

    for step in ALL_STEPS:
        ret_copy(step).start()
    ret_r[holder_at] = ret_s[hi * 32 + lo]
    for step in Q_STEPS:
        first_copy(step).wait_send()
    for step in XY_STEPS:
        second_copy(step).wait_send()
    every = rcopy(ret_s.at[0:ndev - 1], ret_r.at[0:ndev - 1], t_send, t_recv, dev(q_peer(1), xy))
    every.wait_recv()
    result = ret_r[...]
    out_ref[...] = result
    flag_ref[0] = jnp.max(jnp.where(result != result, 1.0, 0.0)).astype(jnp.int32)
    every.wait_send()


def target_kernel(state_ref, phase_ref, table_ref, out_ref):
    lb, points = phase_ref.shape
    half = lb // 2
    for jj in range(2):
        rows = slice(jj * half, jj * half + half)
        high, low = split(state_ref[pl.ds(jj, half, stride=2), :])
        stacked = jnp.concatenate([high, low, high], axis=1)
        value = jnp.dot(stacked, table_ref[...], preferred_element_type=F32)
        sinv, cosv = sincos(phase_ref[rows, :])
        v_re = value[:, 0:points]
        v_im = value[:, points:2 * points]
        out_ref[0, rows, :] = v_re * cosv - v_im * sinv
        out_ref[1, rows, :] = v_re * sinv + v_im * cosv


def local(side, src_position, src_weight, src_phase, block_box, block_count, node_rate, target_phase):
    slots, points = src_phase.shape
    lb = node_rate.shape[0]
    nxy, nq = 16, 8
    dma = pltpu.SemaphoreType.DMA
    hbm = pl.BlockSpec(memory_space=pltpu.HBM)
    operands = (
        src_position.reshape(2 * slots, points), src_weight.reshape(2 * slots, points), src_phase, node_rate.T,
        level_weight(0), level_weight(1), block_box.reshape(1, slots), block_count)
    held = [
        pltpu.VMEM((2 * slots, points), F32),
        pltpu.VMEM((2 * slots, points), F32),
        pltpu.VMEM((slots, points), F32),
        pltpu.VMEM((64, lb), F32),
        pltpu.VMEM((256, 256), BF16),
        pltpu.VMEM((256, 256), BF16),
        pltpu.VMEM((1, slots), jnp.int32),
        pltpu.VMEM((16, points, slots), F32),
        pltpu.VMEM((8, points, slots), F32),
        pltpu.VMEM((128, slots), F32),
    ]
    returned = [
        pltpu.VMEM((nq, 2 * nxy, 128), F32),
        pltpu.VMEM((lb, 128), F32),
        pltpu.VMEM((nxy, 2 * nq, 128), F32),
        pltpu.VMEM((nxy, 2 * nq, 128), F32),
    ]
    state_shape = jax.ShapeDtypeStruct((lb, 128), F32)

    def exact(key):
        return pl.pallas_call(
            exact_kernel,
            out_shape=state_shape,
            in_specs=[hbm] * 6 + [VMEM],
            out_specs=VMEM,
            scratch_shapes=held[0:6] + held[7:] + [
                pltpu.VMEM((nxy, 72, 128), F32),
                pltpu.VMEM((nxy, 64, 128), F32),
                pltpu.VMEM((nxy * slots, 256), BF16),
                pltpu.VMEM((nxy * nq, 128), F32),
                pltpu.VMEM((nxy * nq, 128), F32),
                pltpu.VMEM((nq, nxy, 128), F32),
                pltpu.VMEM((nq, nxy, 128), F32),
                pltpu.VMEM((4, lb, 128), F32),
                pltpu.VMEM((4, lb, 128), F32),
                pltpu.VMEM((4, lb, 128), F32),
                pltpu.VMEM((2, lb, 128), F32),
                pltpu.VMEM((2, lb // 2, 128), F32),
            ] + returned + [
                dma((6,)),
                dma((2, 20)), dma((2, 20)), dma((nxy,)), dma((nxy,)), dma((nq,)), dma((nq,)),
                dma((4,)), dma((4,)), dma((4,)), dma((4,)),
                dma((nq,)), dma((nq,)), dma((nxy,)), dma((nxy,)),
            ],
            compiler_params=pltpu.CompilerParams(
                collective_id=1, has_side_effects=True, vmem_limit_bytes=60 * 2**20),
            name="exact",
        )(*operands[0:6], key)

    def targets(state):
        return pl.pallas_call(
            target_kernel,
            out_shape=jax.ShapeDtypeStruct((2, lb, target_phase.shape[1]), F32),
            in_specs=[VMEM] * 3,
            out_specs=VMEM,
            compiler_params=pltpu.CompilerParams(vmem_limit_bytes=32 * 2**20),
            name="target",
        )(state, target_phase, target_weight(side))

    state, flag, key = pl.pallas_call(
        slot_kernel,
        out_shape=(jax.ShapeDtypeStruct((lb // 2, 2, 128), F32), jax.ShapeDtypeStruct((1,), jnp.int32),
                   jax.ShapeDtypeStruct((1, slots), jnp.int32)),
        in_specs=[hbm] * 7 + [SMEM],
        out_specs=(VMEM, SMEM, VMEM),
        scratch_shapes=held + [
            pltpu.VMEM((nxy * nq, 128), F32),
            pltpu.VMEM((nq, M1, 128), F32),
            pltpu.VMEM((nq * M1, 128), F32),
            pltpu.VMEM((nq * 64, 256), BF16),
            pltpu.VMEM((nxy, M2, 128), F32),
            pltpu.VMEM((nxy * M2, 128), F32),
            pltpu.VMEM((lb, 128), F32),
            pltpu.VMEM((lb, 128), F32),
            pltpu.VMEM((nxy * nq, 2, 128), F32),
            pltpu.VMEM((nxy * nq, 2, 128), F32),
            dma((7,)),
            dma((nq,)), dma((nq,)), dma((nxy,)), dma((nxy,)), dma, dma,
        ],
        compiler_params=pltpu.CompilerParams(
            collective_id=0, has_side_effects=True, vmem_limit_bytes=60 * 2**20),
        name="slots",
    )(*operands)
    state = state.reshape(lb, 128)
    return lax.cond(flag[0] > 0, lambda: targets(exact(key)), lambda: targets(state))


def solution(mesh):
    placed = (
        P(("hi", "lo"), None, None),
        P(("hi", "lo"), None, None),
        P(("hi", "lo"), None),
        P(("hi", "lo")),
        P(("hi", "lo")),
        P(("hi", "lo"), None),
        P(("hi", "lo"), None),
    )
    return jax.shard_map(
        functools.partial(local, 16),
        mesh=mesh, in_specs=placed, out_specs=P(None, ("hi", "lo"), None), check_vma=False
    )
```

```python
import functools
import math

import jax
import jax.numpy as jnp
import ml_dtypes
import numpy as np
from jax import lax
from jax.experimental import pallas as pl
from jax.experimental.pallas import tpu as pltpu
from jax.sharding import PartitionSpec as P

MESH = pl.DeviceIdType.MESH
F32 = jnp.float32
BF16 = jnp.bfloat16
VMEM = pl.BlockSpec(memory_space=pltpu.VMEM)
SMEM = pl.BlockSpec(memory_space=pltpu.SMEM)


def np_nodes():
    return np.cos((2.0 * np.arange(8) + 1.0) * math.pi / 16.0)


def np_lagrange(points):
    nodes = np_nodes()
    columns = []
    for index in range(8):
        value = np.ones_like(points)
        for other in range(8):
            if other != index:
                value = value * (points - nodes[other]) / (nodes[index] - nodes[other])
        columns.append(value)
    return np.stack(columns, axis=0)


def split_np(array):
    high = array.astype(np.float32).astype(ml_dtypes.bfloat16)
    low = (array - high.astype(np.float64)).astype(np.float32).astype(ml_dtypes.bfloat16)
    return high, low


def level_weight(parity):
    blocks = []
    for child in range(2):
        inner = np_lagrange((np_nodes() + (2.0 * child - 1.0)) / 2.0).T
        middle = np.kron(inner, np.eye(8)) if parity == 0 else np.kron(np.eye(8), inner)
        blocks.append(np.kron(np.eye(2), middle))
    weight = 0.70710678 * np.concatenate(blocks, axis=0)
    return np.concatenate(split_np(weight), axis=1)


def target_weight(side):
    grid = (2.0 * np.arange(side) + 1.0) / side - 1.0
    basis = np_lagrange(grid)
    table = np.einsum("am,bn->abmn", basis, basis).reshape(64, side * side)
    high, low = split_np(np.kron(np.eye(2), table))
    return np.concatenate([high, high, low], axis=0)


def sincos(angle):
    half = 0.5 * angle
    sq = half * half
    s = -1.0 / 39916800.0
    for term in (1.0 / 362880.0, -1.0 / 5040.0, 1.0 / 120.0, -1.0 / 6.0, 1.0):
        s = s * sq + term
    s = s * half
    c = 1.0 / 479001600.0
    for term in (-1.0 / 3628800.0, 1.0 / 40320.0, -1.0 / 720.0, 1.0 / 24.0, -0.5, 1.0):
        c = c * sq + term
    return 2.0 * s * c, 1.0 - 2.0 * s * s


def lagrange_rows(points):
    nodes = [float(v) for v in np_nodes()]
    diff = [points - v for v in nodes]
    before = [None] * 8
    after = [None] * 8
    for index in range(1, 8):
        before[index] = diff[0] if index == 1 else before[index - 1] * diff[index - 1]
    for index in range(6, -1, -1):
        after[index] = diff[7] if index == 6 else after[index + 1] * diff[index + 1]
    rows = []
    for index in range(8):
        scale = 1.0
        for other in range(8):
            if other != index:
                scale = scale / (nodes[index] - nodes[other])
        if index == 0:
            value = after[0]
        elif index == 7:
            value = before[7]
        else:
            value = before[index] * after[index]
        rows.append(value * scale)
    return rows


def split(value):
    high = value.astype(BF16)
    low = (value - high.astype(F32)).astype(BF16)
    return high, low


def leaf(pos_ref, wgt_ref, phase_ref, gx, ly, ct):
    slots = phase_ref.shape[0]
    sinv, cosv = sincos(phase_ref[...])
    w_re = wgt_ref[pl.ds(0, slots, stride=2), :]
    w_im = wgt_ref[pl.ds(1, slots, stride=2), :]
    g_re = (0.5 * (w_re * cosv - w_im * sinv)).T
    g_im = (0.5 * (w_re * sinv + w_im * cosv)).T
    x = pos_ref[pl.ds(0, slots, stride=2), :].T
    y = pos_ref[pl.ds(1, slots, stride=2), :].T
    for index, value in enumerate(lagrange_rows(x)):
        gx[index] = value * g_re
        gx[8 + index] = value * g_im
    for index, value in enumerate(lagrange_rows(y)):
        ly[index] = value

    def row(index, carry):
        total = gx[index, 0:8, :][None] * ly[:, 0:8, :]
        for part in range(1, slots // 8):
            rows = slice(8 * part, 8 * part + 8)
            total = total + gx[index, rows, :][None] * ly[:, rows, :]
        ct[pl.ds(pl.multiple_of(index * 8, 8), 8), :] = jnp.sum(total, axis=1)
        return carry

    lax.fori_loop(0, 16, row, 0)
    return ct[...].T


def exact_kernel(pos_hbm, wgt_hbm, phase_hbm, rate_hbm, w0_hbm, w1_hbm, key_ref, out_ref,
                     pos_ref, wgt_ref, phase_ref, rate_ref, w0_ref, w1_ref, gx, ly, ct,
                     gath_a, gath_b, cat, rate_s, rate_r, rate_s2, rate_r2,
                     sib_s, sib_r, own, zrecv, z2recv, ret_s, ret_r, fin_s, fin_r,
                     in_sem, g_send, g_recv, r_send, r_recv, r2_send, r2_recv,
                     b_send, b_recv, z_send, z_recv, t_send, t_recv, f_send, f_recv):
    nxy, nq = 16, 8
    ndev = nxy * nq
    lb = 2 * ndev
    lx = 4
    slots = 128
    hi = lax.axis_index("hi")
    lo = lax.axis_index("lo")
    xy = lax.div(lo, 2)
    zlo = lax.rem(lo, 2)
    q = hi * 2 + zlo
    core = lax.rem(hi, 2)
    z = lax.div(hi, 2) * 2 + zlo

    loads = [
        pltpu.make_async_copy(src, dst, in_sem.at[i])
        for i, (src, dst) in enumerate([
            (phase_hbm, phase_ref), (wgt_hbm, wgt_ref), (pos_hbm, pos_ref),
            (rate_hbm, rate_ref), (w0_hbm, w0_ref), (w1_hbm, w1_ref)])
    ]
    for load in loads:
        load.start()

    def dev(q_at, xy_at):
        return lax.div(q_at, 2), xy_at * 2 + lax.rem(q_at, 2)

    def xy_peer(step):
        return lax.rem(xy + step, nxy)

    def q_peer(step):
        return lax.rem(q + step, nq)

    def q_of(z_at, core_at):
        return lax.div(z_at, 2) * 4 + core_at * 2 + lax.rem(z_at, 2)

    def rcopy(src, dst, send, recv, target):
        return pltpu.make_async_remote_copy(
            src_ref=src, dst_ref=dst, send_sem=send, recv_sem=recv,
            device_id=target, device_id_type=MESH)

    barrier = pltpu.get_barrier_semaphore()

    def greet_xy(step, carry):
        pl.semaphore_signal(barrier, inc=1, device_id=dev(q, xy_peer(step)), device_id_type=MESH)
        return carry

    def greet_q(step, carry):
        pl.semaphore_signal(barrier, inc=1, device_id=dev(q_peer(step), xy), device_id_type=MESH)
        return carry

    lax.fori_loop(1, nxy, greet_xy, 0)
    lax.fori_loop(1, nq, greet_q, 0)

    x_at = lax.rem(xy, 4)
    y_at = lax.div(xy, 4)
    for load in loads[0:3]:
        load.wait()
    coeff = leaf(pos_ref, wgt_ref, phase_ref, gx, ly, ct)
    key = key_ref[...].astype(F32)
    gath_a[y_at * 4 + x_at, 0:64, :] = coeff[64:128]
    gath_a[y_at * 4 + x_at, 64:72, :] = jnp.broadcast_to(key, (8, slots))
    gath_b[x_at * 4 + y_at] = coeff[0:64]
    loads[3].wait()
    rate_s[...] = jnp.concatenate([rate_ref[:, 0:ndev], rate_ref[:, ndev:lb]], axis=0).T
    pl.semaphore_wait(barrier, nxy - 1 + nq - 1)

    xs = {0: x_at, -1: lax.rem(x_at + 3, 4), 1: lax.rem(x_at + 1, 4), 2: lax.rem(x_at + 2, 4)}
    ys = {0: y_at, -1: lax.rem(y_at + 3, 4), 1: lax.rem(y_at + 1, 4), 2: lax.rem(y_at + 2, 4)}
    order = (0, -1, 1, 2)
    sent = []

    def block(part, first, second, rows=None):
        ref = gath_a if part == 0 else gath_b
        at = ys[second] * 4 + xs[first] if part == 0 else xs[second] * 4 + ys[first]
        return ref.at[at] if rows is None else ref.at[at, rows]

    def halves(part):
        return (slice(0, 40), slice(40, 72)) if part == 0 else (slice(0, 32), slice(32, 64))

    def ring_copy(part, axis, sem, first, second, way, rows=None):
        along_x = (part == 0) == (axis == 0)
        to = ys[0] * 4 + xs[way] if along_x else ys[way] * 4 + xs[0]
        ref = block(part, first, second, rows)
        return rcopy(ref, ref, g_send.at[part, sem], g_recv.at[part, sem], dev(q, to))

    def start(copy):
        copy.start()
        sent.append(copy)

    for part in range(2):
        start(ring_copy(part, 0, 0, 0, 0, 1))
        start(ring_copy(part, 0, 1, 0, 0, -1))
    for part in range(2):
        start(ring_copy(part, 1, 4, 0, 0, 1))
        start(ring_copy(part, 1, 5, 0, 0, -1))

    def rate_copy(step):
        to = xy_peer(step)
        rows_to = pl.ds(pl.multiple_of(to * nq, nq), nq)
        rows_me = pl.ds(pl.multiple_of(xy * nq, nq), nq)
        return rcopy(rate_s.at[rows_to], rate_r.at[rows_me], r_send.at[step], r_recv.at[step], dev(q, to))

    def send_rate(step, carry):
        rate_copy(step).start()
        return carry

    lax.fori_loop(1, nxy, send_rate, 0)
    rows_me = pl.ds(pl.multiple_of(xy * nq, nq), nq)
    rate_r[rows_me, :] = rate_s[rows_me, :]

    for part in range(2):
        low, high = halves(part)
        ring_copy(part, 0, 0, -1, 0, 1).wait_recv()
        start(ring_copy(part, 0, 2, -1, 0, 1, low))
        ring_copy(part, 0, 1, 1, 0, -1).wait_recv()
        start(ring_copy(part, 0, 3, 1, 0, -1, high))
    for part in range(2):
        for r in (1, 2):
            start(ring_copy(part, 1, 4 + 4 * r, order[r], 0, 1))
            start(ring_copy(part, 1, 5 + 4 * r, order[r], 0, -1))
    for part in range(2):
        low, high = halves(part)
        ring_copy(part, 0, 2, 2, 0, 1, low).wait_recv()
        ring_copy(part, 0, 3, 2, 0, -1, high).wait_recv()
        start(ring_copy(part, 1, 4 + 12, 2, 0, 1))
        start(ring_copy(part, 1, 5 + 12, 2, 0, -1))
    for r in range(4):
        for part in range(2):
            low, high = halves(part)
            ring_copy(part, 1, 4 + 4 * r, order[r], -1, 1).wait_recv()
            start(ring_copy(part, 1, 6 + 4 * r, order[r], -1, 1, low))
            ring_copy(part, 1, 5 + 4 * r, order[r], 1, -1).wait_recv()
            start(ring_copy(part, 1, 7 + 4 * r, order[r], 1, -1, high))

    def wait_rate(step, carry):
        rate_copy(step).wait()
        return carry

    lax.fori_loop(1, nxy, wait_rate, 0)
    for at in range(nq):
        rate_s2[at] = rate_r[pl.ds(at, nxy, stride=nq), :]

    def rate2_copy(step):
        to = q_peer(step)
        return rcopy(rate_s2.at[to], rate_r2.at[q], r2_send.at[step], r2_recv.at[step], dev(to, xy))

    def send_rate2(step, carry):
        rate2_copy(step).start()
        return carry

    lax.fori_loop(1, nq, send_rate2, 0)
    rate_r2[q] = rate_s2[q]

    for r in range(4):
        for part in range(2):
            low, high = halves(part)
            ring_copy(part, 1, 6 + 4 * r, order[r], 2, 1, low).wait_recv()
            ring_copy(part, 1, 7 + 4 * r, order[r], 2, -1, high).wait_recv()

    def split_rows(index, carry):
        rows_a = pl.ds(pl.multiple_of(index * slots + 64, 64), 64)
        rows_b = pl.ds(pl.multiple_of(index * slots, 64), 64)
        high, low = split(gath_a[index, 0:64, :])
        cat[rows_a, 0:128] = high
        cat[rows_a, 128:256] = low
        high, low = split(gath_b[lax.rem(index, 4) * 4 + lax.div(index, 4)])
        cat[rows_b, 0:128] = high
        cat[rows_b, 128:256] = low
        return carry

    lax.fori_loop(0, nxy, split_rows, 0)

    n = gath_a[:, 64, :].astype(jnp.int32)
    lbits = lb.bit_length() - 1
    dbits = ndev.bit_length() - 1
    j = n & (lb - 1)
    owner = n >> lbits
    holder = j & (ndev - 1)
    q_d = ((owner >> (lx + 1)) << 1) | (owner & 1)
    xy_d = (owner >> 1) & (nxy - 1)
    local_row = ((j >> dbits) << dbits) + q_d * nxy + xy_d
    code = (holder & (nq - 1)) * lb + local_row
    code = jnp.where((n >= 0) & ((holder >> 3) == xy), code, -1)
    row_id = lax.broadcasted_iota(jnp.int32, (lb, slots), 0)

    def chunk(q_at):
        rel = code - q_at * lb
        hot = [jnp.where(rel[i:i + 1, :] == row_id, 1.0, 0.0).astype(BF16) for i in range(nxy)]
        both = jnp.dot(jnp.concatenate(hot, axis=1), cat[...], preferred_element_type=F32)
        return both[:, 0:128] + both[:, 128:256]

    def sib_copy(off):
        return rcopy(sib_s.at[off], sib_r.at[off], b_send.at[off], b_recv.at[off],
                     dev(q_of(z, 1 - core), xy))

    def z_dev(off):
        return dev(q_of(lax.rem(z + off, 4), core), xy)

    up_half = rcopy(own.at[2, 0:ndev], z2recv.at[0], z_send.at[0], z_recv.at[0], z_dev(1))
    down_half = rcopy(own.at[2, ndev:lb], z2recv.at[1], z_send.at[1], z_recv.at[1], z_dev(3))
    up_full = rcopy(own.at[1], zrecv.at[0], z_send.at[2], z_recv.at[2], z_dev(1))
    down_full = rcopy(own.at[3], zrecv.at[1], z_send.at[3], z_recv.at[3], z_dev(3))

    def fold(off):
        sib_copy(off).wait()
        own[off] = own[off] + sib_r[off]

    def scatter(step, carry):
        off = lax.rem(step + 2, 4)
        to = lax.rem(z + off, 4)
        sib_s[off] = chunk(q_of(to, 1 - core))
        sib_copy(off).start()

        @pl.when(step == 1)
        def _():
            fold(2)
            up_half.start()
            down_half.start()

        @pl.when(step == 3)
        def _():
            fold(3)
            down_half.wait_recv()
            own[3, ndev:lb] = own[3, ndev:lb] + z2recv[1]
            down_full.start()

        own[off] = chunk(q_of(to, core))
        return carry

    lax.fori_loop(0, 4, scatter, 0)
    fold(1)
    up_half.wait_recv()
    own[1, 0:ndev] = own[1, 0:ndev] + z2recv[0]
    up_full.start()
    fold(0)

    def wait_rate2(step, carry):
        rate2_copy(step).wait()
        return carry

    lax.fori_loop(1, nq, wait_rate2, 0)
    sin_p, cos_p = sincos(rate_r2[...].reshape(ndev, 128))
    left = lax.broadcasted_iota(jnp.int32, (ndev, 128), 1) < 64
    cos_o = pltpu.roll(cos_p, 64, 1)
    sin_o = pltpu.roll(sin_p, 64, 1)
    cos1 = jnp.concatenate([jnp.where(left, cos_p, cos_o), jnp.where(left, cos_o, cos_p)], axis=0)
    sin1 = jnp.concatenate([jnp.where(left, -sin_p, sin_o), jnp.where(left, -sin_o, sin_p)], axis=0)
    for load in loads[4:6]:
        load.wait()

    down_full.wait_recv()
    up_full.wait_recv()
    state = own[0] + (zrecv[0] + zrecv[1])

    cosv, sinv = cos1, sin1
    sub = lax.broadcasted_iota(jnp.int32, (lb // 8, 8, 128), 1)
    for step in range(dbits):
        if step > 0:
            cosv, sinv = cosv * cos1 - sinv * sin1, sinv * cos1 + cosv * sin1
        bit = lx if step == 0 else (step - 1 if step <= lx else step)
        if bit < 3:
            tiles = state.reshape(lb // 8, 8, 128)
            dist = 1 << bit
            upper = (sub & dist) != 0
            first = jnp.where(upper, pltpu.roll(tiles, dist, 1), tiles).reshape(lb, 128)
            second = jnp.where(upper, tiles, pltpu.roll(tiles, 8 - dist, 1)).reshape(lb, 128)
        else:
            pairs = state.reshape(lb >> (bit + 1), 2, 1 << bit, 128)
            first = jnp.concatenate([pairs[:, 0:1], pairs[:, 0:1]], axis=1).reshape(lb, 128)
            second = jnp.concatenate([pairs[:, 1:2], pairs[:, 1:2]], axis=1).reshape(lb, 128)
        first = cosv * first + sinv * pltpu.roll(first, 64, 1)
        second = cosv * second + sinv * pltpu.roll(second, 64, 1)
        high, low = split(jnp.concatenate([first, second], axis=1))
        w_ref = w0_ref if step % 2 == 0 else w1_ref
        main = jnp.dot(high, w_ref[...], preferred_element_type=F32)
        rest = jnp.dot(low, w_ref[:, 0:128], preferred_element_type=F32)
        state = main[:, 0:128] + (main[:, 128:256] + rest)

    for at in range(nq):
        for jj in range(2):
            base = jj * ndev + at * nxy
            ret_s[at, jj * nxy:(jj + 1) * nxy] = state[base:base + nxy]

    def ret_copy(step):
        to = q_peer(step)
        rows = pl.ds(pl.multiple_of(q * 2 * nxy, 2 * nxy), 2 * nxy)
        return rcopy(ret_s.at[to], ret_r.at[rows], t_send.at[step], t_recv.at[step], dev(to, xy))

    def send_ret(step, carry):
        ret_copy(step).start()
        return carry

    def wait_ret(step, carry):
        ret_copy(step).wait()
        return carry

    lax.fori_loop(1, nq, send_ret, 0)
    ret_r[pl.ds(pl.multiple_of(q * 2 * nxy, 2 * nxy), 2 * nxy), :] = ret_s[q]
    lax.fori_loop(1, nq, wait_ret, 0)
    for at in range(nxy):
        fin_s[at] = ret_r[pl.ds(at, 2 * nq, stride=nxy), :]

    def fin_copy(step):
        to = xy_peer(step)
        return rcopy(fin_s.at[to], fin_r.at[xy], f_send.at[step], f_recv.at[step], dev(q, to))

    def send_fin(step, carry):
        fin_copy(step).start()
        return carry

    def wait_fin(step, carry):
        fin_copy(step).wait()
        return carry

    lax.fori_loop(1, nxy, send_fin, 0)
    fin_r[xy] = fin_s[xy]
    for copy in sent + [up_half, down_half, up_full, down_full]:
        copy.wait_send()
    lax.fori_loop(1, nxy, wait_fin, 0)
    out_ref[...] = fin_r[...].reshape(lb, 128)


S1, S2 = 40, 24


def far(step, size):
    return min(step, size - step)


XY_STEPS = sorted(range(1, 16), key=lambda s: -far(s // 4, 4) - far(s % 4, 4))
Q_STEPS = sorted(range(1, 8), key=lambda s: -far(s // 4 * 2 + s % 2, 4))
ALL_STEPS = sorted(range(1, 128), key=lambda s: -far(s // 64 * 2 + s % 2, 4) - far(s // 8 % 4, 4) - far(s // 2 % 4, 4))


def nt_dot(left, right):
    return lax.dot_general(left, right, (((1,), (1,)), ((), ())), preferred_element_type=F32)


def hot(cond):
    return jnp.where(cond, 1.0, 0.0)


def slot_kernel(pos_hbm, wgt_hbm, phase_hbm, rate_hbm, w0_hbm, w1_hbm, box_hbm, count_hbm, target_hbm,
                out_ref, flag_ref, key_ref, cos_out, sin_out,
                pos_ref, wgt_ref, phase_ref, rate_ref, w0_ref, w1_ref, box_ref, count_ref, target_ref, gx, ly, ct,
                rate_s, rate_r, rate_s2, rate_r2, msg1_s, msg1_r, cat2, msg2_s, msg2_r, cos_s, sin_s, ret_s, ret_r,
                in_sem, a_send, a_recv, c_send, c_recv, r_send, r_recv, r2_send, r2_recv, t_send, t_recv):
    nxy, nq = 16, 8
    ndev = nxy * nq
    lb = 2 * ndev
    slots = 128
    lbits = lb.bit_length() - 1
    dbits = ndev.bit_length() - 1
    hi = lax.axis_index("hi")
    lo = lax.axis_index("lo")
    xy = lax.div(lo, 2)
    q = hi * 2 + lax.rem(lo, 2)

    def dev(q_at, xy_at):
        return lax.div(q_at, 2), xy_at * 2 + lax.rem(q_at, 2)

    def xy_peer(step):
        return lax.rem(xy + step, nxy)

    def q_peer(step):
        return lax.rem(q + step, nq)

    def rcopy(src, dst, send, recv, target):
        return pltpu.make_async_remote_copy(
            src_ref=src, dst_ref=dst, send_sem=send, recv_sem=recv,
            device_id=target, device_id_type=MESH)

    barrier = pltpu.get_barrier_semaphore()
    for step in XY_STEPS:
        pl.semaphore_signal(barrier, inc=1, device_id=dev(q, xy_peer(step)), device_id_type=MESH)
    for step in Q_STEPS:
        pl.semaphore_signal(barrier, inc=1, device_id=dev(q_peer(step), xy), device_id_type=MESH)

    loads = [
        pltpu.make_async_copy(src, dst, in_sem.at[i])
        for i, (src, dst) in enumerate([
            (box_hbm, box_ref), (phase_hbm, phase_ref), (wgt_hbm, wgt_ref), (pos_hbm, pos_ref),
            (rate_hbm, rate_ref), (w0_hbm, w0_ref), (w1_hbm, w1_ref), (target_hbm, target_ref),
            (count_hbm, count_ref)])
    ]
    for load in loads[8:] + loads[:8]:
        load.start()

    loads[8].wait()
    loads[0].wait()
    lane = lax.broadcasted_iota(jnp.int32, (1, slots), 1)
    n = jnp.where(lane < count_ref[...], box_ref[...], -1)
    key_ref[...] = n
    j = n & (lb - 1)
    owner = n >> lbits
    holder = j & (ndev - 1)
    q_d = ((owner >> 5) << 1) | (owner & 1)
    xy_d = (owner >> 1) & (nxy - 1)
    row_at = ((j >> dbits) << dbits) + q_d * nxy + xy_d
    live = n >= 0
    q_to = jnp.where(live, holder & (nq - 1), -1)
    before = hot(lax.broadcasted_iota(jnp.int32, (slots, slots), 0) < lax.broadcasted_iota(jnp.int32, (slots, slots), 1))
    before = before.astype(BF16)
    row128 = lax.broadcasted_iota(jnp.int32, (128, 128), 0)

    to_q = hot(q_to == lax.broadcasted_iota(jnp.int32, (16, slots), 0))
    ahead = jnp.dot(to_q.astype(BF16), before, preferred_element_type=F32)
    rank = jnp.sum(to_q * ahead, axis=0, keepdims=True).astype(jnp.int32)
    slot = jnp.where(live & (rank < S1 - 1), q_to * S1 + rank, -1)
    names = jnp.concatenate([to_q * ((holder >> 3) + 1).astype(F32), to_q * row_at.astype(F32)], axis=0)
    named = nt_dot(names.astype(BF16), hot(rank == row128).astype(BF16))
    named = named[0:8] * 256.0 + named[16:24]
    place = hot(slot == lax.broadcasted_iota(jnp.int32, (nq * S1, slots), 0)).astype(BF16)

    for load in loads[1:5]:
        load.wait()
    rate_s[...] = jnp.concatenate([rate_ref[:, 0:ndev], rate_ref[:, ndev:lb]], axis=0).T
    zeros = jnp.zeros((16, 256), BF16)
    for at in range(nq):
        cat2[at * 64 + 48:at * 64 + 64, :] = zeros
    coeff = leaf(pos_ref, wgt_ref, phase_ref, gx, ly, ct)
    both = jnp.dot(place, jnp.concatenate(split(coeff), axis=1), preferred_element_type=F32)
    both = both[:, 0:128] + both[:, 128:256]
    for at in range(nq):
        msg1_s[at * S1:(at + 1) * S1] = both[at * S1:(at + 1) * S1]
        msg1_s[(at + 1) * S1 - 1:(at + 1) * S1] = named[at:at + 1]
    pl.semaphore_wait(barrier, nxy - 1 + nq - 1)

    def slot_rows(at, size):
        return pl.ds(pl.multiple_of(at * size, 8), size)

    def first_copy(step):
        to = q_peer(step)
        return rcopy(msg1_s.at[slot_rows(to, S1)], msg1_r.at[slot_rows(q, S1)], a_send, a_recv, dev(to, xy))

    def rate_copy(step):
        to = xy_peer(step)
        return rcopy(rate_s.at[slot_rows(to, nq)], rate_r.at[slot_rows(xy, nq)], r_send, r_recv, dev(q, to))

    def rate2_copy(step):
        to = q_peer(step)
        return rcopy(rate_s2.at[to], rate_r2.at[q], r2_send, r2_recv, dev(to, xy))

    first_all = rcopy(msg1_s.at[0:(nq - 1) * S1], msg1_r.at[0:(nq - 1) * S1], a_send, a_recv, dev(q_peer(1), xy))
    second_all = rcopy(msg2_s.at[0:(nxy - 1) * S2], msg2_r.at[0:(nxy - 1) * S2], c_send, c_recv, dev(q, xy_peer(1)))
    rate_all = rcopy(rate_s.at[0:(nxy - 1) * nq], rate_r.at[0:(nxy - 1) * nq], r_send, r_recv, dev(q, xy_peer(1)))
    rate2_all = rcopy(rate_s2.at[0:nq - 1], rate_r2.at[0:nq - 1], r2_send, r2_recv, dev(q_peer(1), xy))

    for step in Q_STEPS:
        first_copy(step).start()
    for step in XY_STEPS:
        rate_copy(step).start()
    rate_r[slot_rows(xy, nq), :] = rate_s[slot_rows(xy, nq), :]
    for load in loads[5:8]:
        load.wait()
    sin_t, cos_t = sincos(target_ref[...])
    cos_out[...] = cos_t
    sin_out[...] = sin_t
    msg1_r[slot_rows(q, S1), :] = msg1_s[slot_rows(q, S1), :]
    first_all.wait_recv()

    meta = msg1_r[pl.ds(S1 - 1, nq, stride=S1), :]
    lanes8 = lax.broadcasted_iota(jnp.int32, (nq, 128), 1)
    over = jnp.max(jnp.where(lanes8 >= S1 - 1, meta, 0.0), axis=(0, 1), keepdims=True)
    meta = jnp.where(lanes8 < S1 - 1, meta, 0.0)
    odd = (lax.broadcasted_iota(jnp.int32, (nq, 128), 0) & 1) == 1
    meta = jnp.where(odd, pltpu.roll(meta, 64, 1), meta)
    codes = [(meta[2 * g:2 * g + 1] + meta[2 * g + 1:2 * g + 2]).astype(jnp.int32) for g in range(4)]
    xy_to = [code >> 8 for code in codes]
    row_to = [((code & 255) + 1).astype(F32) for code in codes]
    id16 = lax.broadcasted_iota(jnp.int32, (nxy, 128), 0) + 1
    to_xy = [hot(value == id16) for value in xy_to]
    counted = jnp.dot(jnp.concatenate(to_xy, axis=0).astype(BF16),
                      jnp.concatenate([before, jnp.ones((128, 128), BF16)], axis=1), preferred_element_type=F32)
    ranks = []
    total = jnp.zeros((nxy, 128), F32)
    for g in range(4):
        part = counted[g * nxy:(g + 1) * nxy]
        ranks.append(jnp.sum(to_xy[g] * (part[:, 0:128] + total), axis=0, keepdims=True).astype(jnp.int32))
        total = total + part[:, 128:256]
    place_id = lax.broadcasted_iota(jnp.int32, (nxy * S2, 128), 0)
    place2 = []
    for g in range(4):
        slot = jnp.where((xy_to[g] > 0) & (ranks[g] < S2 - 1), (xy_to[g] - 1) * S2 + ranks[g], -1)
        place2.append(hot(slot == place_id).astype(BF16))
    for at in range(nq):
        rows = jnp.concatenate([msg1_r[at * S1:at * S1 + S1, :], jnp.zeros((48 - S1, 128), F32)], axis=0)
        high, low = split(rows)
        cat2[at * 64:at * 64 + 48, 0:128] = high
        cat2[at * 64:at * 64 + 48, 128:256] = low
    both = jnp.dot(jnp.concatenate(place2, axis=1), cat2[...], preferred_element_type=F32)
    both = both[:, 0:128] + both[:, 128:256]
    names = jnp.concatenate([to_xy[g] * row_to[g] for g in range(4)], axis=1)
    named = nt_dot(names.astype(BF16), jnp.concatenate([hot(ranks[g] == row128).astype(BF16) for g in range(4)], axis=1))
    lanes16 = lax.broadcasted_iota(jnp.int32, (nxy, 128), 1)
    named = named + jnp.where((lanes16 == 127) & (over > 0.0), 1.0, 0.0)
    for at in range(nxy):
        msg2_s[at * S2:(at + 1) * S2] = both[at * S2:(at + 1) * S2]
        msg2_s[(at + 1) * S2 - 1:(at + 1) * S2] = named[at:at + 1]

    def second_copy(step):
        to = xy_peer(step)
        return rcopy(msg2_s.at[slot_rows(to, S2)], msg2_r.at[slot_rows(xy, S2)], c_send, c_recv, dev(q, to))

    for step in XY_STEPS:
        second_copy(step).start()
    msg2_r[slot_rows(xy, S2), :] = msg2_s[slot_rows(xy, S2), :]
    rate_all.wait_recv()
    for at in range(nq):
        rate_s2[at] = rate_r[pl.ds(at, nxy, stride=nq), :]
    for step in Q_STEPS:
        rate2_copy(step).start()
    rate_r2[q] = rate_s2[q]
    rate2_all.wait_recv()
    rates = rate_r2[...].reshape(ndev, 128)
    sin_p, cos_p = sincos(rates)
    left = lax.broadcasted_iota(jnp.int32, (ndev, 128), 1) < 64
    cos_o = pltpu.roll(cos_p, 64, 1)
    sin_o = pltpu.roll(sin_p, 64, 1)
    cos_s[0] = jnp.where(left, cos_p, cos_o)
    cos_s[1] = jnp.where(left, cos_o, cos_p)
    sin_s[0] = jnp.where(left, -sin_p, sin_o)
    sin_s[1] = jnp.where(left, -sin_o, sin_p)
    second_all.wait_recv()

    meta = msg2_r[pl.ds(S2 - 1, nxy, stride=S2), :]
    over = jnp.max(jnp.where(lanes16 >= S2 - 1, meta, 0.0), axis=(0, 1), keepdims=True)
    mark = jnp.where(over > 0.0, jnp.nan, 0.0)
    meta = jnp.where(lanes16 < S2 - 1, meta, 0.0)
    sub4 = lax.broadcasted_iota(jnp.int32, (nxy, 128), 0) & 3
    for turn in range(1, 4):
        meta = jnp.where(sub4 == turn, pltpu.roll(meta, 32 * turn, 1), meta)
    row_id = lax.broadcasted_iota(jnp.int32, (lb, 128), 0)
    spread = []
    for at in range(nxy):
        spread += [msg2_r[at * S2:(at + 1) * S2, :], jnp.zeros((32 - S2, 128), F32)]
    spread = jnp.concatenate(spread, axis=0)
    put = []
    for g in range(4):
        code = jnp.sum(meta[4 * g:4 * g + 4], axis=0, keepdims=True).astype(jnp.int32) - 1
        put.append(hot(code == row_id).astype(BF16))
    both = jnp.dot(jnp.concatenate(put, axis=1), jnp.concatenate(split(spread), axis=1), preferred_element_type=F32)
    state = both[:, 0:128] + both[:, 128:256]

    sub = lax.broadcasted_iota(jnp.int32, (ndev // 8, 8, 128), 1)
    states = [state[0:ndev], state[ndev:lb]]
    cosv = [cos_s[0], cos_s[1]]
    sinv = [sin_s[0], sin_s[1]]
    for step in range(dbits):
        bit = 4 if step == 0 else (step - 1 if step <= 4 else step)
        w_ref = w0_ref if step % 2 == 0 else w1_ref
        for jj in range(2):
            state = states[jj]
            if step > 0:
                cosv[jj], sinv[jj] = (cosv[jj] * cos_s[jj] - sinv[jj] * sin_s[jj],
                                      sinv[jj] * cos_s[jj] + cosv[jj] * sin_s[jj])
            if bit < 3:
                tiles = state.reshape(ndev // 8, 8, 128)
                dist = 1 << bit
                upper = (sub & dist) != 0
                first = jnp.where(upper, pltpu.roll(tiles, dist, 1), tiles).reshape(ndev, 128)
                second = jnp.where(upper, tiles, pltpu.roll(tiles, 8 - dist, 1)).reshape(ndev, 128)
            else:
                pairs = state.reshape(ndev >> (bit + 1), 2, 1 << bit, 128)
                first = jnp.concatenate([pairs[:, 0:1], pairs[:, 0:1]], axis=1).reshape(ndev, 128)
                second = jnp.concatenate([pairs[:, 1:2], pairs[:, 1:2]], axis=1).reshape(ndev, 128)
            first = cosv[jj] * first + sinv[jj] * pltpu.roll(first, 64, 1)
            second = cosv[jj] * second + sinv[jj] * pltpu.roll(second, 64, 1)
            high, low = split(jnp.concatenate([first, second], axis=1))
            main = jnp.dot(high, w_ref[...], preferred_element_type=F32)
            rest = jnp.dot(low, w_ref[:, 0:128], preferred_element_type=F32)
            states[jj] = main[:, 0:128] + (main[:, 128:256] + rest)

    for jj in range(2):
        ret_s[pl.ds(jj, ndev, stride=2), :] = states[jj] + mark
    holder_at = xy * nq + q

    def ret_to(hi_step, lo_step):
        hi_to = lax.rem(hi + hi_step, 4)
        lo_to = lax.rem(lo + lo_step, 32)
        at = (hi_to * 2 + lax.rem(lo_to, 2)) * nxy + lax.div(lo_to, 2)
        return rcopy(ret_s.at[pl.ds(at * 2, 2)], ret_r.at[pl.ds(holder_at * 2, 2)], t_send, t_recv, (hi_to, lo_to))

    def send_eight(block, carry):
        for a in range(1, 4):
            for b in range(8):
                ret_to(a, block * 8 + b).start()
        return carry

    lax.fori_loop(0, 4, send_eight, 0)
    for step in range(1, 32):
        ret_to(0, step).start()
    ret_r[pl.ds(holder_at * 2, 2), :] = ret_s[pl.ds((q * nxy + xy) * 2, 2), :]
    every = rcopy(ret_s.at[0:lb - 2], ret_r.at[0:lb - 2], t_send, t_recv, dev(q_peer(1), xy))
    every.wait_recv()
    result = ret_r[...]
    out_ref[...] = result
    total = jnp.sum(result, axis=0, keepdims=True)
    flag_ref[0] = jnp.max(jnp.where(total != total, 1.0, 0.0)).astype(jnp.int32)
    for copy in (first_all, second_all, rate_all, rate2_all, every):
        copy.wait_send()


def target_kernel(state_ref, cos_ref, sin_ref, table_ref, out_ref):
    lb, points = cos_ref.shape
    half = lb // 2
    for jj in range(2):
        rows = slice(jj * half, jj * half + half)
        high, low = split(state_ref[pl.ds(jj, half, stride=2), :])
        stacked = jnp.concatenate([high, low, high], axis=1)
        value = jnp.dot(stacked, table_ref[...], preferred_element_type=F32)
        cosv, sinv = cos_ref[rows, :], sin_ref[rows, :]
        v_re = value[:, 0:points]
        v_im = value[:, points:2 * points]
        out_ref[0, rows, :] = v_re * cosv - v_im * sinv
        out_ref[1, rows, :] = v_re * sinv + v_im * cosv


def local(side, src_position, src_weight, src_phase, block_box, block_count, node_rate, target_phase):
    slots, points = src_phase.shape
    lb = node_rate.shape[0]
    nxy, nq = 16, 8
    dma = pltpu.SemaphoreType.DMA
    hbm = pl.BlockSpec(memory_space=pltpu.HBM)
    operands = (
        src_position.reshape(2 * slots, points), src_weight.reshape(2 * slots, points), src_phase, node_rate.T,
        level_weight(0), level_weight(1), block_box.reshape(1, slots), block_count.reshape(1, 1), target_phase)
    held = [
        pltpu.VMEM((2 * slots, points), F32),
        pltpu.VMEM((2 * slots, points), F32),
        pltpu.VMEM((slots, points), F32),
        pltpu.VMEM((64, lb), F32),
        pltpu.VMEM((256, 256), BF16),
        pltpu.VMEM((256, 256), BF16),
        pltpu.VMEM((1, slots), jnp.int32),
        pltpu.VMEM((1, 1), jnp.int32),
        pltpu.VMEM(target_phase.shape, F32),
        pltpu.VMEM((16, points, slots), F32),
        pltpu.VMEM((8, points, slots), F32),
        pltpu.VMEM((128, slots), F32),
    ]
    returned = [
        pltpu.VMEM((nq, 2 * nxy, 128), F32),
        pltpu.VMEM((lb, 128), F32),
        pltpu.VMEM((nxy, 2 * nq, 128), F32),
        pltpu.VMEM((nxy, 2 * nq, 128), F32),
    ]
    state_shape = jax.ShapeDtypeStruct((lb, 128), F32)

    def exact(key):
        return pl.pallas_call(
            exact_kernel,
            out_shape=state_shape,
            in_specs=[hbm] * 6 + [VMEM],
            out_specs=VMEM,
            scratch_shapes=held[0:6] + held[9:] + [
                pltpu.VMEM((nxy, 72, 128), F32),
                pltpu.VMEM((nxy, 64, 128), F32),
                pltpu.VMEM((nxy * slots, 256), BF16),
                pltpu.VMEM((nxy * nq, 128), F32),
                pltpu.VMEM((nxy * nq, 128), F32),
                pltpu.VMEM((nq, nxy, 128), F32),
                pltpu.VMEM((nq, nxy, 128), F32),
                pltpu.VMEM((4, lb, 128), F32),
                pltpu.VMEM((4, lb, 128), F32),
                pltpu.VMEM((4, lb, 128), F32),
                pltpu.VMEM((2, lb, 128), F32),
                pltpu.VMEM((2, lb // 2, 128), F32),
            ] + returned + [
                dma((6,)),
                dma((2, 20)), dma((2, 20)), dma((nxy,)), dma((nxy,)), dma((nq,)), dma((nq,)),
                dma((4,)), dma((4,)), dma((4,)), dma((4,)),
                dma((nq,)), dma((nq,)), dma((nxy,)), dma((nxy,)),
            ],
            compiler_params=pltpu.CompilerParams(
                collective_id=1, has_side_effects=True, vmem_limit_bytes=60 * 2**20),
            name="exact",
        )(*operands[0:6], key)

    def targets(state):
        return pl.pallas_call(
            target_kernel,
            out_shape=jax.ShapeDtypeStruct((2, lb, target_phase.shape[1]), F32),
            in_specs=[VMEM] * 4,
            out_specs=VMEM,
            compiler_params=pltpu.CompilerParams(vmem_limit_bytes=32 * 2**20),
            name="target",
        )(state, cosv, sinv, target_weight(side))

    state, flag, key, cosv, sinv = pl.pallas_call(
        slot_kernel,
        out_shape=(state_shape, jax.ShapeDtypeStruct((1,), jnp.int32),
                   jax.ShapeDtypeStruct((1, slots), jnp.int32),
                   jax.ShapeDtypeStruct(target_phase.shape, F32), jax.ShapeDtypeStruct(target_phase.shape, F32)),
        in_specs=[hbm] * 9,
        out_specs=(VMEM, SMEM, VMEM, VMEM, VMEM),
        scratch_shapes=held + [
            pltpu.VMEM((nxy * nq, 128), F32),
            pltpu.VMEM((nxy * nq, 128), F32),
            pltpu.VMEM((nq, nxy, 128), F32),
            pltpu.VMEM((nq, nxy, 128), F32),
            pltpu.VMEM((nq * S1, 128), F32),
            pltpu.VMEM((nq * S1, 128), F32),
            pltpu.VMEM((nq * 64, 256), BF16),
            pltpu.VMEM((nxy * S2, 128), F32),
            pltpu.VMEM((nxy * S2, 128), F32),
            pltpu.VMEM((2, lb // 2, 128), F32),
            pltpu.VMEM((2, lb // 2, 128), F32),
            pltpu.VMEM((lb, 128), F32),
            pltpu.VMEM((lb, 128), F32),
            dma((9,)),
            dma, dma, dma, dma, dma, dma, dma, dma, dma, dma,
        ],
        compiler_params=pltpu.CompilerParams(
            collective_id=0, has_side_effects=True, vmem_limit_bytes=60 * 2**20),
        name="slots",
    )(*operands)
    return lax.switch(flag[0], (lambda: targets(state), lambda: targets(exact(key))))


def solution(mesh):
    placed = (
        P(("hi", "lo"), None, None),
        P(("hi", "lo"), None, None),
        P(("hi", "lo"), None),
        P(("hi", "lo")),
        P(("hi", "lo")),
        P(("hi", "lo"), None),
        P(("hi", "lo"), None),
    )
    return jax.shard_map(
        functools.partial(local, 16),
        mesh=mesh, in_specs=placed, out_specs=P(None, ("hi", "lo"), None), check_vma=False
    )
```

```python
import functools
import math

import jax
import jax.numpy as jnp
import ml_dtypes
import numpy as np
from jax import lax
from jax.experimental import pallas as pl
from jax.experimental.pallas import tpu as pltpu
from jax.sharding import PartitionSpec as P

MESH = pl.DeviceIdType.MESH
F32 = jnp.float32
BF16 = jnp.bfloat16
VMEM = pl.BlockSpec(memory_space=pltpu.VMEM)
SMEM = pl.BlockSpec(memory_space=pltpu.SMEM)


def np_nodes():
    return np.cos((2.0 * np.arange(8) + 1.0) * math.pi / 16.0)


def np_lagrange(points):
    nodes = np_nodes()
    columns = []
    for index in range(8):
        value = np.ones_like(points)
        for other in range(8):
            if other != index:
                value = value * (points - nodes[other]) / (nodes[index] - nodes[other])
        columns.append(value)
    return np.stack(columns, axis=0)


def split_np(array):
    high = array.astype(np.float32).astype(ml_dtypes.bfloat16)
    low = (array - high.astype(np.float64)).astype(np.float32).astype(ml_dtypes.bfloat16)
    return high, low


def level_weight(parity):
    blocks = []
    for child in range(2):
        inner = np_lagrange((np_nodes() + (2.0 * child - 1.0)) / 2.0).T
        middle = np.kron(inner, np.eye(8)) if parity == 0 else np.kron(np.eye(8), inner)
        blocks.append(np.kron(np.eye(2), middle))
    weight = 0.70710678 * np.concatenate(blocks, axis=0)
    return np.concatenate(split_np(weight), axis=1)


def target_weight(side):
    grid = (2.0 * np.arange(side) + 1.0) / side - 1.0
    basis = np_lagrange(grid)
    table = np.einsum("am,bn->abmn", basis, basis).reshape(64, side * side)
    high, low = split_np(np.kron(np.eye(2), table))
    return np.concatenate([high, high, low], axis=0)


def sincos(angle):
    half = 0.5 * angle
    sq = half * half
    s = -1.0 / 39916800.0
    for term in (1.0 / 362880.0, -1.0 / 5040.0, 1.0 / 120.0, -1.0 / 6.0, 1.0):
        s = s * sq + term
    s = s * half
    c = 1.0 / 479001600.0
    for term in (-1.0 / 3628800.0, 1.0 / 40320.0, -1.0 / 720.0, 1.0 / 24.0, -0.5, 1.0):
        c = c * sq + term
    return 2.0 * s * c, 1.0 - 2.0 * s * s


def lagrange_rows(points):
    nodes = [float(v) for v in np_nodes()]
    diff = [points - v for v in nodes]
    before = [None] * 8
    after = [None] * 8
    for index in range(1, 8):
        before[index] = diff[0] if index == 1 else before[index - 1] * diff[index - 1]
    for index in range(6, -1, -1):
        after[index] = diff[7] if index == 6 else after[index + 1] * diff[index + 1]
    rows = []
    for index in range(8):
        scale = 1.0
        for other in range(8):
            if other != index:
                scale = scale / (nodes[index] - nodes[other])
        if index == 0:
            value = after[0]
        elif index == 7:
            value = before[7]
        else:
            value = before[index] * after[index]
        rows.append(value * scale)
    return rows


def split(value):
    high = value.astype(BF16)
    low = (value - high.astype(F32)).astype(BF16)
    return high, low


def leaf(pos_ref, wgt_ref, phase_ref, gx, ly, ct):
    slots = phase_ref.shape[0]
    sinv, cosv = sincos(phase_ref[...])
    w_re = wgt_ref[pl.ds(0, slots, stride=2), :]
    w_im = wgt_ref[pl.ds(1, slots, stride=2), :]
    g_re = (0.5 * (w_re * cosv - w_im * sinv)).T
    g_im = (0.5 * (w_re * sinv + w_im * cosv)).T
    x = pos_ref[pl.ds(0, slots, stride=2), :].T
    y = pos_ref[pl.ds(1, slots, stride=2), :].T
    for index, value in enumerate(lagrange_rows(x)):
        gx[index] = value * g_re
        gx[8 + index] = value * g_im
    for index, value in enumerate(lagrange_rows(y)):
        ly[index] = value

    def row(index, carry):
        total = gx[index, 0:8, :][None] * ly[:, 0:8, :]
        for part in range(1, slots // 8):
            rows = slice(8 * part, 8 * part + 8)
            total = total + gx[index, rows, :][None] * ly[:, rows, :]
        ct[pl.ds(pl.multiple_of(index * 8, 8), 8), :] = jnp.sum(total, axis=1)
        return carry

    lax.fori_loop(0, 16, row, 0)
    return ct[...].T


def exact_kernel(pos_hbm, wgt_hbm, phase_hbm, rate_hbm, w0_hbm, w1_hbm, key_ref, out_ref,
                     pos_ref, wgt_ref, phase_ref, rate_ref, w0_ref, w1_ref, gx, ly, ct,
                     gath_a, gath_b, cat, rate_s, rate_r, rate_s2, rate_r2,
                     sib_s, sib_r, own, zrecv, z2recv, ret_s, ret_r, fin_s, fin_r,
                     in_sem, g_send, g_recv, r_send, r_recv, r2_send, r2_recv,
                     b_send, b_recv, z_send, z_recv, t_send, t_recv, f_send, f_recv):
    nxy, nq = 16, 8
    ndev = nxy * nq
    lb = 2 * ndev
    lx = 4
    slots = 128
    hi = lax.axis_index("hi")
    lo = lax.axis_index("lo")
    xy = lax.div(lo, 2)
    zlo = lax.rem(lo, 2)
    q = hi * 2 + zlo
    core = lax.rem(hi, 2)
    z = lax.div(hi, 2) * 2 + zlo

    loads = [
        pltpu.make_async_copy(src, dst, in_sem.at[i])
        for i, (src, dst) in enumerate([
            (phase_hbm, phase_ref), (wgt_hbm, wgt_ref), (pos_hbm, pos_ref),
            (rate_hbm, rate_ref), (w0_hbm, w0_ref), (w1_hbm, w1_ref)])
    ]
    for load in loads:
        load.start()

    def dev(q_at, xy_at):
        return lax.div(q_at, 2), xy_at * 2 + lax.rem(q_at, 2)

    def xy_peer(step):
        return lax.rem(xy + step, nxy)

    def q_peer(step):
        return lax.rem(q + step, nq)

    def q_of(z_at, core_at):
        return lax.div(z_at, 2) * 4 + core_at * 2 + lax.rem(z_at, 2)

    def rcopy(src, dst, send, recv, target):
        return pltpu.make_async_remote_copy(
            src_ref=src, dst_ref=dst, send_sem=send, recv_sem=recv,
            device_id=target, device_id_type=MESH)

    barrier = pltpu.get_barrier_semaphore()

    def greet_xy(step, carry):
        pl.semaphore_signal(barrier, inc=1, device_id=dev(q, xy_peer(step)), device_id_type=MESH)
        return carry

    def greet_q(step, carry):
        pl.semaphore_signal(barrier, inc=1, device_id=dev(q_peer(step), xy), device_id_type=MESH)
        return carry

    lax.fori_loop(1, nxy, greet_xy, 0)
    lax.fori_loop(1, nq, greet_q, 0)

    x_at = lax.rem(xy, 4)
    y_at = lax.div(xy, 4)
    for load in loads[0:3]:
        load.wait()
    coeff = leaf(pos_ref, wgt_ref, phase_ref, gx, ly, ct)
    key = key_ref[...].astype(F32)
    gath_a[y_at * 4 + x_at, 0:64, :] = coeff[64:128]
    gath_a[y_at * 4 + x_at, 64:72, :] = jnp.broadcast_to(key, (8, slots))
    gath_b[x_at * 4 + y_at] = coeff[0:64]
    loads[3].wait()
    rate_s[...] = jnp.concatenate([rate_ref[:, 0:ndev], rate_ref[:, ndev:lb]], axis=0).T
    pl.semaphore_wait(barrier, nxy - 1 + nq - 1)

    xs = {0: x_at, -1: lax.rem(x_at + 3, 4), 1: lax.rem(x_at + 1, 4), 2: lax.rem(x_at + 2, 4)}
    ys = {0: y_at, -1: lax.rem(y_at + 3, 4), 1: lax.rem(y_at + 1, 4), 2: lax.rem(y_at + 2, 4)}
    order = (0, -1, 1, 2)
    sent = []

    def block(part, first, second, rows=None):
        ref = gath_a if part == 0 else gath_b
        at = ys[second] * 4 + xs[first] if part == 0 else xs[second] * 4 + ys[first]
        return ref.at[at] if rows is None else ref.at[at, rows]

    def halves(part):
        return (slice(0, 40), slice(40, 72)) if part == 0 else (slice(0, 32), slice(32, 64))

    def ring_copy(part, axis, sem, first, second, way, rows=None):
        along_x = (part == 0) == (axis == 0)
        to = ys[0] * 4 + xs[way] if along_x else ys[way] * 4 + xs[0]
        ref = block(part, first, second, rows)
        return rcopy(ref, ref, g_send.at[part, sem], g_recv.at[part, sem], dev(q, to))

    def start(copy):
        copy.start()
        sent.append(copy)

    for part in range(2):
        start(ring_copy(part, 0, 0, 0, 0, 1))
        start(ring_copy(part, 0, 1, 0, 0, -1))
    for part in range(2):
        start(ring_copy(part, 1, 4, 0, 0, 1))
        start(ring_copy(part, 1, 5, 0, 0, -1))

    def rate_copy(step):
        to = xy_peer(step)
        rows_to = pl.ds(pl.multiple_of(to * nq, nq), nq)
        rows_me = pl.ds(pl.multiple_of(xy * nq, nq), nq)
        return rcopy(rate_s.at[rows_to], rate_r.at[rows_me], r_send.at[step], r_recv.at[step], dev(q, to))

    def send_rate(step, carry):
        rate_copy(step).start()
        return carry

    lax.fori_loop(1, nxy, send_rate, 0)
    rows_me = pl.ds(pl.multiple_of(xy * nq, nq), nq)
    rate_r[rows_me, :] = rate_s[rows_me, :]

    for part in range(2):
        low, high = halves(part)
        ring_copy(part, 0, 0, -1, 0, 1).wait_recv()
        start(ring_copy(part, 0, 2, -1, 0, 1, low))
        ring_copy(part, 0, 1, 1, 0, -1).wait_recv()
        start(ring_copy(part, 0, 3, 1, 0, -1, high))
    for part in range(2):
        for r in (1, 2):
            start(ring_copy(part, 1, 4 + 4 * r, order[r], 0, 1))
            start(ring_copy(part, 1, 5 + 4 * r, order[r], 0, -1))
    for part in range(2):
        low, high = halves(part)
        ring_copy(part, 0, 2, 2, 0, 1, low).wait_recv()
        ring_copy(part, 0, 3, 2, 0, -1, high).wait_recv()
        start(ring_copy(part, 1, 4 + 12, 2, 0, 1))
        start(ring_copy(part, 1, 5 + 12, 2, 0, -1))
    for r in range(4):
        for part in range(2):
            low, high = halves(part)
            ring_copy(part, 1, 4 + 4 * r, order[r], -1, 1).wait_recv()
            start(ring_copy(part, 1, 6 + 4 * r, order[r], -1, 1, low))
            ring_copy(part, 1, 5 + 4 * r, order[r], 1, -1).wait_recv()
            start(ring_copy(part, 1, 7 + 4 * r, order[r], 1, -1, high))

    def wait_rate(step, carry):
        rate_copy(step).wait()
        return carry

    lax.fori_loop(1, nxy, wait_rate, 0)
    for at in range(nq):
        rate_s2[at] = rate_r[pl.ds(at, nxy, stride=nq), :]

    def rate2_copy(step):
        to = q_peer(step)
        return rcopy(rate_s2.at[to], rate_r2.at[q], r2_send.at[step], r2_recv.at[step], dev(to, xy))

    def send_rate2(step, carry):
        rate2_copy(step).start()
        return carry

    lax.fori_loop(1, nq, send_rate2, 0)
    rate_r2[q] = rate_s2[q]

    for r in range(4):
        for part in range(2):
            low, high = halves(part)
            ring_copy(part, 1, 6 + 4 * r, order[r], 2, 1, low).wait_recv()
            ring_copy(part, 1, 7 + 4 * r, order[r], 2, -1, high).wait_recv()

    def split_rows(index, carry):
        rows_a = pl.ds(pl.multiple_of(index * slots + 64, 64), 64)
        rows_b = pl.ds(pl.multiple_of(index * slots, 64), 64)
        high, low = split(gath_a[index, 0:64, :])
        cat[rows_a, 0:128] = high
        cat[rows_a, 128:256] = low
        high, low = split(gath_b[lax.rem(index, 4) * 4 + lax.div(index, 4)])
        cat[rows_b, 0:128] = high
        cat[rows_b, 128:256] = low
        return carry

    lax.fori_loop(0, nxy, split_rows, 0)

    n = gath_a[:, 64, :].astype(jnp.int32)
    lbits = lb.bit_length() - 1
    dbits = ndev.bit_length() - 1
    j = n & (lb - 1)
    owner = n >> lbits
    holder = j & (ndev - 1)
    q_d = ((owner >> (lx + 1)) << 1) | (owner & 1)
    xy_d = (owner >> 1) & (nxy - 1)
    local_row = ((j >> dbits) << dbits) + q_d * nxy + xy_d
    code = (holder & (nq - 1)) * lb + local_row
    code = jnp.where((n >= 0) & ((holder >> 3) == xy), code, -1)
    row_id = lax.broadcasted_iota(jnp.int32, (lb, slots), 0)

    def chunk(q_at):
        rel = code - q_at * lb
        hot = [jnp.where(rel[i:i + 1, :] == row_id, 1.0, 0.0).astype(BF16) for i in range(nxy)]
        both = jnp.dot(jnp.concatenate(hot, axis=1), cat[...], preferred_element_type=F32)
        return both[:, 0:128] + both[:, 128:256]

    def sib_copy(off):
        return rcopy(sib_s.at[off], sib_r.at[off], b_send.at[off], b_recv.at[off],
                     dev(q_of(z, 1 - core), xy))

    def z_dev(off):
        return dev(q_of(lax.rem(z + off, 4), core), xy)

    up_half = rcopy(own.at[2, 0:ndev], z2recv.at[0], z_send.at[0], z_recv.at[0], z_dev(1))
    down_half = rcopy(own.at[2, ndev:lb], z2recv.at[1], z_send.at[1], z_recv.at[1], z_dev(3))
    up_full = rcopy(own.at[1], zrecv.at[0], z_send.at[2], z_recv.at[2], z_dev(1))
    down_full = rcopy(own.at[3], zrecv.at[1], z_send.at[3], z_recv.at[3], z_dev(3))

    def fold(off):
        sib_copy(off).wait()
        own[off] = own[off] + sib_r[off]

    def scatter(step, carry):
        off = lax.rem(step + 2, 4)
        to = lax.rem(z + off, 4)
        sib_s[off] = chunk(q_of(to, 1 - core))
        sib_copy(off).start()

        @pl.when(step == 1)
        def _():
            fold(2)
            up_half.start()
            down_half.start()

        @pl.when(step == 3)
        def _():
            fold(3)
            down_half.wait_recv()
            own[3, ndev:lb] = own[3, ndev:lb] + z2recv[1]
            down_full.start()

        own[off] = chunk(q_of(to, core))
        return carry

    lax.fori_loop(0, 4, scatter, 0)
    fold(1)
    up_half.wait_recv()
    own[1, 0:ndev] = own[1, 0:ndev] + z2recv[0]
    up_full.start()
    fold(0)

    def wait_rate2(step, carry):
        rate2_copy(step).wait()
        return carry

    lax.fori_loop(1, nq, wait_rate2, 0)
    sin_p, cos_p = sincos(rate_r2[...].reshape(ndev, 128))
    left = lax.broadcasted_iota(jnp.int32, (ndev, 128), 1) < 64
    cos_o = pltpu.roll(cos_p, 64, 1)
    sin_o = pltpu.roll(sin_p, 64, 1)
    cos1 = jnp.concatenate([jnp.where(left, cos_p, cos_o), jnp.where(left, cos_o, cos_p)], axis=0)
    sin1 = jnp.concatenate([jnp.where(left, -sin_p, sin_o), jnp.where(left, -sin_o, sin_p)], axis=0)
    for load in loads[4:6]:
        load.wait()

    down_full.wait_recv()
    up_full.wait_recv()
    state = own[0] + (zrecv[0] + zrecv[1])

    cosv, sinv = cos1, sin1
    sub = lax.broadcasted_iota(jnp.int32, (lb // 8, 8, 128), 1)
    for step in range(dbits):
        if step > 0:
            cosv, sinv = cosv * cos1 - sinv * sin1, sinv * cos1 + cosv * sin1
        bit = lx if step == 0 else (step - 1 if step <= lx else step)
        if bit < 3:
            tiles = state.reshape(lb // 8, 8, 128)
            dist = 1 << bit
            upper = (sub & dist) != 0
            first = jnp.where(upper, pltpu.roll(tiles, dist, 1), tiles).reshape(lb, 128)
            second = jnp.where(upper, tiles, pltpu.roll(tiles, 8 - dist, 1)).reshape(lb, 128)
        else:
            pairs = state.reshape(lb >> (bit + 1), 2, 1 << bit, 128)
            first = jnp.concatenate([pairs[:, 0:1], pairs[:, 0:1]], axis=1).reshape(lb, 128)
            second = jnp.concatenate([pairs[:, 1:2], pairs[:, 1:2]], axis=1).reshape(lb, 128)
        first = cosv * first + sinv * pltpu.roll(first, 64, 1)
        second = cosv * second + sinv * pltpu.roll(second, 64, 1)
        high, low = split(jnp.concatenate([first, second], axis=1))
        w_ref = w0_ref if step % 2 == 0 else w1_ref
        main = jnp.dot(high, w_ref[...], preferred_element_type=F32)
        rest = jnp.dot(low, w_ref[:, 0:128], preferred_element_type=F32)
        state = main[:, 0:128] + (main[:, 128:256] + rest)

    for at in range(nq):
        for jj in range(2):
            base = jj * ndev + at * nxy
            ret_s[at, jj * nxy:(jj + 1) * nxy] = state[base:base + nxy]

    def ret_copy(step):
        to = q_peer(step)
        rows = pl.ds(pl.multiple_of(q * 2 * nxy, 2 * nxy), 2 * nxy)
        return rcopy(ret_s.at[to], ret_r.at[rows], t_send.at[step], t_recv.at[step], dev(to, xy))

    def send_ret(step, carry):
        ret_copy(step).start()
        return carry

    def wait_ret(step, carry):
        ret_copy(step).wait()
        return carry

    lax.fori_loop(1, nq, send_ret, 0)
    ret_r[pl.ds(pl.multiple_of(q * 2 * nxy, 2 * nxy), 2 * nxy), :] = ret_s[q]
    lax.fori_loop(1, nq, wait_ret, 0)
    for at in range(nxy):
        fin_s[at] = ret_r[pl.ds(at, 2 * nq, stride=nxy), :]

    def fin_copy(step):
        to = xy_peer(step)
        return rcopy(fin_s.at[to], fin_r.at[xy], f_send.at[step], f_recv.at[step], dev(q, to))

    def send_fin(step, carry):
        fin_copy(step).start()
        return carry

    def wait_fin(step, carry):
        fin_copy(step).wait()
        return carry

    lax.fori_loop(1, nxy, send_fin, 0)
    fin_r[xy] = fin_s[xy]
    for copy in sent + [up_half, down_half, up_full, down_full]:
        copy.wait_send()
    lax.fori_loop(1, nxy, wait_fin, 0)
    out_ref[...] = fin_r[...].reshape(lb, 128)


S1, S2 = 40, 24


def far(step, size):
    return min(step, size - step)


XY_STEPS = sorted(range(1, 16), key=lambda s: -far(s // 4, 4) - far(s % 4, 4))
Q_STEPS = sorted(range(1, 8), key=lambda s: -far(s // 4 * 2 + s % 2, 4))
ALL_STEPS = sorted(range(1, 128), key=lambda s: -far(s // 64 * 2 + s % 2, 4) - far(s // 8 % 4, 4) - far(s // 2 % 4, 4))


def nt_dot(left, right):
    return lax.dot_general(left, right, (((1,), (1,)), ((), ())), preferred_element_type=F32)


def hot(cond):
    return jnp.where(cond, 1.0, 0.0)


def slot_kernel(pos_hbm, wgt_hbm, phase_hbm, rate_hbm, w0_hbm, w1_hbm, box_hbm, count_hbm, target_hbm,
                out_ref, flag_ref, key_ref, cos_out, sin_out,
                pos_ref, wgt_ref, phase_ref, rate_ref, w0_ref, w1_ref, box_ref, count_ref, target_ref, gx, ly, ct,
                rate_s, rate_r, rate_s2, rate_r2, msg1_s, msg1_r, cat2, msg2_s, msg2_r, cos_s, sin_s, ret_s, ret_r,
                in_sem, a_send, a_recv, c_send, c_recv, r_send, r_recv, r2_send, r2_recv, t_send, t_recv):
    nxy, nq = 16, 8
    ndev = nxy * nq
    lb = 2 * ndev
    slots = 128
    lbits = lb.bit_length() - 1
    dbits = ndev.bit_length() - 1
    hi = lax.axis_index("hi")
    lo = lax.axis_index("lo")
    xy = lax.div(lo, 2)
    q = hi * 2 + lax.rem(lo, 2)

    def dev(q_at, xy_at):
        return lax.div(q_at, 2), xy_at * 2 + lax.rem(q_at, 2)

    def xy_peer(step):
        return lax.rem(xy + step, nxy)

    def q_peer(step):
        return lax.rem(q + step, nq)

    def rcopy(src, dst, send, recv, target):
        return pltpu.make_async_remote_copy(
            src_ref=src, dst_ref=dst, send_sem=send, recv_sem=recv,
            device_id=target, device_id_type=MESH)

    barrier = pltpu.get_barrier_semaphore()
    for step in XY_STEPS:
        pl.semaphore_signal(barrier, inc=1, device_id=dev(q, xy_peer(step)), device_id_type=MESH)
    for step in Q_STEPS:
        pl.semaphore_signal(barrier, inc=1, device_id=dev(q_peer(step), xy), device_id_type=MESH)

    loads = [
        pltpu.make_async_copy(src, dst, in_sem.at[i])
        for i, (src, dst) in enumerate([
            (box_hbm, box_ref), (phase_hbm, phase_ref), (wgt_hbm, wgt_ref), (pos_hbm, pos_ref),
            (rate_hbm, rate_ref), (w0_hbm, w0_ref), (w1_hbm, w1_ref), (target_hbm, target_ref),
            (count_hbm, count_ref)])
    ]
    for load in loads[8:] + loads[:8]:
        load.start()

    loads[8].wait()
    loads[0].wait()
    lane = lax.broadcasted_iota(jnp.int32, (1, slots), 1)
    n = jnp.where(lane < count_ref[...], box_ref[...], -1)
    key_ref[...] = n
    j = n & (lb - 1)
    owner = n >> lbits
    holder = j & (ndev - 1)
    q_d = ((owner >> 5) << 1) | (owner & 1)
    xy_d = (owner >> 1) & (nxy - 1)
    row_at = ((j >> dbits) << dbits) + q_d * nxy + xy_d
    live = n >= 0
    q_to = jnp.where(live, holder & (nq - 1), -1)
    before = hot(lax.broadcasted_iota(jnp.int32, (slots, slots), 0) < lax.broadcasted_iota(jnp.int32, (slots, slots), 1))
    before = before.astype(BF16)
    row128 = lax.broadcasted_iota(jnp.int32, (128, 128), 0)

    to_q = hot(q_to == lax.broadcasted_iota(jnp.int32, (16, slots), 0))
    ahead = jnp.dot(to_q.astype(BF16), before, preferred_element_type=F32)
    rank = jnp.sum(to_q * ahead, axis=0, keepdims=True).astype(jnp.int32)
    slot = jnp.where(live & (rank < S1 - 1), q_to * S1 + rank, -1)
    names = jnp.concatenate([to_q * ((holder >> 3) + 1).astype(F32), to_q * row_at.astype(F32)], axis=0)
    named = nt_dot(names.astype(BF16), hot(rank == row128).astype(BF16))
    named = named[0:8] * 256.0 + named[16:24]
    place = hot(slot == lax.broadcasted_iota(jnp.int32, (nq * S1, slots), 0)).astype(BF16)

    for load in loads[1:5]:
        load.wait()
    rate_s[...] = jnp.concatenate([rate_ref[:, 0:ndev], rate_ref[:, ndev:lb]], axis=0).T
    zeros = jnp.zeros((16, 256), BF16)
    for at in range(nq):
        cat2[at * 64 + 48:at * 64 + 64, :] = zeros
    coeff = leaf(pos_ref, wgt_ref, phase_ref, gx, ly, ct)
    both = jnp.dot(place, jnp.concatenate(split(coeff), axis=1), preferred_element_type=F32)
    both = both[:, 0:128] + both[:, 128:256]
    for at in range(nq):
        msg1_s[at * S1:(at + 1) * S1] = both[at * S1:(at + 1) * S1]
        msg1_s[(at + 1) * S1 - 1:(at + 1) * S1] = named[at:at + 1]
    pl.semaphore_wait(barrier, nxy - 1 + nq - 1)

    def slot_rows(at, size):
        return pl.ds(pl.multiple_of(at * size, 8), size)

    def first_copy(step):
        to = q_peer(step)
        return rcopy(msg1_s.at[slot_rows(to, S1)], msg1_r.at[slot_rows(q, S1)], a_send, a_recv, dev(to, xy))

    def rate_copy(step):
        to = xy_peer(step)
        return rcopy(rate_s.at[slot_rows(to, nq)], rate_r.at[slot_rows(xy, nq)], r_send, r_recv, dev(q, to))

    def rate2_copy(step):
        to = q_peer(step)
        return rcopy(rate_s2.at[to], rate_r2.at[q], r2_send, r2_recv, dev(to, xy))

    first_all = rcopy(msg1_s.at[0:(nq - 1) * S1], msg1_r.at[0:(nq - 1) * S1], a_send, a_recv, dev(q_peer(1), xy))
    second_all = rcopy(msg2_s.at[0:(nxy - 1) * S2], msg2_r.at[0:(nxy - 1) * S2], c_send, c_recv, dev(q, xy_peer(1)))
    rate_all = rcopy(rate_s.at[0:(nxy - 1) * nq], rate_r.at[0:(nxy - 1) * nq], r_send, r_recv, dev(q, xy_peer(1)))
    rate2_all = rcopy(rate_s2.at[0:nq - 1], rate_r2.at[0:nq - 1], r2_send, r2_recv, dev(q_peer(1), xy))

    for step in Q_STEPS:
        first_copy(step).start()
    for step in XY_STEPS:
        rate_copy(step).start()
    rate_r[slot_rows(xy, nq), :] = rate_s[slot_rows(xy, nq), :]
    for load in loads[5:8]:
        load.wait()
    sin_t, cos_t = sincos(target_ref[...])
    cos_out[...] = cos_t
    sin_out[...] = sin_t
    msg1_r[slot_rows(q, S1), :] = msg1_s[slot_rows(q, S1), :]
    first_all.wait_recv()

    meta = msg1_r[pl.ds(S1 - 1, nq, stride=S1), :]
    lanes8 = lax.broadcasted_iota(jnp.int32, (nq, 128), 1)
    over = jnp.max(jnp.where(lanes8 >= S1 - 1, meta, 0.0), axis=(0, 1), keepdims=True)
    meta = jnp.where(lanes8 < S1 - 1, meta, 0.0)
    odd = (lax.broadcasted_iota(jnp.int32, (nq, 128), 0) & 1) == 1
    meta = jnp.where(odd, pltpu.roll(meta, 64, 1), meta)
    codes = [(meta[2 * g:2 * g + 1] + meta[2 * g + 1:2 * g + 2]).astype(jnp.int32) for g in range(4)]
    xy_to = [code >> 8 for code in codes]
    row_to = [((code & 255) + 1).astype(F32) for code in codes]
    id16 = lax.broadcasted_iota(jnp.int32, (nxy, 128), 0) + 1
    to_xy = [hot(value == id16) for value in xy_to]
    counted = jnp.dot(jnp.concatenate(to_xy, axis=0).astype(BF16),
                      jnp.concatenate([before, jnp.ones((128, 128), BF16)], axis=1), preferred_element_type=F32)
    ranks = []
    total = jnp.zeros((nxy, 128), F32)
    for g in range(4):
        part = counted[g * nxy:(g + 1) * nxy]
        ranks.append(jnp.sum(to_xy[g] * (part[:, 0:128] + total), axis=0, keepdims=True).astype(jnp.int32))
        total = total + part[:, 128:256]
    place_id = lax.broadcasted_iota(jnp.int32, (nxy * S2, 128), 0)
    place2 = []
    for g in range(4):
        slot = jnp.where((xy_to[g] > 0) & (ranks[g] < S2 - 1), (xy_to[g] - 1) * S2 + ranks[g], -1)
        place2.append(hot(slot == place_id).astype(BF16))
    for at in range(nq):
        rows = jnp.concatenate([msg1_r[at * S1:at * S1 + S1, :], jnp.zeros((48 - S1, 128), F32)], axis=0)
        high, low = split(rows)
        cat2[at * 64:at * 64 + 48, 0:128] = high
        cat2[at * 64:at * 64 + 48, 128:256] = low
    both = jnp.dot(jnp.concatenate(place2, axis=1), cat2[...], preferred_element_type=F32)
    both = both[:, 0:128] + both[:, 128:256]
    names = jnp.concatenate([to_xy[g] * row_to[g] for g in range(4)], axis=1)
    named = nt_dot(names.astype(BF16), jnp.concatenate([hot(ranks[g] == row128).astype(BF16) for g in range(4)], axis=1))
    lanes16 = lax.broadcasted_iota(jnp.int32, (nxy, 128), 1)
    named = named + jnp.where((lanes16 == 127) & (over > 0.0), 1.0, 0.0)
    for at in range(nxy):
        msg2_s[at * S2:(at + 1) * S2] = both[at * S2:(at + 1) * S2]
        msg2_s[(at + 1) * S2 - 1:(at + 1) * S2] = named[at:at + 1]

    def second_copy(step):
        to = xy_peer(step)
        return rcopy(msg2_s.at[slot_rows(to, S2)], msg2_r.at[slot_rows(xy, S2)], c_send, c_recv, dev(q, to))

    for step in XY_STEPS:
        second_copy(step).start()
    msg2_r[slot_rows(xy, S2), :] = msg2_s[slot_rows(xy, S2), :]
    rate_all.wait_recv()
    for at in range(nq):
        rate_s2[at] = rate_r[pl.ds(at, nxy, stride=nq), :]
    for step in Q_STEPS:
        rate2_copy(step).start()
    rate_r2[q] = rate_s2[q]
    rate2_all.wait_recv()
    rates = rate_r2[...].reshape(ndev, 128)
    sin_p, cos_p = sincos(rates)
    left = lax.broadcasted_iota(jnp.int32, (ndev, 128), 1) < 64
    cos_o = pltpu.roll(cos_p, 64, 1)
    sin_o = pltpu.roll(sin_p, 64, 1)
    cos1 = [jnp.where(left, cos_p, cos_o), jnp.where(left, cos_o, cos_p)]
    sin1 = [jnp.where(left, -sin_p, sin_o), jnp.where(left, -sin_o, sin_p)]
    for jj in range(2):
        cosv, sinv = cos1[jj], sin1[jj]
        for step in range(dbits):
            if step > 0:
                cosv, sinv = cosv * cos1[jj] - sinv * sin1[jj], sinv * cos1[jj] + cosv * sin1[jj]
            cos_s[step, jj] = cosv
            sin_s[step, jj] = sinv
    second_all.wait_recv()

    meta = msg2_r[pl.ds(S2 - 1, nxy, stride=S2), :]
    over = jnp.max(jnp.where(lanes16 >= S2 - 1, meta, 0.0), axis=(0, 1), keepdims=True)
    mark = jnp.where(over > 0.0, jnp.nan, 0.0)
    meta = jnp.where(lanes16 < S2 - 1, meta, 0.0)
    sub4 = lax.broadcasted_iota(jnp.int32, (nxy, 128), 0) & 3
    for turn in range(1, 4):
        meta = jnp.where(sub4 == turn, pltpu.roll(meta, 32 * turn, 1), meta)
    row_id = lax.broadcasted_iota(jnp.int32, (lb, 128), 0)
    spread = []
    for at in range(nxy):
        spread += [msg2_r[at * S2:(at + 1) * S2, :], jnp.zeros((32 - S2, 128), F32)]
    spread = jnp.concatenate(spread, axis=0)
    put = []
    for g in range(4):
        code = jnp.sum(meta[4 * g:4 * g + 4], axis=0, keepdims=True).astype(jnp.int32) - 1
        put.append(hot(code == row_id).astype(BF16))
    both = jnp.dot(jnp.concatenate(put, axis=1), jnp.concatenate(split(spread), axis=1), preferred_element_type=F32)
    state = both[:, 0:128] + both[:, 128:256]

    sub = lax.broadcasted_iota(jnp.int32, (ndev // 8, 8, 128), 1)
    states = [state[0:ndev], state[ndev:lb]]
    for step in range(dbits):
        bit = 4 if step == 0 else (step - 1 if step <= 4 else step)
        w_ref = w0_ref if step % 2 == 0 else w1_ref
        for jj in range(2):
            state = states[jj]
            cosv, sinv = cos_s[step, jj], sin_s[step, jj]
            if bit < 3:
                tiles = state.reshape(ndev // 8, 8, 128)
                dist = 1 << bit
                upper = (sub & dist) != 0
                first = jnp.where(upper, pltpu.roll(tiles, dist, 1), tiles).reshape(ndev, 128)
                second = jnp.where(upper, tiles, pltpu.roll(tiles, 8 - dist, 1)).reshape(ndev, 128)
            else:
                pairs = state.reshape(ndev >> (bit + 1), 2, 1 << bit, 128)
                first = jnp.concatenate([pairs[:, 0:1], pairs[:, 0:1]], axis=1).reshape(ndev, 128)
                second = jnp.concatenate([pairs[:, 1:2], pairs[:, 1:2]], axis=1).reshape(ndev, 128)
            first = cosv * first + sinv * pltpu.roll(first, 64, 1)
            second = cosv * second + sinv * pltpu.roll(second, 64, 1)
            high, low = split(jnp.concatenate([first, second], axis=1))
            main = jnp.dot(high, w_ref[...], preferred_element_type=F32)
            rest = jnp.dot(low, w_ref[:, 0:128], preferred_element_type=F32)
            states[jj] = main[:, 0:128] + (main[:, 128:256] + rest)

    for jj in range(2):
        ret_s[pl.ds(jj, ndev, stride=2), :] = states[jj] + mark
    holder_at = xy * nq + q

    def ret_to(hi_step, lo_step):
        hi_to = lax.rem(hi + hi_step, 4)
        lo_to = lax.rem(lo + lo_step, 32)
        at = (hi_to * 2 + lax.rem(lo_to, 2)) * nxy + lax.div(lo_to, 2)
        return rcopy(ret_s.at[pl.ds(at * 2, 2)], ret_r.at[pl.ds(holder_at * 2, 2)], t_send, t_recv, (hi_to, lo_to))

    def send_eight(block, carry):
        for a in (2, 3, 1):
            for b in range(8):
                ret_to(a, block * 8 + b).start()
        return carry

    lax.fori_loop(0, 4, send_eight, 0)
    for step in range(1, 32):
        ret_to(0, step).start()
    ret_r[pl.ds(holder_at * 2, 2), :] = ret_s[pl.ds((q * nxy + xy) * 2, 2), :]
    every = rcopy(ret_s.at[0:lb - 2], ret_r.at[0:lb - 2], t_send, t_recv, dev(q_peer(1), xy))
    every.wait_recv()
    result = ret_r[...]
    out_ref[...] = result
    total = jnp.sum(result, axis=0, keepdims=True)
    flag_ref[0] = jnp.max(jnp.where(total != total, 1.0, 0.0)).astype(jnp.int32)
    for copy in (first_all, second_all, rate_all, rate2_all, every):
        copy.wait_send()


def target_kernel(state_ref, cos_ref, sin_ref, table_ref, out_ref):
    lb, points = cos_ref.shape
    half = lb // 2
    for jj in range(2):
        rows = slice(jj * half, jj * half + half)
        high, low = split(state_ref[pl.ds(jj, half, stride=2), :])
        stacked = jnp.concatenate([high, low, high], axis=1)
        value = jnp.dot(stacked, table_ref[...], preferred_element_type=F32)
        cosv, sinv = cos_ref[rows, :], sin_ref[rows, :]
        v_re = value[:, 0:points]
        v_im = value[:, points:2 * points]
        out_ref[0, rows, :] = v_re * cosv - v_im * sinv
        out_ref[1, rows, :] = v_re * sinv + v_im * cosv


def local(side, src_position, src_weight, src_phase, block_box, block_count, node_rate, target_phase):
    slots, points = src_phase.shape
    lb = node_rate.shape[0]
    nxy, nq = 16, 8
    dma = pltpu.SemaphoreType.DMA
    hbm = pl.BlockSpec(memory_space=pltpu.HBM)
    operands = (
        src_position.reshape(2 * slots, points), src_weight.reshape(2 * slots, points), src_phase, node_rate.T,
        level_weight(0), level_weight(1), block_box.reshape(1, slots), block_count.reshape(1, 1), target_phase)
    held = [
        pltpu.VMEM((2 * slots, points), F32),
        pltpu.VMEM((2 * slots, points), F32),
        pltpu.VMEM((slots, points), F32),
        pltpu.VMEM((64, lb), F32),
        pltpu.VMEM((256, 256), BF16),
        pltpu.VMEM((256, 256), BF16),
        pltpu.VMEM((1, slots), jnp.int32),
        pltpu.VMEM((1, 1), jnp.int32),
        pltpu.VMEM(target_phase.shape, F32),
        pltpu.VMEM((16, points, slots), F32),
        pltpu.VMEM((8, points, slots), F32),
        pltpu.VMEM((128, slots), F32),
    ]
    returned = [
        pltpu.VMEM((nq, 2 * nxy, 128), F32),
        pltpu.VMEM((lb, 128), F32),
        pltpu.VMEM((nxy, 2 * nq, 128), F32),
        pltpu.VMEM((nxy, 2 * nq, 128), F32),
    ]
    state_shape = jax.ShapeDtypeStruct((lb, 128), F32)

    def exact(key):
        return pl.pallas_call(
            exact_kernel,
            out_shape=state_shape,
            in_specs=[hbm] * 6 + [VMEM],
            out_specs=VMEM,
            scratch_shapes=held[0:6] + held[9:] + [
                pltpu.VMEM((nxy, 72, 128), F32),
                pltpu.VMEM((nxy, 64, 128), F32),
                pltpu.VMEM((nxy * slots, 256), BF16),
                pltpu.VMEM((nxy * nq, 128), F32),
                pltpu.VMEM((nxy * nq, 128), F32),
                pltpu.VMEM((nq, nxy, 128), F32),
                pltpu.VMEM((nq, nxy, 128), F32),
                pltpu.VMEM((4, lb, 128), F32),
                pltpu.VMEM((4, lb, 128), F32),
                pltpu.VMEM((4, lb, 128), F32),
                pltpu.VMEM((2, lb, 128), F32),
                pltpu.VMEM((2, lb // 2, 128), F32),
            ] + returned + [
                dma((6,)),
                dma((2, 20)), dma((2, 20)), dma((nxy,)), dma((nxy,)), dma((nq,)), dma((nq,)),
                dma((4,)), dma((4,)), dma((4,)), dma((4,)),
                dma((nq,)), dma((nq,)), dma((nxy,)), dma((nxy,)),
            ],
            compiler_params=pltpu.CompilerParams(
                collective_id=1, has_side_effects=True, vmem_limit_bytes=60 * 2**20),
            name="exact",
        )(*operands[0:6], key)

    def targets(state):
        return pl.pallas_call(
            target_kernel,
            out_shape=jax.ShapeDtypeStruct((2, lb, target_phase.shape[1]), F32),
            in_specs=[VMEM] * 4,
            out_specs=VMEM,
            compiler_params=pltpu.CompilerParams(vmem_limit_bytes=32 * 2**20),
            name="target",
        )(state, cosv, sinv, target_weight(side))

    state, flag, key, cosv, sinv = pl.pallas_call(
        slot_kernel,
        out_shape=(state_shape, jax.ShapeDtypeStruct((1,), jnp.int32),
                   jax.ShapeDtypeStruct((1, slots), jnp.int32),
                   jax.ShapeDtypeStruct(target_phase.shape, F32), jax.ShapeDtypeStruct(target_phase.shape, F32)),
        in_specs=[hbm] * 9,
        out_specs=(VMEM, SMEM, VMEM, VMEM, VMEM),
        scratch_shapes=held + [
            pltpu.VMEM((nxy * nq, 128), F32),
            pltpu.VMEM((nxy * nq, 128), F32),
            pltpu.VMEM((nq, nxy, 128), F32),
            pltpu.VMEM((nq, nxy, 128), F32),
            pltpu.VMEM((nq * S1, 128), F32),
            pltpu.VMEM((nq * S1, 128), F32),
            pltpu.VMEM((nq * 64, 256), BF16),
            pltpu.VMEM((nxy * S2, 128), F32),
            pltpu.VMEM((nxy * S2, 128), F32),
            pltpu.VMEM((7, 2, lb // 2, 128), F32),
            pltpu.VMEM((7, 2, lb // 2, 128), F32),
            pltpu.VMEM((lb, 128), F32),
            pltpu.VMEM((lb, 128), F32),
            dma((9,)),
            dma, dma, dma, dma, dma, dma, dma, dma, dma, dma,
        ],
        compiler_params=pltpu.CompilerParams(
            collective_id=0, has_side_effects=True, vmem_limit_bytes=60 * 2**20),
        name="slots",
    )(*operands)
    return lax.switch(flag[0], (lambda: targets(state), lambda: targets(exact(key))))


def solution(mesh):
    placed = (
        P(("hi", "lo"), None, None),
        P(("hi", "lo"), None, None),
        P(("hi", "lo"), None),
        P(("hi", "lo")),
        P(("hi", "lo")),
        P(("hi", "lo"), None),
        P(("hi", "lo"), None),
    )
    return jax.shard_map(
        functools.partial(local, 16),
        mesh=mesh, in_specs=placed, out_specs=P(None, ("hi", "lo"), None), check_vma=False
    )
```

```python
import functools
import math

import jax
import jax.numpy as jnp
import ml_dtypes
import numpy as np
from jax import lax
from jax.experimental import pallas as pl
from jax.experimental.pallas import tpu as pltpu
from jax.sharding import PartitionSpec as P

MESH = pl.DeviceIdType.MESH
F32 = jnp.float32
BF16 = jnp.bfloat16
VMEM = pl.BlockSpec(memory_space=pltpu.VMEM)
SMEM = pl.BlockSpec(memory_space=pltpu.SMEM)


def np_nodes():
    return np.cos((2.0 * np.arange(8) + 1.0) * math.pi / 16.0)


def np_lagrange(points):
    nodes = np_nodes()
    columns = []
    for index in range(8):
        value = np.ones_like(points)
        for other in range(8):
            if other != index:
                value = value * (points - nodes[other]) / (nodes[index] - nodes[other])
        columns.append(value)
    return np.stack(columns, axis=0)


def split_np(array):
    high = array.astype(np.float32).astype(ml_dtypes.bfloat16)
    low = (array - high.astype(np.float64)).astype(np.float32).astype(ml_dtypes.bfloat16)
    return high, low


def level_weight(parity):
    blocks = []
    for child in range(2):
        inner = np_lagrange((np_nodes() + (2.0 * child - 1.0)) / 2.0).T
        middle = np.kron(inner, np.eye(8)) if parity == 0 else np.kron(np.eye(8), inner)
        blocks.append(np.kron(np.eye(2), middle))
    weight = 0.70710678 * np.concatenate(blocks, axis=0)
    return np.concatenate(split_np(weight), axis=1)


def target_weight(side):
    grid = (2.0 * np.arange(side) + 1.0) / side - 1.0
    basis = np_lagrange(grid)
    table = np.einsum("am,bn->abmn", basis, basis).reshape(64, side * side)
    high, low = split_np(np.kron(np.eye(2), table))
    return np.concatenate([high, high, low], axis=0)


def sincos(angle):
    half = 0.5 * angle
    sq = half * half
    s = -1.0 / 39916800.0
    for term in (1.0 / 362880.0, -1.0 / 5040.0, 1.0 / 120.0, -1.0 / 6.0, 1.0):
        s = s * sq + term
    s = s * half
    c = 1.0 / 479001600.0
    for term in (-1.0 / 3628800.0, 1.0 / 40320.0, -1.0 / 720.0, 1.0 / 24.0, -0.5, 1.0):
        c = c * sq + term
    return 2.0 * s * c, 1.0 - 2.0 * s * s


def lagrange_rows(points):
    nodes = [float(v) for v in np_nodes()]
    diff = [points - v for v in nodes]
    before = [None] * 8
    after = [None] * 8
    for index in range(1, 8):
        before[index] = diff[0] if index == 1 else before[index - 1] * diff[index - 1]
    for index in range(6, -1, -1):
        after[index] = diff[7] if index == 6 else after[index + 1] * diff[index + 1]
    rows = []
    for index in range(8):
        scale = 1.0
        for other in range(8):
            if other != index:
                scale = scale / (nodes[index] - nodes[other])
        if index == 0:
            value = after[0]
        elif index == 7:
            value = before[7]
        else:
            value = before[index] * after[index]
        rows.append(value * scale)
    return rows


def split(value):
    high = value.astype(BF16)
    low = (value - high.astype(F32)).astype(BF16)
    return high, low


def leaf(pos_ref, wgt_ref, phase_ref, gx, ly, ct):
    slots = phase_ref.shape[0]
    sinv, cosv = sincos(phase_ref[...])
    w_re = wgt_ref[pl.ds(0, slots, stride=2), :]
    w_im = wgt_ref[pl.ds(1, slots, stride=2), :]
    g_re = (0.5 * (w_re * cosv - w_im * sinv)).T
    g_im = (0.5 * (w_re * sinv + w_im * cosv)).T
    x = pos_ref[pl.ds(0, slots, stride=2), :].T
    y = pos_ref[pl.ds(1, slots, stride=2), :].T
    for index, value in enumerate(lagrange_rows(x)):
        gx[index] = value * g_re
        gx[8 + index] = value * g_im
    for index, value in enumerate(lagrange_rows(y)):
        ly[index] = value

    def row(index, carry):
        total = gx[index, 0:8, :][None] * ly[:, 0:8, :]
        for part in range(1, slots // 8):
            rows = slice(8 * part, 8 * part + 8)
            total = total + gx[index, rows, :][None] * ly[:, rows, :]
        ct[pl.ds(pl.multiple_of(index * 8, 8), 8), :] = jnp.sum(total, axis=1)
        return carry

    lax.fori_loop(0, 16, row, 0)
    return ct[...].T


def exact_kernel(pos_hbm, wgt_hbm, phase_hbm, rate_hbm, w0_hbm, w1_hbm, key_ref, out_ref,
                     pos_ref, wgt_ref, phase_ref, rate_ref, w0_ref, w1_ref, gx, ly, ct,
                     gath_a, gath_b, cat, rate_s, rate_r, rate_s2, rate_r2,
                     sib_s, sib_r, own, zrecv, z2recv, ret_s, ret_r, fin_s, fin_r,
                     in_sem, g_send, g_recv, r_send, r_recv, r2_send, r2_recv,
                     b_send, b_recv, z_send, z_recv, t_send, t_recv, f_send, f_recv):
    nxy, nq = 16, 8
    ndev = nxy * nq
    lb = 2 * ndev
    lx = 4
    slots = 128
    hi = lax.axis_index("hi")
    lo = lax.axis_index("lo")
    xy = lax.div(lo, 2)
    zlo = lax.rem(lo, 2)
    q = hi * 2 + zlo
    core = lax.rem(hi, 2)
    z = lax.div(hi, 2) * 2 + zlo

    loads = [
        pltpu.make_async_copy(src, dst, in_sem.at[i])
        for i, (src, dst) in enumerate([
            (phase_hbm, phase_ref), (wgt_hbm, wgt_ref), (pos_hbm, pos_ref),
            (rate_hbm, rate_ref), (w0_hbm, w0_ref), (w1_hbm, w1_ref)])
    ]
    for load in loads:
        load.start()

    def dev(q_at, xy_at):
        return lax.div(q_at, 2), xy_at * 2 + lax.rem(q_at, 2)

    def xy_peer(step):
        return lax.rem(xy + step, nxy)

    def q_peer(step):
        return lax.rem(q + step, nq)

    def q_of(z_at, core_at):
        return lax.div(z_at, 2) * 4 + core_at * 2 + lax.rem(z_at, 2)

    def rcopy(src, dst, send, recv, target):
        return pltpu.make_async_remote_copy(
            src_ref=src, dst_ref=dst, send_sem=send, recv_sem=recv,
            device_id=target, device_id_type=MESH)

    barrier = pltpu.get_barrier_semaphore()

    def greet_xy(step, carry):
        pl.semaphore_signal(barrier, inc=1, device_id=dev(q, xy_peer(step)), device_id_type=MESH)
        return carry

    def greet_q(step, carry):
        pl.semaphore_signal(barrier, inc=1, device_id=dev(q_peer(step), xy), device_id_type=MESH)
        return carry

    lax.fori_loop(1, nxy, greet_xy, 0)
    lax.fori_loop(1, nq, greet_q, 0)

    x_at = lax.rem(xy, 4)
    y_at = lax.div(xy, 4)
    for load in loads[0:3]:
        load.wait()
    coeff = leaf(pos_ref, wgt_ref, phase_ref, gx, ly, ct)
    key = key_ref[...].astype(F32)
    gath_a[y_at * 4 + x_at, 0:64, :] = coeff[64:128]
    gath_a[y_at * 4 + x_at, 64:72, :] = jnp.broadcast_to(key, (8, slots))
    gath_b[x_at * 4 + y_at] = coeff[0:64]
    loads[3].wait()
    rate_s[...] = jnp.concatenate([rate_ref[:, 0:ndev], rate_ref[:, ndev:lb]], axis=0).T
    pl.semaphore_wait(barrier, nxy - 1 + nq - 1)

    xs = {0: x_at, -1: lax.rem(x_at + 3, 4), 1: lax.rem(x_at + 1, 4), 2: lax.rem(x_at + 2, 4)}
    ys = {0: y_at, -1: lax.rem(y_at + 3, 4), 1: lax.rem(y_at + 1, 4), 2: lax.rem(y_at + 2, 4)}
    order = (0, -1, 1, 2)
    sent = []

    def block(part, first, second, rows=None):
        ref = gath_a if part == 0 else gath_b
        at = ys[second] * 4 + xs[first] if part == 0 else xs[second] * 4 + ys[first]
        return ref.at[at] if rows is None else ref.at[at, rows]

    def halves(part):
        return (slice(0, 40), slice(40, 72)) if part == 0 else (slice(0, 32), slice(32, 64))

    def ring_copy(part, axis, sem, first, second, way, rows=None):
        along_x = (part == 0) == (axis == 0)
        to = ys[0] * 4 + xs[way] if along_x else ys[way] * 4 + xs[0]
        ref = block(part, first, second, rows)
        return rcopy(ref, ref, g_send.at[part, sem], g_recv.at[part, sem], dev(q, to))

    def start(copy):
        copy.start()
        sent.append(copy)

    for part in range(2):
        start(ring_copy(part, 0, 0, 0, 0, 1))
        start(ring_copy(part, 0, 1, 0, 0, -1))
    for part in range(2):
        start(ring_copy(part, 1, 4, 0, 0, 1))
        start(ring_copy(part, 1, 5, 0, 0, -1))

    def rate_copy(step):
        to = xy_peer(step)
        rows_to = pl.ds(pl.multiple_of(to * nq, nq), nq)
        rows_me = pl.ds(pl.multiple_of(xy * nq, nq), nq)
        return rcopy(rate_s.at[rows_to], rate_r.at[rows_me], r_send.at[step], r_recv.at[step], dev(q, to))

    def send_rate(step, carry):
        rate_copy(step).start()
        return carry

    lax.fori_loop(1, nxy, send_rate, 0)
    rows_me = pl.ds(pl.multiple_of(xy * nq, nq), nq)
    rate_r[rows_me, :] = rate_s[rows_me, :]

    for part in range(2):
        low, high = halves(part)
        ring_copy(part, 0, 0, -1, 0, 1).wait_recv()
        start(ring_copy(part, 0, 2, -1, 0, 1, low))
        ring_copy(part, 0, 1, 1, 0, -1).wait_recv()
        start(ring_copy(part, 0, 3, 1, 0, -1, high))
    for part in range(2):
        for r in (1, 2):
            start(ring_copy(part, 1, 4 + 4 * r, order[r], 0, 1))
            start(ring_copy(part, 1, 5 + 4 * r, order[r], 0, -1))
    for part in range(2):
        low, high = halves(part)
        ring_copy(part, 0, 2, 2, 0, 1, low).wait_recv()
        ring_copy(part, 0, 3, 2, 0, -1, high).wait_recv()
        start(ring_copy(part, 1, 4 + 12, 2, 0, 1))
        start(ring_copy(part, 1, 5 + 12, 2, 0, -1))
    for r in range(4):
        for part in range(2):
            low, high = halves(part)
            ring_copy(part, 1, 4 + 4 * r, order[r], -1, 1).wait_recv()
            start(ring_copy(part, 1, 6 + 4 * r, order[r], -1, 1, low))
            ring_copy(part, 1, 5 + 4 * r, order[r], 1, -1).wait_recv()
            start(ring_copy(part, 1, 7 + 4 * r, order[r], 1, -1, high))

    def wait_rate(step, carry):
        rate_copy(step).wait()
        return carry

    lax.fori_loop(1, nxy, wait_rate, 0)
    for at in range(nq):
        rate_s2[at] = rate_r[pl.ds(at, nxy, stride=nq), :]

    def rate2_copy(step):
        to = q_peer(step)
        return rcopy(rate_s2.at[to], rate_r2.at[q], r2_send.at[step], r2_recv.at[step], dev(to, xy))

    def send_rate2(step, carry):
        rate2_copy(step).start()
        return carry

    lax.fori_loop(1, nq, send_rate2, 0)
    rate_r2[q] = rate_s2[q]

    for r in range(4):
        for part in range(2):
            low, high = halves(part)
            ring_copy(part, 1, 6 + 4 * r, order[r], 2, 1, low).wait_recv()
            ring_copy(part, 1, 7 + 4 * r, order[r], 2, -1, high).wait_recv()

    def split_rows(index, carry):
        rows_a = pl.ds(pl.multiple_of(index * slots + 64, 64), 64)
        rows_b = pl.ds(pl.multiple_of(index * slots, 64), 64)
        high, low = split(gath_a[index, 0:64, :])
        cat[rows_a, 0:128] = high
        cat[rows_a, 128:256] = low
        high, low = split(gath_b[lax.rem(index, 4) * 4 + lax.div(index, 4)])
        cat[rows_b, 0:128] = high
        cat[rows_b, 128:256] = low
        return carry

    lax.fori_loop(0, nxy, split_rows, 0)

    n = gath_a[:, 64, :].astype(jnp.int32)
    lbits = lb.bit_length() - 1
    dbits = ndev.bit_length() - 1
    j = n & (lb - 1)
    owner = n >> lbits
    holder = j & (ndev - 1)
    q_d = ((owner >> (lx + 1)) << 1) | (owner & 1)
    xy_d = (owner >> 1) & (nxy - 1)
    local_row = ((j >> dbits) << dbits) + q_d * nxy + xy_d
    code = (holder & (nq - 1)) * lb + local_row
    code = jnp.where((n >= 0) & ((holder >> 3) == xy), code, -1)
    row_id = lax.broadcasted_iota(jnp.int32, (lb, slots), 0)

    def chunk(q_at):
        rel = code - q_at * lb
        hot = [jnp.where(rel[i:i + 1, :] == row_id, 1.0, 0.0).astype(BF16) for i in range(nxy)]
        both = jnp.dot(jnp.concatenate(hot, axis=1), cat[...], preferred_element_type=F32)
        return both[:, 0:128] + both[:, 128:256]

    def sib_copy(off):
        return rcopy(sib_s.at[off], sib_r.at[off], b_send.at[off], b_recv.at[off],
                     dev(q_of(z, 1 - core), xy))

    def z_dev(off):
        return dev(q_of(lax.rem(z + off, 4), core), xy)

    up_half = rcopy(own.at[2, 0:ndev], z2recv.at[0], z_send.at[0], z_recv.at[0], z_dev(1))
    down_half = rcopy(own.at[2, ndev:lb], z2recv.at[1], z_send.at[1], z_recv.at[1], z_dev(3))
    up_full = rcopy(own.at[1], zrecv.at[0], z_send.at[2], z_recv.at[2], z_dev(1))
    down_full = rcopy(own.at[3], zrecv.at[1], z_send.at[3], z_recv.at[3], z_dev(3))

    def fold(off):
        sib_copy(off).wait()
        own[off] = own[off] + sib_r[off]

    def scatter(step, carry):
        off = lax.rem(step + 2, 4)
        to = lax.rem(z + off, 4)
        sib_s[off] = chunk(q_of(to, 1 - core))
        sib_copy(off).start()

        @pl.when(step == 1)
        def _():
            fold(2)
            up_half.start()
            down_half.start()

        @pl.when(step == 3)
        def _():
            fold(3)
            down_half.wait_recv()
            own[3, ndev:lb] = own[3, ndev:lb] + z2recv[1]
            down_full.start()

        own[off] = chunk(q_of(to, core))
        return carry

    lax.fori_loop(0, 4, scatter, 0)
    fold(1)
    up_half.wait_recv()
    own[1, 0:ndev] = own[1, 0:ndev] + z2recv[0]
    up_full.start()
    fold(0)

    def wait_rate2(step, carry):
        rate2_copy(step).wait()
        return carry

    lax.fori_loop(1, nq, wait_rate2, 0)
    sin_p, cos_p = sincos(rate_r2[...].reshape(ndev, 128))
    left = lax.broadcasted_iota(jnp.int32, (ndev, 128), 1) < 64
    cos_o = pltpu.roll(cos_p, 64, 1)
    sin_o = pltpu.roll(sin_p, 64, 1)
    cos1 = jnp.concatenate([jnp.where(left, cos_p, cos_o), jnp.where(left, cos_o, cos_p)], axis=0)
    sin1 = jnp.concatenate([jnp.where(left, -sin_p, sin_o), jnp.where(left, -sin_o, sin_p)], axis=0)
    for load in loads[4:6]:
        load.wait()

    down_full.wait_recv()
    up_full.wait_recv()
    state = own[0] + (zrecv[0] + zrecv[1])

    cosv, sinv = cos1, sin1
    sub = lax.broadcasted_iota(jnp.int32, (lb // 8, 8, 128), 1)
    for step in range(dbits):
        if step > 0:
            cosv, sinv = cosv * cos1 - sinv * sin1, sinv * cos1 + cosv * sin1
        bit = lx if step == 0 else (step - 1 if step <= lx else step)
        if bit < 3:
            tiles = state.reshape(lb // 8, 8, 128)
            dist = 1 << bit
            upper = (sub & dist) != 0
            first = jnp.where(upper, pltpu.roll(tiles, dist, 1), tiles).reshape(lb, 128)
            second = jnp.where(upper, tiles, pltpu.roll(tiles, 8 - dist, 1)).reshape(lb, 128)
        else:
            pairs = state.reshape(lb >> (bit + 1), 2, 1 << bit, 128)
            first = jnp.concatenate([pairs[:, 0:1], pairs[:, 0:1]], axis=1).reshape(lb, 128)
            second = jnp.concatenate([pairs[:, 1:2], pairs[:, 1:2]], axis=1).reshape(lb, 128)
        first = cosv * first + sinv * pltpu.roll(first, 64, 1)
        second = cosv * second + sinv * pltpu.roll(second, 64, 1)
        high, low = split(jnp.concatenate([first, second], axis=1))
        w_ref = w0_ref if step % 2 == 0 else w1_ref
        main = jnp.dot(high, w_ref[...], preferred_element_type=F32)
        rest = jnp.dot(low, w_ref[:, 0:128], preferred_element_type=F32)
        state = main[:, 0:128] + (main[:, 128:256] + rest)

    for at in range(nq):
        for jj in range(2):
            base = jj * ndev + at * nxy
            ret_s[at, jj * nxy:(jj + 1) * nxy] = state[base:base + nxy]

    def ret_copy(step):
        to = q_peer(step)
        rows = pl.ds(pl.multiple_of(q * 2 * nxy, 2 * nxy), 2 * nxy)
        return rcopy(ret_s.at[to], ret_r.at[rows], t_send.at[step], t_recv.at[step], dev(to, xy))

    def send_ret(step, carry):
        ret_copy(step).start()
        return carry

    def wait_ret(step, carry):
        ret_copy(step).wait()
        return carry

    lax.fori_loop(1, nq, send_ret, 0)
    ret_r[pl.ds(pl.multiple_of(q * 2 * nxy, 2 * nxy), 2 * nxy), :] = ret_s[q]
    lax.fori_loop(1, nq, wait_ret, 0)
    for at in range(nxy):
        fin_s[at] = ret_r[pl.ds(at, 2 * nq, stride=nxy), :]

    def fin_copy(step):
        to = xy_peer(step)
        return rcopy(fin_s.at[to], fin_r.at[xy], f_send.at[step], f_recv.at[step], dev(q, to))

    def send_fin(step, carry):
        fin_copy(step).start()
        return carry

    def wait_fin(step, carry):
        fin_copy(step).wait()
        return carry

    lax.fori_loop(1, nxy, send_fin, 0)
    fin_r[xy] = fin_s[xy]
    for copy in sent + [up_half, down_half, up_full, down_full]:
        copy.wait_send()
    lax.fori_loop(1, nxy, wait_fin, 0)
    out_ref[...] = fin_r[...].reshape(lb, 128)


S1, S2 = 40, 24


def far(step, size):
    return min(step, size - step)


XY_STEPS = sorted(range(1, 16), key=lambda s: -far(s // 4, 4) - far(s % 4, 4))
Q_STEPS = sorted(range(1, 8), key=lambda s: far(s // 4 * 2 + s % 2, 4))


def nt_dot(left, right):
    return lax.dot_general(left, right, (((1,), (1,)), ((), ())), preferred_element_type=F32)


def hot(cond):
    return jnp.where(cond, 1.0, 0.0)


def slot_kernel(pos_hbm, wgt_hbm, phase_hbm, rate_hbm, w0_hbm, w1_hbm, box_hbm, count_hbm, target_hbm,
                out_ref, flag_ref, key_ref, cos_out, sin_out,
                pos_ref, wgt_ref, phase_ref, rate_ref, w0_ref, w1_ref, box_ref, count_ref, target_ref, gx, ly, ct,
                rate_s, rate_r, rate_s2, rate_r2, msg1_s, msg1_r, cat2, msg2_s, msg2_r, cos_s, sin_s, ret_s, ret_r,
                in_sem, a_send, a_recv, c_send, c_recv, r_send, r_recv, r2_send, r2_recv, t_send, t_recv):
    nxy, nq = 16, 8
    ndev = nxy * nq
    lb = 2 * ndev
    slots = 128
    lbits = lb.bit_length() - 1
    dbits = ndev.bit_length() - 1
    hi = lax.axis_index("hi")
    lo = lax.axis_index("lo")
    xy = lax.div(lo, 2)
    q = hi * 2 + lax.rem(lo, 2)

    def dev(q_at, xy_at):
        return lax.div(q_at, 2), xy_at * 2 + lax.rem(q_at, 2)

    def xy_peer(step):
        return lax.rem(xy + step, nxy)

    def q_peer(step):
        return lax.rem(q + step, nq)

    def rcopy(src, dst, send, recv, target):
        return pltpu.make_async_remote_copy(
            src_ref=src, dst_ref=dst, send_sem=send, recv_sem=recv,
            device_id=target, device_id_type=MESH)

    barrier = pltpu.get_barrier_semaphore()
    for step in XY_STEPS:
        pl.semaphore_signal(barrier, inc=1, device_id=dev(q, xy_peer(step)), device_id_type=MESH)
    for step in Q_STEPS:
        pl.semaphore_signal(barrier, inc=1, device_id=dev(q_peer(step), xy), device_id_type=MESH)

    loads = [
        pltpu.make_async_copy(src, dst, in_sem.at[i])
        for i, (src, dst) in enumerate([
            (box_hbm, box_ref), (phase_hbm, phase_ref), (wgt_hbm, wgt_ref), (pos_hbm, pos_ref),
            (rate_hbm, rate_ref), (w0_hbm, w0_ref), (w1_hbm, w1_ref), (target_hbm, target_ref),
            (count_hbm, count_ref)])
    ]
    for load in loads[8:] + loads[:8]:
        load.start()

    loads[8].wait()
    loads[0].wait()
    lane = lax.broadcasted_iota(jnp.int32, (1, slots), 1)
    n = jnp.where(lane < count_ref[...], box_ref[...], -1)
    key_ref[...] = n
    j = n & (lb - 1)
    owner = n >> lbits
    holder = j & (ndev - 1)
    q_d = ((owner >> 5) << 1) | (owner & 1)
    xy_d = (owner >> 1) & (nxy - 1)
    row_at = ((j >> dbits) << dbits) + q_d * nxy + xy_d
    live = n >= 0
    q_to = jnp.where(live, holder & (nq - 1), -1)
    before = hot(lax.broadcasted_iota(jnp.int32, (slots, slots), 0) < lax.broadcasted_iota(jnp.int32, (slots, slots), 1))
    before = before.astype(BF16)
    row128 = lax.broadcasted_iota(jnp.int32, (128, 128), 0)

    to_q = hot(q_to == lax.broadcasted_iota(jnp.int32, (16, slots), 0))
    ahead = jnp.dot(to_q.astype(BF16), before, preferred_element_type=F32)
    rank = jnp.sum(to_q * ahead, axis=0, keepdims=True).astype(jnp.int32)
    slot = jnp.where(live & (rank < S1 - 1), q_to * S1 + rank, -1)
    names = jnp.concatenate([to_q * ((holder >> 3) + 1).astype(F32), to_q * row_at.astype(F32)], axis=0)
    named = nt_dot(names.astype(BF16), hot(rank == row128).astype(BF16))
    named = named[0:8] * 256.0 + named[16:24]
    place = hot(slot == lax.broadcasted_iota(jnp.int32, (nq * S1, slots), 0)).astype(BF16)

    for load in loads[1:5]:
        load.wait()
    rate_s[...] = jnp.concatenate([rate_ref[:, 0:ndev], rate_ref[:, ndev:lb]], axis=0).T
    zeros = jnp.zeros((16, 256), BF16)
    for at in range(nq):
        cat2[at * 64 + 48:at * 64 + 64, :] = zeros
    coeff = leaf(pos_ref, wgt_ref, phase_ref, gx, ly, ct)
    both = jnp.dot(place, jnp.concatenate(split(coeff), axis=1), preferred_element_type=F32)
    both = both[:, 0:128] + both[:, 128:256]
    for at in range(nq):
        msg1_s[at * S1:(at + 1) * S1] = both[at * S1:(at + 1) * S1]
        msg1_s[(at + 1) * S1 - 1:(at + 1) * S1] = named[at:at + 1]
    pl.semaphore_wait(barrier, nxy - 1 + nq - 1)

    def slot_rows(at, size):
        return pl.ds(pl.multiple_of(at * size, 8), size)

    def first_copy(step):
        to = q_peer(step)
        return rcopy(msg1_s.at[slot_rows(to, S1)], msg1_r.at[slot_rows(q, S1)], a_send, a_recv, dev(to, xy))

    def rate_copy(step):
        to = xy_peer(step)
        return rcopy(rate_s.at[slot_rows(to, nq)], rate_r.at[slot_rows(xy, nq)], r_send, r_recv, dev(q, to))

    def rate2_copy(step):
        to = q_peer(step)
        return rcopy(rate_s2.at[to], rate_r2.at[q], r2_send, r2_recv, dev(to, xy))

    first_all = rcopy(msg1_s.at[0:(nq - 1) * S1], msg1_r.at[0:(nq - 1) * S1], a_send, a_recv, dev(q_peer(1), xy))
    second_all = rcopy(msg2_s.at[0:(nxy - 1) * S2], msg2_r.at[0:(nxy - 1) * S2], c_send, c_recv, dev(q, xy_peer(1)))
    rate_all = rcopy(rate_s.at[0:(nxy - 1) * nq], rate_r.at[0:(nxy - 1) * nq], r_send, r_recv, dev(q, xy_peer(1)))
    rate2_all = rcopy(rate_s2.at[0:nq - 1], rate_r2.at[0:nq - 1], r2_send, r2_recv, dev(q_peer(1), xy))

    for step in Q_STEPS:
        first_copy(step).start()
    for step in XY_STEPS:
        rate_copy(step).start()
    rate_r[slot_rows(xy, nq), :] = rate_s[slot_rows(xy, nq), :]
    for load in loads[5:8]:
        load.wait()
    sin_t, cos_t = sincos(target_ref[...])
    cos_out[...] = cos_t
    sin_out[...] = sin_t
    msg1_r[slot_rows(q, S1), :] = msg1_s[slot_rows(q, S1), :]
    first_all.wait_recv()

    meta = msg1_r[pl.ds(S1 - 1, nq, stride=S1), :]
    lanes8 = lax.broadcasted_iota(jnp.int32, (nq, 128), 1)
    over = jnp.max(jnp.where(lanes8 >= S1 - 1, meta, 0.0), axis=(0, 1), keepdims=True)
    meta = jnp.where(lanes8 < S1 - 1, meta, 0.0)
    odd = (lax.broadcasted_iota(jnp.int32, (nq, 128), 0) & 1) == 1
    meta = jnp.where(odd, pltpu.roll(meta, 64, 1), meta)
    codes = [(meta[2 * g:2 * g + 1] + meta[2 * g + 1:2 * g + 2]).astype(jnp.int32) for g in range(4)]
    xy_to = [code >> 8 for code in codes]
    row_to = [((code & 255) + 1).astype(F32) for code in codes]
    id16 = lax.broadcasted_iota(jnp.int32, (nxy, 128), 0) + 1
    to_xy = [hot(value == id16) for value in xy_to]
    counted = jnp.dot(jnp.concatenate(to_xy, axis=0).astype(BF16),
                      jnp.concatenate([before, jnp.ones((128, 128), BF16)], axis=1), preferred_element_type=F32)
    ranks = []
    total = jnp.zeros((nxy, 128), F32)
    for g in range(4):
        part = counted[g * nxy:(g + 1) * nxy]
        ranks.append(jnp.sum(to_xy[g] * (part[:, 0:128] + total), axis=0, keepdims=True).astype(jnp.int32))
        total = total + part[:, 128:256]
    place_id = lax.broadcasted_iota(jnp.int32, (nxy * S2, 128), 0)
    place2 = []
    for g in range(4):
        slot = jnp.where((xy_to[g] > 0) & (ranks[g] < S2 - 1), (xy_to[g] - 1) * S2 + ranks[g], -1)
        place2.append(hot(slot == place_id).astype(BF16))
    for at in range(nq):
        rows = jnp.concatenate([msg1_r[at * S1:at * S1 + S1, :], jnp.zeros((48 - S1, 128), F32)], axis=0)
        high, low = split(rows)
        cat2[at * 64:at * 64 + 48, 0:128] = high
        cat2[at * 64:at * 64 + 48, 128:256] = low
    both = jnp.dot(jnp.concatenate(place2, axis=1), cat2[...], preferred_element_type=F32)
    both = both[:, 0:128] + both[:, 128:256]
    names = jnp.concatenate([to_xy[g] * row_to[g] for g in range(4)], axis=1)
    named = nt_dot(names.astype(BF16), jnp.concatenate([hot(ranks[g] == row128).astype(BF16) for g in range(4)], axis=1))
    lanes16 = lax.broadcasted_iota(jnp.int32, (nxy, 128), 1)
    named = named + jnp.where((lanes16 == 127) & (over > 0.0), 1.0, 0.0)
    for at in range(nxy):
        msg2_s[at * S2:(at + 1) * S2] = both[at * S2:(at + 1) * S2]
        msg2_s[(at + 1) * S2 - 1:(at + 1) * S2] = named[at:at + 1]

    def second_copy(step):
        to = xy_peer(step)
        return rcopy(msg2_s.at[slot_rows(to, S2)], msg2_r.at[slot_rows(xy, S2)], c_send, c_recv, dev(q, to))

    for step in XY_STEPS:
        second_copy(step).start()
    msg2_r[slot_rows(xy, S2), :] = msg2_s[slot_rows(xy, S2), :]
    rate_all.wait_recv()
    for at in range(nq):
        rate_s2[at] = rate_r[pl.ds(at, nxy, stride=nq), :]
    for step in Q_STEPS:
        rate2_copy(step).start()
    rate_r2[q] = rate_s2[q]
    rate2_all.wait_recv()
    rates = rate_r2[...].reshape(ndev, 128)
    sin_p, cos_p = sincos(rates)
    left = lax.broadcasted_iota(jnp.int32, (ndev, 128), 1) < 64
    cos_o = pltpu.roll(cos_p, 64, 1)
    sin_o = pltpu.roll(sin_p, 64, 1)
    cos1 = [jnp.where(left, cos_p, cos_o), jnp.where(left, cos_o, cos_p)]
    sin1 = [jnp.where(left, -sin_p, sin_o), jnp.where(left, -sin_o, sin_p)]
    for jj in range(2):
        cosv, sinv = cos1[jj], sin1[jj]
        for step in range(dbits):
            if step > 0:
                cosv, sinv = cosv * cos1[jj] - sinv * sin1[jj], sinv * cos1[jj] + cosv * sin1[jj]
            cos_s[step, jj] = cosv
            sin_s[step, jj] = sinv
    second_all.wait_recv()

    meta = msg2_r[pl.ds(S2 - 1, nxy, stride=S2), :]
    over = jnp.max(jnp.where(lanes16 >= S2 - 1, meta, 0.0), axis=(0, 1), keepdims=True)
    mark = jnp.where(over > 0.0, jnp.nan, 0.0)
    meta = jnp.where(lanes16 < S2 - 1, meta, 0.0)
    sub4 = lax.broadcasted_iota(jnp.int32, (nxy, 128), 0) & 3
    for turn in range(1, 4):
        meta = jnp.where(sub4 == turn, pltpu.roll(meta, 32 * turn, 1), meta)
    row_id = lax.broadcasted_iota(jnp.int32, (lb, 128), 0)
    spread = []
    for at in range(nxy):
        spread += [msg2_r[at * S2:(at + 1) * S2, :], jnp.zeros((32 - S2, 128), F32)]
    spread = jnp.concatenate(spread, axis=0)
    put = []
    for g in range(4):
        code = jnp.sum(meta[4 * g:4 * g + 4], axis=0, keepdims=True).astype(jnp.int32) - 1
        put.append(hot(code == row_id).astype(BF16))
    both = jnp.dot(jnp.concatenate(put, axis=1), jnp.concatenate(split(spread), axis=1), preferred_element_type=F32)
    state = both[:, 0:128] + both[:, 128:256]

    sub = lax.broadcasted_iota(jnp.int32, (ndev // 8, 8, 128), 1)
    states = [state[0:ndev], state[ndev:lb]]
    for step in range(dbits):
        bit = 4 if step == 0 else (step - 1 if step <= 4 else step)
        w_ref = w0_ref if step % 2 == 0 else w1_ref
        for jj in range(2):
            state = states[jj]
            cosv, sinv = cos_s[step, jj], sin_s[step, jj]
            if bit < 3:
                tiles = state.reshape(ndev // 8, 8, 128)
                dist = 1 << bit
                upper = (sub & dist) != 0
                first = jnp.where(upper, pltpu.roll(tiles, dist, 1), tiles).reshape(ndev, 128)
                second = jnp.where(upper, tiles, pltpu.roll(tiles, 8 - dist, 1)).reshape(ndev, 128)
            else:
                pairs = state.reshape(ndev >> (bit + 1), 2, 1 << bit, 128)
                first = jnp.concatenate([pairs[:, 0:1], pairs[:, 0:1]], axis=1).reshape(ndev, 128)
                second = jnp.concatenate([pairs[:, 1:2], pairs[:, 1:2]], axis=1).reshape(ndev, 128)
            first = cosv * first + sinv * pltpu.roll(first, 64, 1)
            second = cosv * second + sinv * pltpu.roll(second, 64, 1)
            high, low = split(jnp.concatenate([first, second], axis=1))
            main = jnp.dot(high, w_ref[...], preferred_element_type=F32)
            rest = jnp.dot(low, w_ref[:, 0:128], preferred_element_type=F32)
            states[jj] = main[:, 0:128] + (main[:, 128:256] + rest)

    for jj in range(2):
        ret_s[pl.ds(jj, ndev, stride=2), :] = states[jj] + mark
    holder_at = xy * nq + q

    def ret_to(hi_step, lo_step):
        hi_to = lax.rem(hi + hi_step, 4)
        lo_to = lax.rem(lo + lo_step, 32)
        at = (hi_to * 2 + lax.rem(lo_to, 2)) * nxy + lax.div(lo_to, 2)
        return rcopy(ret_s.at[pl.ds(at * 2, 2)], ret_r.at[pl.ds(holder_at * 2, 2)], t_send, t_recv, (hi_to, lo_to))

    def send_eight(block, carry):
        for a in (2, 3, 1):
            for b in range(8):
                ret_to(a, block * 8 + b).start()
        return carry

    lax.fori_loop(0, 4, send_eight, 0)
    for step in range(1, 32):
        ret_to(0, step).start()
    ret_r[pl.ds(holder_at * 2, 2), :] = ret_s[pl.ds((q * nxy + xy) * 2, 2), :]
    every = rcopy(ret_s.at[0:lb - 2], ret_r.at[0:lb - 2], t_send, t_recv, dev(q_peer(1), xy))
    every.wait_recv()
    result = ret_r[...]
    out_ref[...] = result
    total = jnp.sum(result, axis=0, keepdims=True)
    flag_ref[0] = jnp.max(jnp.where(total != total, 1.0, 0.0)).astype(jnp.int32)
    for copy in (first_all, second_all, rate_all, rate2_all, every):
        copy.wait_send()


def target_kernel(state_ref, cos_ref, sin_ref, table_ref, out_ref):
    lb, points = cos_ref.shape
    half = lb // 2
    for jj in range(2):
        rows = slice(jj * half, jj * half + half)
        high, low = split(state_ref[pl.ds(jj, half, stride=2), :])
        stacked = jnp.concatenate([high, low, high], axis=1)
        value = jnp.dot(stacked, table_ref[...], preferred_element_type=F32)
        cosv, sinv = cos_ref[rows, :], sin_ref[rows, :]
        v_re = value[:, 0:points]
        v_im = value[:, points:2 * points]
        out_ref[0, rows, :] = v_re * cosv - v_im * sinv
        out_ref[1, rows, :] = v_re * sinv + v_im * cosv


def local(side, src_position, src_weight, src_phase, block_box, block_count, node_rate, target_phase):
    slots, points = src_phase.shape
    lb = node_rate.shape[0]
    nxy, nq = 16, 8
    dma = pltpu.SemaphoreType.DMA
    hbm = pl.BlockSpec(memory_space=pltpu.HBM)
    operands = (
        src_position.reshape(2 * slots, points), src_weight.reshape(2 * slots, points), src_phase, node_rate.T,
        level_weight(0), level_weight(1), block_box.reshape(1, slots), block_count.reshape(1, 1), target_phase)
    held = [
        pltpu.VMEM((2 * slots, points), F32),
        pltpu.VMEM((2 * slots, points), F32),
        pltpu.VMEM((slots, points), F32),
        pltpu.VMEM((64, lb), F32),
        pltpu.VMEM((256, 256), BF16),
        pltpu.VMEM((256, 256), BF16),
        pltpu.VMEM((1, slots), jnp.int32),
        pltpu.VMEM((1, 1), jnp.int32),
        pltpu.VMEM(target_phase.shape, F32),
        pltpu.VMEM((16, points, slots), F32),
        pltpu.VMEM((8, points, slots), F32),
        pltpu.VMEM((128, slots), F32),
    ]
    returned = [
        pltpu.VMEM((nq, 2 * nxy, 128), F32),
        pltpu.VMEM((lb, 128), F32),
        pltpu.VMEM((nxy, 2 * nq, 128), F32),
        pltpu.VMEM((nxy, 2 * nq, 128), F32),
    ]
    state_shape = jax.ShapeDtypeStruct((lb, 128), F32)

    def exact(key):
        return pl.pallas_call(
            exact_kernel,
            out_shape=state_shape,
            in_specs=[hbm] * 6 + [VMEM],
            out_specs=VMEM,
            scratch_shapes=held[0:6] + held[9:] + [
                pltpu.VMEM((nxy, 72, 128), F32),
                pltpu.VMEM((nxy, 64, 128), F32),
                pltpu.VMEM((nxy * slots, 256), BF16),
                pltpu.VMEM((nxy * nq, 128), F32),
                pltpu.VMEM((nxy * nq, 128), F32),
                pltpu.VMEM((nq, nxy, 128), F32),
                pltpu.VMEM((nq, nxy, 128), F32),
                pltpu.VMEM((4, lb, 128), F32),
                pltpu.VMEM((4, lb, 128), F32),
                pltpu.VMEM((4, lb, 128), F32),
                pltpu.VMEM((2, lb, 128), F32),
                pltpu.VMEM((2, lb // 2, 128), F32),
            ] + returned + [
                dma((6,)),
                dma((2, 20)), dma((2, 20)), dma((nxy,)), dma((nxy,)), dma((nq,)), dma((nq,)),
                dma((4,)), dma((4,)), dma((4,)), dma((4,)),
                dma((nq,)), dma((nq,)), dma((nxy,)), dma((nxy,)),
            ],
            compiler_params=pltpu.CompilerParams(
                collective_id=1, has_side_effects=True, vmem_limit_bytes=60 * 2**20),
            name="exact",
        )(*operands[0:6], key)

    def targets(state):
        return pl.pallas_call(
            target_kernel,
            out_shape=jax.ShapeDtypeStruct((2, lb, target_phase.shape[1]), F32),
            in_specs=[VMEM] * 4,
            out_specs=VMEM,
            compiler_params=pltpu.CompilerParams(vmem_limit_bytes=32 * 2**20),
            name="target",
        )(state, cosv, sinv, target_weight(side))

    state, flag, key, cosv, sinv = pl.pallas_call(
        slot_kernel,
        out_shape=(state_shape, jax.ShapeDtypeStruct((1,), jnp.int32),
                   jax.ShapeDtypeStruct((1, slots), jnp.int32),
                   jax.ShapeDtypeStruct(target_phase.shape, F32), jax.ShapeDtypeStruct(target_phase.shape, F32)),
        in_specs=[hbm] * 9,
        out_specs=(VMEM, SMEM, VMEM, VMEM, VMEM),
        scratch_shapes=held + [
            pltpu.VMEM((nxy * nq, 128), F32),
            pltpu.VMEM((nxy * nq, 128), F32),
            pltpu.VMEM((nq, nxy, 128), F32),
            pltpu.VMEM((nq, nxy, 128), F32),
            pltpu.VMEM((nq * S1, 128), F32),
            pltpu.VMEM((nq * S1, 128), F32),
            pltpu.VMEM((nq * 64, 256), BF16),
            pltpu.VMEM((nxy * S2, 128), F32),
            pltpu.VMEM((nxy * S2, 128), F32),
            pltpu.VMEM((7, 2, lb // 2, 128), F32),
            pltpu.VMEM((7, 2, lb // 2, 128), F32),
            pltpu.VMEM((lb, 128), F32),
            pltpu.VMEM((lb, 128), F32),
            dma((9,)),
            dma, dma, dma, dma, dma, dma, dma, dma, dma, dma,
        ],
        compiler_params=pltpu.CompilerParams(
            collective_id=0, has_side_effects=True, vmem_limit_bytes=60 * 2**20),
        name="slots",
    )(*operands)
    return lax.switch(flag[0], (lambda: targets(state), lambda: targets(exact(key))))


def solution(mesh):
    placed = (
        P(("hi", "lo"), None, None),
        P(("hi", "lo"), None, None),
        P(("hi", "lo"), None),
        P(("hi", "lo")),
        P(("hi", "lo")),
        P(("hi", "lo"), None),
        P(("hi", "lo"), None),
    )
    return jax.shard_map(
        functools.partial(local, 16),
        mesh=mesh, in_specs=placed, out_specs=P(None, ("hi", "lo"), None), check_vma=False
    )
```
